128 devices in a mesh: fsdp: 16 (over y_hi, z, core), ctx: 2 (over y_lo), tp: 4 (over x).
Axes of the slice: x: 4, y: 4 (y_hi: 2, y_lo: 2; y = y_hi * 2 + y_lo), z: 4, core: 2. Of those that a mesh axis runs over, the one named last changes fastest.
Arguments:
- tokens: bfloat16 [32768, 1024], P(('fsdp', 'ctx')), may hold values from -6 to 6
- cotangent: bfloat16 [32768, 1024], P(('fsdp', 'ctx')), may hold values from -6 to 6
- expert_ids: int32 [32768, 1], P(('fsdp', 'ctx')), may hold values from 0 to 63
- segment_ids: int32 [32768], P('fsdp'), may hold values from 0 to 162, never falling along the last dimension, each value on 1 to 800 neighbouring positions
- priority: int32 [32, 1024], P(('fsdp', 'ctx')), may hold values from 0 to 1023, each once within a row
- w_qkv: bfloat16 [3, 1024, 1024], P(None, ('fsdp', 'ctx'), 'tp'), may hold values from -0.1875 to 0.1875
- w_out: bfloat16 [1024, 1024], P('tp', ('fsdp', 'ctx')), may hold values from -0.75 to 0.75
- norm_gains: bfloat16 [2, 1024], P(None, ('fsdp', 'ctx')), may hold values from 0.5 to 1.5
- norm_shifts: bfloat16 [3, 1024], P(None, ('fsdp', 'ctx')), may hold values from -0.59765625 to 0.59765625
- qv_bias: bfloat16 [2, 16, 64], P(None, 'tp', ('fsdp', 'ctx')), may hold values from -0.59765625 to 0.59765625
- w_up: bfloat16 [64, 1024, 4096], P(('fsdp', 'ctx'), None, 'tp'), may hold values from -0.1875 to 0.1875
- up_bias: bfloat16 [64, 4096], P(('fsdp', 'ctx'), 'tp'), may hold values from -0.59765625 to 0.59765625
- w_down: bfloat16 [64, 4096, 1024], P(('fsdp', 'ctx'), 'tp'), may hold values from -0.125 to 0.125
- down_bias: bfloat16 [64, 1024], P(('fsdp', 'ctx')), may hold values from -2.390625 to 2.390625
Outputs:
- block_out: bfloat16 [32768, 1024], P(('fsdp', 'ctx'))
- tokens_grad: bfloat16 [32768, 1024], P(('fsdp', 'ctx'))
- w_qkv_grad: float32 [3, 1024, 1024], P(None, ('fsdp', 'ctx'), 'tp')
- w_out_grad: float32 [1024, 1024], P('tp', ('fsdp', 'ctx'))
- norm_gains_grad: float32 [2, 1024], P(None, ('fsdp', 'ctx'))
- norm_shifts_grad: float32 [3, 1024], P(None, ('fsdp', 'ctx'))
- qv_bias_grad: float32 [2, 16, 64], P(None, 'tp', ('fsdp', 'ctx'))
- w_up_grad: float32 [64, 1024, 4096], P(('fsdp', 'ctx'), None, 'tp')
- up_bias_grad: float32 [64, 4096], P(('fsdp', 'ctx'), 'tp')
- w_down_grad: float32 [64, 4096, 1024], P(('fsdp', 'ctx'), 'tp')
- down_bias_grad: float32 [64, 1024], P(('fsdp', 'ctx'))
The draws below stay inside these ranges and needn't reach their ends.
Inputs may be any that keep to these rules, and one draw needn't show every extreme that they name: `expert_ids`: every expert is named by some token. `segment_ids`: never falls along the array; one id covers 1 to 800 consecutive positions, some id exactly 800. `priority`: each row is a permutation of the positions of its block.
All inputs are finite; a program needn't handle non-finite values.
Results may differ from the reference program's by a relative error of at most 0.03.
Values may be sent and summed in bfloat16 or wider, within the bound.
No kernel may reach another device: no remote copies, remote signals or barrier semaphores. Data moves between devices by JAX's collectives and lax.ppermute only.
A program may use at most 192 MiB of HBM per device.

```python
import math
import jax
import jax.numpy as jnp
import numpy as np
from jax import lax

D = 1024
HEADS = 16
HD = 64
FF = 4096
SEQ_LEN = 2048
EXPERTS = 64
NSEQ = 16
ROWS = 1024
BLOCKS = 32
TOKENS = 32768
CAP = 36
DOC_MOST = 800
SEG_COUNT = 163
N_CTX = 2


def with_spikes(entries, key, source, target, shards_of, factor):
    def block_of(dim):
        return (jnp.arange(entries.shape[dim]) // (entries.shape[dim] // shards_of)).reshape((-1,) + (1,) * (entries.ndim - 1 - dim))

    first = jax.random.permutation(key, shards_of)[block_of(target)]
    far = (block_of(target) + shards_of // 2) % shards_of
    return jnp.where((block_of(source) == first) | (block_of(source) == far), factor * entries, entries)


def level_of(rng, shape, shards, low, top_value):
    level, own = 1.0, jax.random.fold_in(rng, 6)
    for dim, shards_of in shards:
        draws = jnp.exp(jax.random.uniform(jax.random.fold_in(own, dim), (shards_of,), jnp.float32, low / len(shards), top_value / len(shards)))
        level = level * jnp.repeat(draws, shape[dim] // shards_of).reshape([-1 if axis == dim else 1 for axis in range(len(shape))])
    return level


def choose_distinct(key, rows, number_of, top, lift):
    ranking = jax.random.permutation(jax.random.fold_in(key, 1), number_of)
    pull = ranking
    for power in range(3):
        pull = pull * pull // number_of
    pull = pull * lift // number_of
    tickets = jax.random.randint(jax.random.fold_in(key, 2), (rows, number_of), 0, 4096) + pull
    fixed_rows = jax.random.permutation(jax.random.fold_in(key, 3), rows)[jnp.arange(number_of) % rows]
    tickets = jnp.where(jnp.arange(rows)[:, None] == fixed_rows[None, :], 1 << 14, tickets)
    merit = tickets * number_of + jnp.arange(number_of)
    return lax.top_k(merit.astype(jnp.int32), top)[1].astype(jnp.int32)


def profile(amount, total, limit, lean):
    loads = [(1 << 20) // math.isqrt(standing ** lean) + 1 for standing in range(2, amount + 1)]
    spare, given = total - limit - (amount - 1), [1] * (amount - 1)
    while spare > 0:
        candidates = [i for i in range(amount - 1) if given[i] < limit]
        pool, remaining = sum([loads[i] for i in candidates]), spare
        for i in candidates:
            extra = min(limit - given[i], max(1, remaining * loads[i] // pool), spare)
            given[i] = given[i] + extra
            spare = spare - extra
    return np.array([limit] + given)


def ragged_sizes(rng, count, total, most, skew):
    if count == 2:
        one = jax.random.randint(rng, (), max(1, total - most), min(most, total - 1) + 1)
        return jnp.stack([one, total - one])
    tallies = jnp.asarray(profile(count, total, most, skew), jnp.int32)
    pairs = (count - 1) // 2
    giver, receiver = tallies[1:1 + 2 * pairs:2], tallies[2:2 + 2 * pairs:2]
    room = jnp.minimum(giver - 1, most - receiver)
    shifted = jax.random.randint(jax.random.fold_in(rng, 1), (pairs,), 0, 1 << 20) % (room + 1)
    tallies = tallies.at[1:1 + 2 * pairs:2].set(giver - shifted).at[2:2 + 2 * pairs:2].set(receiver + shifted)
    return tallies[jax.random.permutation(jax.random.fold_in(rng, 2), count)]


def bell_draw(stream_key, dims, deviation, most, shards=(), kind=jnp.bfloat16):
    factor_of = level_of(stream_key, dims, shards, -0.22, 0.18) if shards else 1.0
    entries = jax.random.normal(stream_key, dims, jnp.float32) * deviation * factor_of
    return jnp.minimum(jnp.maximum(entries, -most), most).astype(kind)


def gaussian_with(key, extent, spread, bound, shards, heavy, held_as=jnp.bfloat16):
    values = spread * jax.random.normal(key, extent, jnp.float32)
    if shards:
        values = values * level_of(key, extent, shards, -0.22, 0.18)
    return jnp.clip(with_spikes(values, jax.random.fold_in(key, 3), *heavy), -bound, bound).astype(held_as)


def setup_inputs(seed: int = 0) -> dict:
    streams_of = jax.random.split(jax.random.key(seed), 15)
    return {
        "tokens": bell_draw(streams_of[0], (TOKENS, D), 1.0, 6.0, ((0, 32),)),
        "cotangent": gaussian_with(streams_of[1], (TOKENS, D), 1.0, 6.0, ((0, 32),), (0, 1, 32, 2.75)),
        "expert_ids": choose_distinct(streams_of[2], TOKENS, EXPERTS, 1, 128),
        "segment_ids": jnp.searchsorted(jnp.cumsum(ragged_sizes(streams_of[3], SEG_COUNT, TOKENS, DOC_MOST, 1)), jnp.arange(TOKENS), side="right").astype(jnp.int32),
        "priority": jax.vmap(lambda own: jax.random.permutation(own, ROWS))(jax.random.split(streams_of[4], BLOCKS)).reshape((BLOCKS, ROWS)).astype(jnp.int32),
        "w_qkv": bell_draw(streams_of[5], (3, D, D), D ** -0.5, 0.1875, ((1, 32), (2, 4))),
        "w_out": bell_draw(streams_of[6], (D, D), (D // 16) ** -0.5, 0.75, ((0, 4), (1, 32))),
        "norm_gains": jnp.clip(1.0 + 0.1 * jax.random.normal(streams_of[7], (2, D), jnp.float32), 0.5, 1.5).astype(jnp.bfloat16),
        "norm_shifts": bell_draw(streams_of[8], (3, D), 0.1, 0.59765625, ((1, 32),)),
        "qv_bias": bell_draw(streams_of[9], (2, HEADS, HD), 0.1, 0.59765625, ((1, 4), (2, 32))),
        "w_up": bell_draw(streams_of[10], (EXPERTS, D, FF), D ** -0.5, 0.1875, ((0, 32), (2, 4))),
        "up_bias": bell_draw(streams_of[11], (EXPERTS, FF), 0.1, 0.59765625, ((0, 32), (1, 4))),
        "w_down": bell_draw(streams_of[12], (EXPERTS, FF, D), (FF // 2) ** -0.5, 0.125, ((0, 32), (1, 4))),
        "down_bias": bell_draw(streams_of[13], (EXPERTS, D), 0.4, 2.390625, ((0, 32),)),
    }


@jax.custom_vjp
def low(v):
    return lax.optimization_barrier(v.astype(jnp.bfloat16)).astype(jnp.float32)

@jax.custom_vjp
def low_back(v):
    return v

def low_keep(v):
    return (low(v), None)

def low_pass(kept, grad):
    return (grad,)

def back_keep(v):
    return (v, None)

def back_low(kept, grad):
    return (low(grad),)
low.defvjp(low_keep, low_pass)
low_back.defvjp(back_keep, back_low)
EPSILON = 1e-05
NEGATIVE = -1e+30
HIGHEST = lax.Precision.HIGHEST

def layer_norm(values, gain_row, shift_row):
    centre = values - lax.optimization_barrier(jnp.mean(values, axis=-1, keepdims=True))
    variance = lax.optimization_barrier(jnp.mean(centre * centre, axis=-1, keepdims=True))
    return centre * lax.rsqrt(variance + EPSILON) * gain_row + shift_row

def slot_targets(expert_ids, priority):
    owner_ids = expert_ids[:, 0].reshape(BLOCKS, ROWS).astype(jnp.int32)
    rank_list = priority.astype(jnp.int32)
    lanes = jnp.arange(BLOCKS, dtype=jnp.int32)[:, None]
    in_order = jnp.zeros((BLOCKS, ROWS), jnp.int32).at[lanes, rank_list].set(owner_ids)
    expert_range = jnp.arange(EXPERTS, dtype=jnp.int32)
    order_table = (in_order[:, :, None] == expert_range[None, None, :]).astype(jnp.int32)
    running = jnp.cumsum(order_table, axis=1, dtype=jnp.int32).astype(jnp.int32)
    rank_sorted = (lax.optimization_barrier(jnp.sum(running * order_table, axis=2, dtype=jnp.int32)) - 1).astype(jnp.int32)
    local_slot = jnp.take_along_axis(rank_sorted, rank_list, axis=1).astype(jnp.int32)
    counts = running[:, -1, :].reshape(NSEQ, N_CTX, EXPERTS)
    carried = (jnp.cumsum(counts, axis=1, dtype=jnp.int32) - counts).reshape(BLOCKS, EXPERTS).astype(jnp.int32)
    slot_index = (jnp.take_along_axis(carried, owner_ids, axis=1) + local_slot).astype(jnp.int32)
    sequence = (jnp.arange(BLOCKS, dtype=jnp.int32)[:, None] // N_CTX).astype(jnp.int32)
    flat_index = ((owner_ids * NSEQ + sequence) * CAP + slot_index).astype(jnp.int32)
    dead_row = EXPERTS * NSEQ * CAP
    target = jnp.where(slot_index < CAP, flat_index, jnp.int32(dead_row)).reshape(TOKENS).astype(jnp.int32)
    token_at = jnp.full((dead_row,), TOKENS, jnp.int32).at[target].set(jnp.arange(TOKENS, dtype=jnp.int32), mode='drop')
    return (target, token_at.astype(jnp.int32))

def attend_one(queries, keys, values, segments):
    scores = jnp.einsum('qhd,khd->hqk', queries, keys, precision=HIGHEST) * HD ** (-0.5)
    scores = low_back(scores)
    places = jnp.arange(SEQ_LEN, dtype=jnp.int32)
    allowed = ((segments[:, None] == segments[None, :]) & (places[None, :] <= places[:, None]))[None]
    masked = jnp.where(allowed, scores, jnp.full(scores.shape, NEGATIVE, scores.dtype))
    peak = lax.optimization_barrier(jnp.max(masked, axis=-1, keepdims=True))
    raised = jnp.where(allowed, jnp.exp(masked - peak), jnp.zeros(scores.shape, scores.dtype))
    weights = raised / lax.optimization_barrier(jnp.sum(raised, axis=-1, keepdims=True))
    mixed_out = jnp.einsum('hqk,khd->qhd', low(weights), values, precision=HIGHEST)
    return low(low_back(mixed_out)).reshape(SEQ_LEN, HEADS * HD)

def forward(tokens, w_qkv, w_out, norm_gains, norm_shifts, qv_bias, w_up, up_bias, w_down, down_bias, segment_ids, target, token_at):
    first_norm = low(layer_norm(tokens, norm_gains[0], norm_shifts[0]))
    projected = jnp.einsum('rd,tdc->trc', first_norm, w_qkv, precision=HIGHEST)
    bias_flat = qv_bias.reshape(2, D)
    queries = low(low_back(projected[0] + bias_flat[0]))
    keys_all = low(low_back(projected[1]))
    values_all = low(low_back(projected[2] + bias_flat[1]))
    shape_seq = (NSEQ, SEQ_LEN, HEADS, HD)

    def one_sequence(carry_value, seq_parts):
        return (carry_value, jax.checkpoint(attend_one)(*seq_parts))
    _, mixed_all = lax.scan(one_sequence, jnp.zeros((), jnp.float32), (queries.reshape(shape_seq), keys_all.reshape(shape_seq), values_all.reshape(shape_seq), segment_ids.reshape(NSEQ, SEQ_LEN)))
    branch = low_back(jnp.dot(mixed_all.reshape(TOKENS, D), w_out, precision=HIGHEST) + norm_shifts[2])
    middle = tokens + branch
    second = low(low_back(layer_norm(middle, norm_gains[1], norm_shifts[1])))
    padded = jnp.concatenate([second, jnp.zeros((1, D), second.dtype)], axis=0)
    buffer = padded[token_at].reshape(EXPERTS, NSEQ * CAP, D)
    hidden = low_back(jnp.einsum('emd,edf->emf', buffer, w_up, precision=HIGHEST) + up_bias[:, None, :])
    active = low(jax.nn.silu(hidden))
    result = low(jnp.einsum('emf,efd->emd', active, w_down, precision=HIGHEST) + down_bias[:, None, :])
    result_pad = jnp.concatenate([result.reshape(EXPERTS * NSEQ * CAP, D), jnp.zeros((1, D), result.dtype)], axis=0)
    return middle + result_pad[target]

def reference(tokens, cotangent, expert_ids, segment_ids, priority, w_qkv, w_out, norm_gains, norm_shifts, qv_bias, w_up, up_bias, w_down, down_bias):
    target, token_at = slot_targets(expert_ids, priority)
    float_inputs = tuple((array_in.astype(jnp.float32) for array_in in (tokens, w_qkv, w_out, norm_gains, norm_shifts, qv_bias, w_up, up_bias, w_down, down_bias)))

    def run_block(*float_args):
        return forward(*float_args, segment_ids, target, token_at)
    output, pullback = jax.vjp(run_block, *float_inputs)
    grads = pullback(cotangent.astype(jnp.float32))
    return (output.astype(jnp.bfloat16), grads[0].astype(jnp.bfloat16), grads[1].astype(jnp.float32), grads[2].astype(jnp.float32), grads[3].astype(jnp.float32), grads[4].astype(jnp.float32), grads[5].astype(jnp.float32), grads[6].astype(jnp.float32), grads[7].astype(jnp.float32), grads[8].astype(jnp.float32), grads[9].astype(jnp.float32))
```

```python
import jax
import jax.numpy as jnp
from jax import lax
from jax.experimental import pallas as pl
from jax.experimental.pallas import tpu as pltpu
from jax.sharding import PartitionSpec as P

HD = 64
EPSILON = 1e-05
NEGATIVE = -1e30
REACH = 800
SIDE = 256
FC = ("fsdp", "ctx")
BF = jnp.bfloat16
F32 = jnp.float32


def dot(a, b, ca, cb):
    return lax.dot_general(a, b, (((ca,), (cb,)), ((), ())), preferred_element_type=F32)


def by_head(cols, heads):
    row = lax.broadcasted_iota(jnp.int32, cols.shape, 0) // HD
    zero = jnp.zeros_like(cols)
    return jnp.concatenate([jnp.where(row == h, cols, zero) for h in range(heads)], axis=1)


def pair_mask(start_row, q_first, k_first):
    k_pos = lax.broadcasted_iota(jnp.int32, (SIDE, SIDE), 0) + k_first
    q_pos = lax.broadcasted_iota(jnp.int32, (SIDE, SIDE), 1) + q_first
    return (k_pos >= start_row) & (k_pos <= q_pos)


def forward_kernel(first_ref, q_ref, start_ref, k_ref, v_ref, o_ref, exact_ref, lse_ref, q_heads, acc):
    heads = q_ref.shape[0] // HD
    halo = (k_ref.shape[0] - SIDE * pl.num_programs(0)) // SIDE
    i = pl.program_id(0)
    own = halo + i
    q_heads[...] = by_head(q_ref[...] * jnp.asarray(HD**-0.5, BF), heads)
    acc[...] = jnp.zeros_like(acc)
    start_row = start_ref[...]

    def step(n, carry):
        peak, total = carry
        j = own - n
        rows = pl.ds(pl.multiple_of(j * SIDE, SIDE), SIDE)
        scores = dot(k_ref[rows, :], q_heads[...], 1, 0)
        allowed = pair_mask(start_row, own * SIDE, j * SIDE)
        scores = jnp.where(jnp.concatenate([allowed] * heads, axis=1), scores, NEGATIVE)
        new_peak = jnp.maximum(peak, jnp.max(scores, axis=0, keepdims=True))
        fade = jnp.exp(peak - new_peak)
        weights = jnp.exp(scores - new_peak)
        total = total * fade + jnp.sum(weights, axis=0, keepdims=True)
        low = weights.astype(BF)
        v_t = v_ref[rows, :].T
        for h in range(heads):
            at, cols = slice(h * HD, (h + 1) * HD), slice(h * SIDE, (h + 1) * SIDE)
            acc[at, :] = acc[at, :] * fade[:, cols] + dot(v_t[at, :], low[:, cols], 1, 0)
        return new_peak, total

    width = heads * SIDE
    peak, total = lax.fori_loop(
        0, own - first_ref[i] + 1, step, (jnp.full((1, width), NEGATIVE, F32), jnp.zeros((1, width), F32))
    )
    scale = 1.0 / total
    for h in range(heads):
        at, cols = slice(h * HD, (h + 1) * HD), slice(h * SIDE, (h + 1) * SIDE)
        exact = acc[at, :] * scale[:, cols]
        exact_ref[at, :] = exact
        o_ref[at, :] = exact.astype(BF)
    lse_ref[0] = peak + jnp.log(total)


def attend_forward(first, q_t, start, k_ext, v_ext):
    channels, rows = q_t.shape
    blocks = rows // SIDE
    width = channels // HD * SIDE
    whole = pl.BlockSpec(k_ext.shape, lambda i, f: (0, 0))
    column = pl.BlockSpec((channels, SIDE), lambda i, f: (0, i))
    return pl.pallas_call(
        forward_kernel,
        out_shape=(
            jax.ShapeDtypeStruct((channels, rows), BF),
            jax.ShapeDtypeStruct((channels, rows), F32),
            jax.ShapeDtypeStruct((blocks, 1, width), F32),
        ),
        grid_spec=pltpu.PrefetchScalarGridSpec(
            num_scalar_prefetch=1,
            grid=(blocks,),
            in_specs=[column, pl.BlockSpec((1, SIDE), lambda i, f: (0, i)), whole, whole],
            out_specs=(column, column, pl.BlockSpec((1, 1, width), lambda i, f: (i, 0, 0))),
            scratch_shapes=[pltpu.VMEM((channels, width), BF), pltpu.VMEM((channels, SIDE), F32)],
        ),
        compiler_params=pltpu.CompilerParams(vmem_limit_bytes=32 * 2**20),
        cost_estimate=pl.CostEstimate(flops=6_000_000_000, bytes_accessed=6_000_000, transcendentals=4_000_000),
        name="attend_forward",
    )(first, q_t, start, k_ext, v_ext)


def backward_kernel(low_block, first_ref, q_ref, g_ref, exact_ref, lse_ref, start_ref, k_ref, v_ref, add_ref,
                    dq_ref, dk_ref, dv_ref, q_heads, g_heads, dq_acc, dk_acc, dv_acc):
    heads = q_ref.shape[0] // HD
    i = pl.program_id(0)
    blocks = pl.num_programs(0)
    halo = 4
    own = halo + i
    q_heads[...] = by_head(q_ref[...] * jnp.asarray(HD**-0.5, BF), heads)
    grad = g_ref[...]
    g_heads[...] = by_head(grad, heads)
    product = grad.astype(F32) * exact_ref[...]
    delta = jnp.concatenate(
        [jnp.sum(product[h * HD : (h + 1) * HD, :], axis=0, keepdims=True) for h in range(heads)], axis=1
    )
    dq_acc[...] = jnp.zeros_like(dq_acc)

    @pl.when(i == 0)
    def _():
        dk_acc[...] = jnp.zeros_like(dk_acc)
        dv_acc[...] = jnp.zeros_like(dv_acc)

    start_row = start_ref[...]
    lse = lse_ref[0]
    near = low_block != 0

    def step(j, carry):
        rows = pl.ds(pl.multiple_of((j - low_block) * SIDE, SIDE), SIDE)
        k_block = k_ref[rows, :]
        scores = dot(k_block, q_heads[...], 1, 0)
        allowed = pair_mask(start_row, own * SIDE, j * SIDE)
        scores = jnp.where(jnp.concatenate([allowed] * heads, axis=1), scores, NEGATIVE)
        weights = jnp.exp(scores - lse)
        grad_weights = dot(v_ref[rows, :], g_heads[...], 1, 0)
        grad_scores = (weights * (grad_weights - delta)).astype(BF)
        dv_acc[rows, :] += dot(weights.astype(BF), g_heads[...], 1, 1)
        dk_acc[rows, :] += dot(grad_scores, q_heads[...], 1, 1)
        k_t = k_block.T
        for h in range(heads):
            at, cols = slice(h * HD, (h + 1) * HD), slice(h * SIDE, (h + 1) * SIDE)
            dq_acc[at, :] += dot(k_t[at, :], grad_scores[:, cols], 1, 0)
        return carry

    first = first_ref[i]
    if near:
        lax.fori_loop(jnp.maximum(first, low_block), own + 1, step, 0)
        dq_ref[...] = (dq_acc[...] * HD**-0.5 + add_ref[...]).T.astype(BF)
    else:
        lax.fori_loop(first, halo, step, 0)
        dq_ref[...] = dq_acc[...] * HD**-0.5

    @pl.when(i == blocks - 1)
    def _():
        dk_ref[...] = dk_acc[...].astype(BF)
        dv_ref[...] = dv_acc[...].astype(BF)


def far_kernel(first_ref, q_ref, g_ref, exact_ref, lse_ref, start_ref, k_ref, v_ref,
               dq_ref, dk_ref, dv_ref, q_heads, g_heads, dq_acc, dk_acc, dv_acc):
    backward_kernel(0, first_ref, q_ref, g_ref, exact_ref, lse_ref, start_ref, k_ref, v_ref, None,
                    dq_ref, dk_ref, dv_ref, q_heads, g_heads, dq_acc, dk_acc, dv_acc)


def near_kernel(*refs):
    backward_kernel(4, *refs)


def attend_backward(near, first, q_t, g_t, exact_t, lse, start, k_part, v_part, add=None):
    channels, rows = q_t.shape
    blocks = rows // SIDE
    width = channels // HD * SIDE
    whole = pl.BlockSpec(k_part.shape, lambda i, f: (0, 0))
    column = pl.BlockSpec((channels, SIDE), lambda i, f: (0, i))
    in_specs = [
        column, column, column,
        pl.BlockSpec((1, 1, width), lambda i, f: (i, 0, 0)),
        pl.BlockSpec((1, SIDE), lambda i, f: (0, i)),
        whole, whole,
    ]
    args = [first, q_t, g_t, exact_t, lse, start, k_part, v_part]
    if near:
        in_specs.append(column)
        args.append(add)
        dq_shape = jax.ShapeDtypeStruct((rows, channels), BF)
        dq_spec = pl.BlockSpec((SIDE, channels), lambda i, f: (i, 0))
    else:
        dq_shape = jax.ShapeDtypeStruct((channels, rows), F32)
        dq_spec = column
    return pl.pallas_call(
        near_kernel if near else far_kernel,
        out_shape=(dq_shape, jax.ShapeDtypeStruct(k_part.shape, BF), jax.ShapeDtypeStruct(k_part.shape, BF)),
        grid_spec=pltpu.PrefetchScalarGridSpec(
            num_scalar_prefetch=1,
            grid=(blocks,),
            in_specs=in_specs,
            out_specs=(dq_spec, whole, whole),
            scratch_shapes=[
                pltpu.VMEM((channels, width), BF),
                pltpu.VMEM((channels, width), BF),
                pltpu.VMEM((channels, SIDE), F32),
                pltpu.VMEM(k_part.shape, F32),
                pltpu.VMEM(k_part.shape, F32),
            ],
        ),
        compiler_params=pltpu.CompilerParams(vmem_limit_bytes=32 * 2**20),
        cost_estimate=pl.CostEstimate(flops=9_000_000_000, bytes_accessed=6_000_000, transcendentals=4_000_000),
        name="attend_near" if near else "attend_far",
    )(*args)


def normalized(values):
    centre = values - jnp.mean(values, axis=-1, keepdims=True)
    variance = jnp.mean(centre * centre, axis=-1, keepdims=True)
    inverse = lax.rsqrt(variance + EPSILON)
    return centre * inverse, inverse


def norm_backward(grad_out, normed, inverse, gain_row):
    scaled = grad_out * gain_row
    inner = jnp.mean(scaled, axis=-1, keepdims=True)
    along = jnp.mean(scaled * normed, axis=-1, keepdims=True)
    return inverse * (scaled - inner - normed * along)


def gather_rows(shard, axis, peers):
    return lax.all_to_all(jnp.broadcast_to(shard[None], (peers, *shard.shape)), axis, 0, 0, tiled=True)


def summed_on_arrival(whole, axis, peers):
    tiles = whole.reshape(peers, -1, whole.shape[-1])
    return lax.all_to_all(tiles, axis, 0, 0, tiled=True).astype(F32).sum(axis=0)


def on_device(tokens, cotangent, expert_ids, segment_ids, priority, w_qkv, w_out, norm_gains, norm_shifts,
              qv_bias, w_up, up_bias, w_down, down_bias):
    rows, model = tokens.shape
    channels = w_qkv.shape[2]
    heads = channels // HD
    seq_len = segment_ids.shape[0]
    f_count, c_count, t_count = (lax.axis_size(a) for a in ("fsdp", "ctx", "tp"))
    groups = f_count * c_count
    ctx_at, tp_at = lax.axis_index("ctx"), lax.axis_index("tp")
    held = w_up.shape[0]
    experts = held * groups
    capacity = (9 * seq_len + 8 * experts - 1) // (8 * experts)
    slots = experts * capacity
    shard = model // groups
    part = rows // t_count
    width = model // t_count
    forth = [(0, 1)]
    back = [(1, 0)]

    bias_column = jnp.pad(qv_bias.reshape(-1), (0, shard - qv_bias.size))[None]
    small = jnp.concatenate([norm_gains, norm_shifts, bias_column], axis=0).T
    small = jnp.pad(small, ((0, 0), (0, 128 - small.shape[1])))
    pack = jnp.concatenate([jnp.moveaxis(w_qkv, 0, 1).reshape(shard, 3 * channels), small], axis=1)
    earlier_ids = lax.ppermute(expert_ids + 1, "ctx", forth)[:, 0]
    packed = gather_rows(pack, FC, groups).reshape(model, -1)
    out_t = gather_rows(w_out.T, FC, groups).reshape(model, channels)
    qkv_full = packed[:, : 3 * channels]
    small = packed[:, 3 * channels : 3 * channels + 6].astype(F32)
    gain_rows = small[:, 0:2].T
    shift_rows = small[:, 2:5].T
    bias_rows = (
        small[:, 5].reshape(groups, shard)[:, : qv_bias.size].reshape(groups, 2, heads, -1)
        .transpose(1, 2, 0, 3).reshape(2, channels)
    )
    out_full = lax.all_gather(out_t.T, "tp", axis=0, tiled=True)

    owner = expert_ids[:, 0]
    rank = priority[0]
    before = (owner[None, :] == owner[:, None]) & (rank[None, :] < rank[:, None])
    carried = earlier_ids[None, :] == owner[:, None] + 1
    slot = jnp.sum(before.astype(jnp.int32), axis=1) + jnp.sum(carried.astype(jnp.int32), axis=1)
    target = jnp.where(slot < capacity, owner * capacity + slot, slots)
    place = (lax.broadcasted_iota(jnp.int32, (slots, rows), 0) == target[None, :]).astype(BF)

    def to_experts(columns):
        sent = dot(place, columns, 1, 0).astype(BF).reshape(groups, held * capacity, width)
        got = lax.all_to_all(sent, FC, 0, 0, tiled=True).reshape(f_count, c_count, held, capacity, width)
        mine = (got[:, 0] + got[:, 1]).transpose(1, 0, 2, 3).reshape(held, f_count * capacity, width)
        return lax.all_gather(mine, "tp", axis=2, tiled=True)

    def from_experts(mine):
        spread = mine.reshape(held, f_count, 1, capacity, width).transpose(1, 2, 0, 3, 4)
        spread = jnp.broadcast_to(spread, (f_count, c_count, held, capacity, width))
        got = lax.all_to_all(spread.reshape(groups, held * capacity, width), FC, 0, 0, tiled=True)
        return dot(place, got.reshape(slots, width), 0, 0).astype(BF)

    cot_columns = lax.dynamic_slice_in_dim(cotangent, tp_at * width, width, 1)
    expert_grads = to_experts(cot_columns)
    active_grad = jnp.einsum("emd,efd->emf", expert_grads, w_down, preferred_element_type=F32)

    inputs = tokens.astype(F32)
    normed_all, _ = normalized(inputs)
    first_low = (normed_all * gain_rows[0] + shift_rows[0]).astype(BF)
    k_low = dot(first_low, qkv_full[:, channels : 2 * channels], 1, 0).astype(BF)
    v_low = (dot(first_low, qkv_full[:, 2 * channels :], 1, 0) + bias_rows[1]).astype(BF)
    kv_far = lax.ppermute(jnp.concatenate([k_low[rows - REACH :], v_low[rows - REACH :]], axis=1), "ctx", forth)
    kv_far = jnp.pad(kv_far, ((rows - REACH, 0), (0, 0)))
    k_far, v_far = kv_far[:, :channels], kv_far[:, channels:]
    q_t = (dot(qkv_full[:, :channels], first_low, 0, 1) + bias_rows[0][:, None]).astype(BF)
    seg_own = lax.dynamic_slice_in_dim(segment_ids, ctx_at * rows, rows)
    start = jnp.sum((segment_ids[None, :] < seg_own[:, None]).astype(jnp.int32), axis=1)
    start = start + jnp.where(ctx_at == 0, rows, 0)
    first = start[::SIDE] // SIDE
    start = start[None, :]
    mixed_t, exact_t, lse = attend_forward(
        first, q_t, start, jnp.concatenate([k_far, k_low]), jnp.concatenate([v_far, v_low])
    )
    mixed_rows_t = lax.all_to_all(mixed_t, "tp", 1, 0, tiled=True)

    inputs_part = lax.dynamic_slice_in_dim(tokens, tp_at * part, part).astype(F32)
    cot_part = lax.dynamic_slice_in_dim(cotangent, tp_at * part, part).astype(F32)
    middle = inputs_part + (dot(mixed_rows_t, out_full, 0, 0) + shift_rows[2])
    normed_two, inverse_two = normalized(middle)
    second_low = (normed_two * gain_rows[1] + shift_rows[1]).astype(BF)
    second_columns = lax.all_to_all(second_low, "tp", 1, 0, tiled=True)

    expert_rows = to_experts(second_columns)
    hidden = (
        jnp.einsum("emd,edf->emf", expert_rows, w_up, preferred_element_type=F32)
        + up_bias.astype(F32)[:, None, :]
    )
    sigmoid_hidden = jax.nn.sigmoid(hidden)
    active_low = (hidden * sigmoid_hidden).astype(BF)
    slope = sigmoid_hidden * (1.0 + hidden * (1.0 - sigmoid_hidden))
    hidden_grad = (active_grad * slope).astype(BF)
    input_part = jnp.einsum("emf,edf->emd", hidden_grad, w_up, preferred_element_type=F32).astype(BF)
    input_low = lax.psum_scatter(input_part, "tp", scatter_dimension=2, tiled=True)
    grad_columns = from_experts(input_low)
    second_grad = lax.all_to_all(grad_columns, "tp", 0, 1, tiled=True).astype(F32)

    result_part = jnp.einsum("emf,efd->emd", active_low, w_down, preferred_element_type=F32).astype(BF)
    bias_columns = lax.dynamic_slice_in_dim(down_bias, tp_at * width, width, 1)
    result_sum = lax.psum_scatter(result_part, "tp", scatter_dimension=2, tiled=True)
    result_low = (result_sum.astype(F32) + bias_columns.astype(F32)[:, None, :]).astype(BF)
    expert_out = lax.all_to_all(from_experts(result_low), "tp", 0, 1, tiled=True)
    block_part = (middle + expert_out.astype(F32)).astype(BF)
    block_out = lax.all_gather(block_part, "tp", axis=0, tiled=True)

    w_up_grad = jnp.einsum("emd,emf->edf", expert_rows, hidden_grad, preferred_element_type=F32)
    w_down_grad = jnp.einsum("emf,emd->efd", active_low, expert_grads, preferred_element_type=F32)
    up_bias_grad = jnp.sum(hidden_grad.astype(F32), axis=1)
    down_bias_grad = jnp.sum(expert_grads.astype(F32), axis=1)

    middle_grad = cot_part + norm_backward(second_grad, normed_two, inverse_two, gain_rows[1])
    branch_low = middle_grad.astype(BF)
    grad_rows_t = dot(out_full, branch_low, 1, 1).astype(BF)
    grad_t = lax.all_to_all(grad_rows_t, "tp", 0, 1, tiled=True)
    branch_all = lax.all_gather(branch_low, "tp", axis=0, tiled=True)
    out_grad_t = dot(branch_all, mixed_t, 0, 1).astype(BF)
    out_shard = summed_on_arrival(out_grad_t, FC, groups).T

    dq_far, dk_far, dv_far = attend_backward(False, first, q_t, grad_t, exact_t, lse, start, k_far, v_far)
    kv_back = lax.ppermute(
        jnp.concatenate([dk_far[rows - REACH :], dv_far[rows - REACH :]], axis=1), "ctx", back
    )
    dq, dk, dv = attend_backward(True, first, q_t, grad_t, exact_t, lse, start, k_low, v_low, dq_far)
    kv_grad = jnp.concatenate([dk, dv], axis=1).astype(F32) + jnp.pad(kv_back, ((rows - REACH, 0), (0, 0))).astype(F32)
    stacked = jnp.concatenate([dq, kv_grad.astype(BF)], axis=1)
    first_part = dot(stacked, qkv_full, 1, 1).astype(BF)
    first_grad = lax.psum_scatter(first_part, "tp", scatter_dimension=0, tiled=True).astype(F32)
    qkv_grad = dot(first_low, stacked, 0, 0).astype(BF)
    qkv_shard = jnp.moveaxis(summed_on_arrival(qkv_grad, FC, groups).reshape(shard, 3, channels), 1, 0)

    normed_one, inverse_one = normalized(inputs_part)
    tokens_part = (middle_grad + norm_backward(first_grad, normed_one, inverse_one, gain_rows[0])).astype(BF)
    tokens_grad = lax.all_gather(tokens_part, "tp", axis=0, tiled=True)

    sums = jnp.stack([
        jnp.sum(first_grad * normed_one, axis=0),
        jnp.sum(second_grad * normed_two, axis=0),
        jnp.sum(first_grad, axis=0),
        jnp.sum(second_grad, axis=0),
        jnp.sum(branch_low.astype(F32), axis=0),
    ])
    stacked_sum = jnp.sum(stacked.astype(F32), axis=0)
    bias_sum = jnp.stack([stacked_sum[:channels], stacked_sum[2 * channels :]])
    sums = jnp.sum(lax.all_gather(sums, "tp", axis=0), axis=0)
    bias_tiles = bias_sum.reshape(2, heads, groups, -1).transpose(2, 0, 1, 3).reshape(groups, -1)
    sum_tiles = sums.reshape(-1, groups, shard).transpose(1, 0, 2).reshape(groups, -1)
    tail = jnp.concatenate([sum_tiles, bias_tiles], axis=1)
    tail = jnp.pad(tail, ((0, 0), (0, 256 - tail.shape[1]))).reshape(groups, 1, 256)
    tail = jnp.sum(lax.all_to_all(tail, FC, 0, 0, tiled=True), axis=0)[0]
    norm_shard = tail[: 5 * shard].reshape(5, shard)
    bias_shard = tail[5 * shard : 5 * shard + qv_bias.size].reshape(qv_bias.shape)
    return (block_out, tokens_grad, qkv_shard, out_shard, norm_shard[:2], norm_shard[2:], bias_shard,
            w_up_grad, up_bias_grad, w_down_grad, down_bias_grad)


def solution(mesh):
    token, weight = P(FC, None), P(None, FC)
    experts = P(FC, None, "tp"), P(FC, "tp"), P(FC, "tp", None), P(FC, None)
    shared = P(None, FC, "tp"), P("tp", FC), weight, weight, P(None, "tp", FC)
    return jax.shard_map(
        on_device,
        mesh=mesh,
        in_specs=(token, token, token, P("fsdp"), token, *shared, *experts),
        out_specs=(token, token, *shared, *experts),
        check_vma=False,
    )
```

```python
import functools

import jax
import jax.numpy as jnp
from jax import lax
from jax.experimental import pallas as pl
from jax.experimental.pallas import tpu as pltpu
from jax.sharding import Mesh, PartitionSpec as P

HD = 64
EPSILON = 1e-05
NEGATIVE = -1e30
REACH = 800
SIDE = 256
FC = ("y_hi", "z", "core", "ctx")
Y = ("y_hi", "ctx")
PARTS = 4
VMEM = 40 * 2**20
BF = jnp.bfloat16
F32 = jnp.float32


def dot(a, b, ca, cb):
    return lax.dot_general(a, b, (((ca,), (cb,)), ((), ())), preferred_element_type=F32)


def by_head(cols, heads):
    row = lax.broadcasted_iota(jnp.int32, cols.shape, 0) // HD
    zero = jnp.zeros_like(cols)
    return jnp.concatenate([jnp.where(row == h, cols, zero) for h in range(heads)], axis=1)


def pair_mask(start_row, q_first, k_first):
    k_pos = lax.broadcasted_iota(jnp.int32, (SIDE, SIDE), 0) + k_first
    q_pos = lax.broadcasted_iota(jnp.int32, (SIDE, SIDE), 1) + q_first
    return (k_pos >= start_row) & (k_pos <= q_pos)


def forward_kernel(at_ref, q_ref, start_ref, k_ref, v_ref, o_ref, exact_ref, lse_ref, q_heads, acc):
    heads = q_ref.shape[0] // HD
    i = pl.program_id(0)
    own = k_ref.shape[0] // SIDE - pl.num_programs(0) + i
    q_heads[...] = by_head(q_ref[...] * jnp.asarray(HD**-0.5, BF), heads)
    acc[...] = jnp.zeros_like(acc)
    start_row = start_ref[...]

    def step(n, carry):
        peak, total = carry
        j = own - n
        rows = pl.ds(pl.multiple_of(j * SIDE, SIDE), SIDE)
        scores = dot(k_ref[rows, :], q_heads[...], 1, 0)
        allowed = pair_mask(start_row, own * SIDE, j * SIDE)
        scores = jnp.where(jnp.concatenate([allowed] * heads, axis=1), scores, NEGATIVE)
        new_peak = jnp.maximum(peak, jnp.max(scores, axis=0, keepdims=True))
        fade = jnp.exp(peak - new_peak)
        weights = jnp.exp(scores - new_peak)
        total = total * fade + jnp.sum(weights, axis=0, keepdims=True)
        low = weights.astype(BF)
        v_t = v_ref[rows, :].T
        for h in range(heads):
            at, cols = slice(h * HD, (h + 1) * HD), slice(h * SIDE, (h + 1) * SIDE)
            acc[at, :] = acc[at, :] * fade[:, cols] + dot(v_t[at, :], low[:, cols], 1, 0)
        return new_peak, total

    width = heads * SIDE
    peak, total = lax.fori_loop(
        0, own - at_ref[i] + 1, step, (jnp.full((1, width), NEGATIVE, F32), jnp.zeros((1, width), F32))
    )
    scale = 1.0 / total
    for h in range(heads):
        at, cols = slice(h * HD, (h + 1) * HD), slice(h * SIDE, (h + 1) * SIDE)
        exact = acc[at, :] * scale[:, cols]
        exact_ref[at, :] = exact
        o_ref[at, :] = exact.astype(BF)
    lse_ref[0] = peak + jnp.log(total)


def turned(i, at):
    return lax.rem(i + PARTS - at[PARTS], PARTS)


def attend_forward(at, q_t, start, k_ext, v_ext):
    channels, rows = q_t.shape
    blocks = rows // SIDE
    width = channels // HD * SIDE
    whole = pl.BlockSpec(k_ext.shape, lambda i, f: (0, 0))
    column = pl.BlockSpec((channels, SIDE), lambda i, f: (0, i))
    return pl.pallas_call(
        forward_kernel,
        out_shape=(
            jax.ShapeDtypeStruct((channels, rows), BF),
            jax.ShapeDtypeStruct((channels, rows), F32),
            jax.ShapeDtypeStruct((blocks, 1, width), F32),
        ),
        grid_spec=pltpu.PrefetchScalarGridSpec(
            num_scalar_prefetch=1,
            grid=(blocks,),
            in_specs=[column, pl.BlockSpec((1, SIDE), lambda i, f: (0, i)), whole, whole],
            out_specs=(
                pl.BlockSpec((channels, SIDE), lambda i, f: (0, turned(i, f))),
                column,
                pl.BlockSpec((1, 1, width), lambda i, f: (i, 0, 0)),
            ),
            scratch_shapes=[pltpu.VMEM((channels, width), BF), pltpu.VMEM((channels, SIDE), F32)],
        ),
        compiler_params=pltpu.CompilerParams(vmem_limit_bytes=VMEM),
        cost_estimate=pl.CostEstimate(flops=6_000_000_000, bytes_accessed=6_000_000, transcendentals=4_000_000),
        name="attend_forward",
    )(at, q_t, start, k_ext, v_ext)


def backward_kernel(low_block, at_ref, q_ref, g_ref, exact_ref, lse_ref, start_ref, k_ref, v_ref, add_ref,
                    dq_ref, dk_ref, dv_ref, q_heads, g_heads, dq_acc, dk_acc, dv_acc):
    heads = q_ref.shape[0] // HD
    i = pl.program_id(0)
    blocks = pl.num_programs(0)
    halo = PARTS
    own = halo + i
    q_heads[...] = by_head(q_ref[...] * jnp.asarray(HD**-0.5, BF), heads)
    grad = g_ref[...]
    g_heads[...] = by_head(grad, heads)
    product = grad.astype(F32) * exact_ref[...]
    delta = jnp.concatenate(
        [jnp.sum(product[h * HD : (h + 1) * HD, :], axis=0, keepdims=True) for h in range(heads)], axis=1
    )
    dq_acc[...] = jnp.zeros_like(dq_acc)

    @pl.when(i == 0)
    def _():
        dk_acc[...] = jnp.zeros_like(dk_acc)
        dv_acc[...] = jnp.zeros_like(dv_acc)

    start_row = start_ref[...]
    lse = lse_ref[0]

    def step(j, carry):
        rows = pl.ds(pl.multiple_of((j - low_block) * SIDE, SIDE), SIDE)
        k_block = k_ref[rows, :]
        scores = dot(k_block, q_heads[...], 1, 0)
        allowed = pair_mask(start_row, own * SIDE, j * SIDE)
        scores = jnp.where(jnp.concatenate([allowed] * heads, axis=1), scores, NEGATIVE)
        weights = jnp.exp(scores - lse)
        grad_weights = dot(v_ref[rows, :], g_heads[...], 1, 0)
        grad_scores = (weights * (grad_weights - delta)).astype(BF)
        dv_acc[rows, :] += dot(weights.astype(BF), g_heads[...], 1, 1)
        dk_acc[rows, :] += dot(grad_scores, q_heads[...], 1, 1)
        k_t = k_block.T
        for h in range(heads):
            at, cols = slice(h * HD, (h + 1) * HD), slice(h * SIDE, (h + 1) * SIDE)
            dq_acc[at, :] += dot(k_t[at, :], grad_scores[:, cols], 1, 0)
        return carry

    first = at_ref[i]
    if low_block:
        lax.fori_loop(jnp.maximum(first, low_block), own + 1, step, 0)
        dq_ref[...] = (dq_acc[...] * HD**-0.5 + add_ref[...]).T.astype(BF)
    else:
        lax.fori_loop(first, halo, step, 0)
        dq_ref[...] = dq_acc[...] * HD**-0.5

    @pl.when(i == blocks - 1)
    def _():
        dk_ref[...] = dk_acc[...].astype(BF)
        dv_ref[...] = dv_acc[...].astype(BF)


def far_kernel(at_ref, q_ref, g_ref, exact_ref, lse_ref, start_ref, k_ref, v_ref, *rest):
    backward_kernel(0, at_ref, q_ref, g_ref, exact_ref, lse_ref, start_ref, k_ref, v_ref, None, *rest)


def near_kernel(*refs):
    backward_kernel(PARTS, *refs)


def attend_backward(near, at, q_t, g_t, exact_t, lse, start, k_part, v_part, add=None):
    channels, rows = q_t.shape
    blocks = rows // SIDE
    width = channels // HD * SIDE
    whole = pl.BlockSpec(k_part.shape, lambda i, f: (0, 0))
    column = pl.BlockSpec((channels, SIDE), lambda i, f: (0, i))
    in_specs = [
        column,
        pl.BlockSpec((channels, SIDE), lambda i, f: (0, turned(i, f))),
        column,
        pl.BlockSpec((1, 1, width), lambda i, f: (i, 0, 0)),
        pl.BlockSpec((1, SIDE), lambda i, f: (0, i)),
        whole, whole,
    ]
    args = [at, q_t, g_t, exact_t, lse, start, k_part, v_part]
    if near:
        in_specs.append(column)
        args.append(add)
        dq_shape = jax.ShapeDtypeStruct((rows, channels), BF)
        dq_spec = pl.BlockSpec((SIDE, channels), lambda i, f: (i, 0))
    else:
        dq_shape = jax.ShapeDtypeStruct((channels, rows), F32)
        dq_spec = column
    return pl.pallas_call(
        near_kernel if near else far_kernel,
        out_shape=(dq_shape, jax.ShapeDtypeStruct(k_part.shape, BF), jax.ShapeDtypeStruct(k_part.shape, BF)),
        grid_spec=pltpu.PrefetchScalarGridSpec(
            num_scalar_prefetch=1,
            grid=(blocks,),
            in_specs=in_specs,
            out_specs=(dq_spec, whole, whole),
            scratch_shapes=[
                pltpu.VMEM((channels, width), BF),
                pltpu.VMEM((channels, width), BF),
                pltpu.VMEM((channels, SIDE), F32),
                pltpu.VMEM(k_part.shape, F32),
                pltpu.VMEM(k_part.shape, F32),
            ],
        ),
        compiler_params=pltpu.CompilerParams(vmem_limit_bytes=VMEM),
        cost_estimate=pl.CostEstimate(flops=9_000_000_000, bytes_accessed=6_000_000, transcendentals=4_000_000),
        name="attend_near" if near else "attend_far",
    )(*args)


def slots_kernel(target_ref, x_ref, o_ref):
    place = lax.broadcasted_iota(jnp.int32, (o_ref.shape[0], x_ref.shape[0]), 0) + pl.program_id(0) * o_ref.shape[0]
    o_ref[...] = dot((place == target_ref[...]).astype(F32).astype(BF), x_ref[...], 1, 0).astype(BF)


def to_slots(target, x, slots):
    return pl.pallas_call(
        slots_kernel,
        out_shape=jax.ShapeDtypeStruct((slots, x.shape[1]), BF),
        grid=(slots // SIDE,),
        in_specs=[pl.BlockSpec((1, x.shape[0]), lambda i: (0, 0)), pl.BlockSpec(x.shape, lambda i: (0, 0))],
        out_specs=pl.BlockSpec((SIDE, x.shape[1]), lambda i: (i, 0)),
        compiler_params=pltpu.CompilerParams(vmem_limit_bytes=VMEM),
        cost_estimate=pl.CostEstimate(flops=1_200_000_000, bytes_accessed=2_000_000, transcendentals=0),
        name="to_slots",
    )(target[None, :], x)


def tokens_kernel(target_ref, x_ref, o_ref):
    place = lax.broadcasted_iota(jnp.int32, (o_ref.shape[0], x_ref.shape[0]), 1)
    o_ref[...] = dot((place == target_ref[...]).astype(F32).astype(BF), x_ref[...], 1, 0).astype(BF)


def to_tokens(target, x):
    rows = target.shape[0]
    return pl.pallas_call(
        tokens_kernel,
        out_shape=jax.ShapeDtypeStruct((rows, x.shape[1]), BF),
        grid=(rows // SIDE,),
        in_specs=[pl.BlockSpec((SIDE, 1), lambda i: (i, 0)), pl.BlockSpec(x.shape, lambda i: (0, 0))],
        out_specs=pl.BlockSpec((SIDE, x.shape[1]), lambda i: (i, 0)),
        compiler_params=pltpu.CompilerParams(vmem_limit_bytes=VMEM),
        cost_estimate=pl.CostEstimate(flops=1_200_000_000, bytes_accessed=2_000_000, transcendentals=0),
        name="to_tokens",
    )(target[:, None], x)


def join_kernel(got_ref, o_ref, held):
    capacity = got_ref.shape[1] // o_ref.shape[0]
    for f in range(got_ref.shape[0] // 2):
        both = got_ref[2 * f].astype(F32) + got_ref[2 * f + 1].astype(F32)
        for e in range(o_ref.shape[0]):
            held[e, f * capacity : (f + 1) * capacity, :] = both[e * capacity : (e + 1) * capacity, :]
    o_ref[...] = held[...].astype(BF)


def join(got, experts):
    shape = (experts, got.shape[0] // 2 * (got.shape[1] // experts), got.shape[2])
    return pl.pallas_call(
        join_kernel,
        out_shape=jax.ShapeDtypeStruct(shape, BF),
        scratch_shapes=[pltpu.VMEM(shape, F32)],
        compiler_params=pltpu.CompilerParams(vmem_limit_bytes=VMEM),
        cost_estimate=pl.CostEstimate(flops=600_000, bytes_accessed=2_000_000, transcendentals=0),
        name="join",
    )(got)


def spread_kernel(bias_ref, *refs):
    o_ref, held, piece = refs[-3:]
    experts = held.shape[0]
    capacity = o_ref.shape[1] // experts
    for e in range(experts):
        total = refs[e * PARTS][...].astype(F32)
        for s in range(1, PARTS):
            total += refs[e * PARTS + s][...].astype(F32)
        held[e] = total + bias_ref[e : e + 1, :]
    for f in range(o_ref.shape[0] // 2):
        for e in range(experts):
            piece[e * capacity : (e + 1) * capacity, :] = held[e, f * capacity : (f + 1) * capacity, :]
        low = piece[...].astype(BF)
        o_ref[2 * f] = low
        o_ref[2 * f + 1] = low


def spread(parts, bias, capacity):
    experts = len(parts)
    rows, n = parts[0][0].shape
    return pl.pallas_call(
        spread_kernel,
        out_shape=jax.ShapeDtypeStruct((rows // capacity * 2, experts * capacity, n), BF),
        scratch_shapes=[pltpu.VMEM((experts, rows, n), F32), pltpu.VMEM((experts * capacity, n), F32)],
        compiler_params=pltpu.CompilerParams(vmem_limit_bytes=VMEM),
        cost_estimate=pl.CostEstimate(flops=2_400_000, bytes_accessed=4_000_000, transcendentals=0),
        name="spread",
    )(bias, *[p for e in parts for p in e])


def expert_kernel(at_ref, r0, r1, r2, r3, w_ref, b_ref, g_ref, act_ref, hg_ref, o_ref, acc):
    rows = (r0, r1, r2, r3)
    n = r0.shape[1]
    j = pl.program_id(0)

    def weights(s):
        place = lax.rem(at_ref[PARTS] + PARTS - s, PARTS)
        return w_ref[0, pl.ds(pl.multiple_of(place * n, n), n), :]

    hidden = b_ref[0].astype(F32)
    for s in range(PARTS):
        hidden = hidden + dot(rows[s][...], weights(s), 1, 0)
    gate = jax.nn.sigmoid(hidden)
    act_ref[...] = (hidden * gate).astype(BF)
    grad = (g_ref[...] * (gate * (1.0 + hidden * (1.0 - gate)))).astype(BF)
    hg_ref[...] = grad

    for s in range(PARTS):
        here = dot(grad, weights(s), 1, 1)

        @pl.when(j == 0)
        def _():
            acc[s] = here

        @pl.when(j > 0)
        def _():
            acc[s] += here

    @pl.when(j == pl.num_programs(0) - 1)
    def _():
        o_ref[...] = acc[...].astype(BF)


def run_expert(e, at, parts, w_up, up_bias, active_grad):
    rows, n = parts[0].shape
    inner = w_up.shape[2]
    whole = pl.BlockSpec((rows, n), lambda j, f: (0, 0))
    block = pl.BlockSpec((rows, SIDE), lambda j, f: (0, j))
    return pl.pallas_call(
        expert_kernel,
        out_shape=(
            jax.ShapeDtypeStruct((rows, inner), BF),
            jax.ShapeDtypeStruct((rows, inner), BF),
            jax.ShapeDtypeStruct((PARTS, rows, n), BF),
        ),
        grid_spec=pltpu.PrefetchScalarGridSpec(
            num_scalar_prefetch=1,
            grid=(inner // SIDE,),
            in_specs=[whole] * PARTS + [
                pl.BlockSpec((1, w_up.shape[1], SIDE), lambda j, f: (e, 0, j)),
                pl.BlockSpec((1, 1, SIDE), lambda j, f: (e, 0, j)),
                block,
            ],
            out_specs=(block, block, pl.BlockSpec((PARTS, rows, n), lambda j, f: (0, 0, 0))),
            scratch_shapes=[pltpu.VMEM((PARTS, rows, n), F32)],
        ),
        compiler_params=pltpu.CompilerParams(vmem_limit_bytes=VMEM),
        cost_estimate=pl.CostEstimate(flops=2_400_000_000, bytes_accessed=8_000_000, transcendentals=600_000),
        name="expert",
    )(at, *parts, w_up, up_bias[:, None, :], active_grad)


def place_kernel(axis, step, at_ref, *refs):
    parts, o_ref, sems = refs[:-2], refs[-2], refs[-1]
    copies = []
    for s, part in enumerate(parts):
        place = lax.rem(at_ref[PARTS] + step * s + PARTS, PARTS)
        n = part.shape[axis]
        window = pl.ds(pl.multiple_of(place * n, n), n)
        target = o_ref.at[window, :] if axis == 0 else o_ref.at[:, window]
        copies.append(pltpu.make_async_copy(part, target, sems.at[s]))
    for copy in copies:
        copy.start()
    for copy in copies:
        copy.wait()


def placed(at, parts, axis, step):
    shape = list(parts[0].shape)
    shape[axis] *= PARTS
    hbm = pl.BlockSpec(memory_space=pl.ANY)
    return pl.pallas_call(
        functools.partial(place_kernel, axis, step),
        out_shape=jax.ShapeDtypeStruct(tuple(shape), parts[0].dtype),
        grid_spec=pltpu.PrefetchScalarGridSpec(
            num_scalar_prefetch=1,
            grid=(1,),
            in_specs=[hbm] * PARTS,
            out_specs=hbm,
            scratch_shapes=[pltpu.SemaphoreType.DMA((PARTS,))],
        ),
        cost_estimate=pl.CostEstimate(flops=0, bytes_accessed=4_000_000, transcendentals=0),
        name="placed",
    )(at, *parts)


def weights_kernel(widths, at_ref, mine_ref, other_ref, *refs):
    outs, sems = refs[:-1], refs[-1]
    y, z, core = at_ref[0], at_ref[1], at_ref[2]
    copies = []
    for q, source in enumerate((mine_ref, other_ref)):
        for r in range(4):
            for s in range(4):
                from_y, from_z = lax.rem(y + 4 - r, 4), lax.rem(z + 4 - s, 4)
                block = ((from_y // 2 * 4 + from_z) * 2 + lax.rem(core + q, 2)) * 2 + lax.rem(from_y, 2)
                n = source.shape[1]
                first = 0
                for k, out in enumerate(outs):
                    window = pl.ds(pl.multiple_of(block * n, n), n)
                    copies.append(pltpu.make_async_copy(
                        source.at[r * 4 + s, :, pl.ds(first, widths[k])],
                        out.at[window, :],
                        sems.at[k, q * 16 + r * 4 + s],
                    ))
                    first += widths[k]
    for copy in copies:
        copy.start()
    for copy in copies:
        copy.wait()


def ordered_weights(at, mine, other, widths):
    model = 2 * mine.shape[0] * mine.shape[1]
    hbm = pl.BlockSpec(memory_space=pl.ANY)
    return pl.pallas_call(
        functools.partial(weights_kernel, widths),
        out_shape=tuple(jax.ShapeDtypeStruct((model, w), mine.dtype) for w in widths),
        grid_spec=pltpu.PrefetchScalarGridSpec(
            num_scalar_prefetch=1,
            grid=(1,),
            in_specs=[hbm] * 2,
            out_specs=(hbm,) * len(widths),
            scratch_shapes=[pltpu.SemaphoreType.DMA((len(widths), 2 * mine.shape[0]))],
        ),
        cost_estimate=pl.CostEstimate(flops=0, bytes_accessed=4_800_000, transcendentals=0),
        name="ordered_weights",
    )(at, mine, other)


def after(value, *others):
    return lax.optimization_barrier((value, *others))[0]


def hops(axis, s):
    n = lax.axis_size(axis)
    return [(i, (i + s) % n) for i in range(n)]


def swapped(blocks, sign):
    return [blocks[0]] + [lax.ppermute(blocks[s], "tp", hops("tp", sign * s)) for s in range(1, PARTS)]


def copied(block):
    return swapped([block] * PARTS, 1)


def from_all(shard, axis):
    return jnp.stack([shard] + [lax.ppermute(shard, axis, hops(axis, s)) for s in range(1, lax.axis_size(axis))])


def summed_on_arrival(whole, axis, peers):
    tiles = whole.reshape(peers, -1, whole.shape[-1])
    return lax.all_to_all(tiles, axis, 0, 0, tiled=True).astype(F32).sum(axis=0)


def in_order(parts, start, axis):
    turned_parts = [parts[-k % PARTS] for k in range(PARTS)]
    size = parts[0].shape[axis]
    both = jnp.concatenate(turned_parts + turned_parts[:-1], axis=axis)
    return lax.dynamic_slice_in_dim(both, (PARTS - start) % PARTS * size, PARTS * size, axis)


def normalized(values):
    centre = values - jnp.mean(values, axis=-1, keepdims=True)
    variance = jnp.mean(centre * centre, axis=-1, keepdims=True)
    inverse = lax.rsqrt(variance + EPSILON)
    return centre * inverse, inverse


def norm_backward(grad_out, normed, inverse, gain_row):
    scaled = grad_out * gain_row
    inner = jnp.mean(scaled, axis=-1, keepdims=True)
    along = jnp.mean(scaled * normed, axis=-1, keepdims=True)
    return inverse * (scaled - inner - normed * along)


def on_device(tokens, cotangent, expert_ids, segment_ids, priority, w_qkv, w_out, norm_gains, norm_shifts,
              qv_bias, w_up, up_bias, w_down, down_bias):
    rows, model = tokens.shape
    channels = w_qkv.shape[2]
    heads = channels // HD
    seq_len = segment_ids.shape[0]
    f_count, c_count = lax.axis_size(FC[:3]), lax.axis_size("ctx")
    groups = f_count * c_count
    ctx_at, tp_at = lax.axis_index("ctx"), lax.axis_index("tp")
    held = w_up.shape[0]
    experts = held * groups
    capacity = (9 * seq_len + 8 * experts - 1) // (8 * experts)
    slots = experts * capacity
    shard = model // groups
    part = rows // PARTS
    width = model // PARTS

    bias_column = jnp.pad(qv_bias.reshape(-1), (0, shard - qv_bias.size))[None]
    small = jnp.concatenate([norm_gains, norm_shifts, bias_column], axis=0).T
    small = jnp.pad(small, ((0, 0), (0, 128 - small.shape[1])))
    pack = jnp.concatenate([jnp.moveaxis(w_qkv, 0, 1).reshape(shard, 3 * channels), w_out.T, small], axis=1)
    plane = from_all(from_all(pack, "z"), Y).reshape(PARTS * PARTS, shard, pack.shape[1])
    chip = jnp.stack([lax.axis_index(Y), lax.axis_index("z"), lax.axis_index("core")])
    qkv_full, out_t, small = ordered_weights(
        chip, plane, lax.ppermute(plane, "core", hops("core", 1)), (3 * channels, channels, 128)
    )
    small = small[:, :6].astype(F32)
    gain_rows = small[:, 0:2].T
    shift_rows = small[:, 2:5].T
    bias_rows = (
        small[:, 5].reshape(groups, shard)[:, : qv_bias.size].reshape(groups, 2, heads, -1)
        .transpose(1, 2, 0, 3).reshape(2, channels)
    )
    out_all = jnp.concatenate(copied(out_t), axis=1)

    owner = expert_ids[:, 0]
    rank = priority[0]
    earlier_ids = lax.ppermute(expert_ids + 1, "ctx", [(0, 1)])[:, 0]
    before = (owner[None, :] == owner[:, None]) & (rank[None, :] < rank[:, None])
    carried = earlier_ids[None, :] == owner[:, None] + 1
    slot = jnp.sum(before.astype(jnp.int32), axis=1) + jnp.sum(carried.astype(jnp.int32), axis=1)
    target = jnp.where(slot < capacity, owner * capacity + slot, slots)
    places = [(tp_at + PARTS - s) % PARTS for s in range(PARTS)]
    target = jnp.concatenate([lax.dynamic_slice_in_dim(target, p * part, part) for p in places])

    def exchanged(sent):
        return lax.all_to_all(sent, FC, 0, 0, tiled=True)

    def sent_rows(columns):
        return to_slots(target, columns, slots).reshape(groups, held * capacity, width)

    cot_columns = [lax.dynamic_slice(cotangent, (p * part, tp_at * width), (part, width)) for p in places]
    cot_sent = sent_rows(jnp.concatenate(cot_columns))

    seg_own = lax.dynamic_slice_in_dim(segment_ids, ctx_at * rows, rows)
    start = jnp.sum((segment_ids[None, :] < seg_own[:, None]).astype(jnp.int32), axis=1)
    start = start + jnp.where(ctx_at == 0, rows, 0)
    at = jnp.concatenate([start[::SIDE] // SIDE, tp_at[None]]).astype(jnp.int32)
    start = start[None, :]
    inputs = tokens.astype(F32)
    normed_all, _ = normalized(inputs)
    first_low = (normed_all * gain_rows[0] + shift_rows[0]).astype(BF)
    k_low = dot(first_low, qkv_full[:, channels : 2 * channels], 1, 0).astype(BF)
    v_low = (dot(first_low, qkv_full[:, 2 * channels :], 1, 0) + bias_rows[1]).astype(BF)
    kv_near = jnp.concatenate([k_low[rows - REACH :], v_low[rows - REACH :]], axis=1)
    kv_far = lax.ppermute(kv_near, "ctx", [(0, 1)])
    cot_got = exchanged(after(cot_sent, kv_near))
    kv_far = jnp.pad(kv_far, ((rows - REACH, 0), (0, 0)))
    k_far, v_far = kv_far[:, :channels], kv_far[:, channels:]
    q_t = (dot(qkv_full[:, :channels], first_low, 0, 1) + bias_rows[0][:, None]).astype(BF)
    mixed_t, exact_t, lse = attend_forward(
        at, q_t, start, jnp.concatenate([k_far, k_low]), jnp.concatenate([v_far, v_low])
    )
    mixed = jnp.concatenate(swapped(jnp.split(mixed_t, PARTS, axis=1), 1))

    inputs_part = lax.dynamic_slice_in_dim(tokens, tp_at * part, part).astype(F32)
    cot_part = lax.dynamic_slice_in_dim(cotangent, tp_at * part, part).astype(F32)
    middle = inputs_part + (dot(mixed, out_all, 0, 1) + shift_rows[2])
    normed_two, inverse_two = normalized(middle)
    second_low = (normed_two * gain_rows[1] + shift_rows[1]).astype(BF)

    def columns_for(values):
        return [
            lax.dynamic_slice_in_dim(values, (tp_at + s) % PARTS * width, width, 1) for s in range(PARTS)
        ]

    second_columns = jnp.concatenate(swapped(columns_for(second_low), 1))
    second_sent = sent_rows(second_columns)
    middle_columns = jnp.concatenate(swapped(columns_for(after(middle.astype(BF), second_sent)), 1))

    cot_mine = join(cot_got, held)
    second_sent, cot_mine = lax.optimization_barrier((second_sent, cot_mine))
    second_got = exchanged(second_sent)
    cot_parts = copied(cot_mine)
    cot_parts = lax.optimization_barrier((*cot_parts, second_got))
    second_got, cot_parts = cot_parts[PARTS], cot_parts[:PARTS]
    mine = join(second_got, held)
    expert_grads = in_order(cot_parts, tp_at, 2)
    active_grad = jnp.einsum("emd,efd->emf", expert_grads, w_down, preferred_element_type=F32)
    parts = [copied(mine[e]) for e in range(held)]
    done = []
    for e in range(held):
        done.append(run_expert(e, at, parts[e], w_up, up_bias, active_grad[e]))
    back_parts = [swapped([o[s] for s in range(PARTS)], -1) for _, _, o in done]
    active_low = jnp.stack([a for a, _, _ in done])
    hidden_grad = jnp.stack([h for _, h, _ in done])
    expert_rows = jnp.stack([in_order(p, tp_at, 1) for p in parts])
    result_part = jnp.einsum("emf,efd->emd", active_low, w_down, preferred_element_type=F32).astype(BF)
    w_down_grad = jnp.einsum("emf,emd->efd", active_low, expert_grads, preferred_element_type=F32)
    w_up_grad = jnp.einsum("emd,emf->edf", expert_rows, hidden_grad, preferred_element_type=F32)
    up_bias_grad = jnp.sum(hidden_grad.astype(F32), axis=1)
    down_bias_grad = jnp.sum(expert_grads.astype(F32), axis=1)

    no_bias = jnp.zeros((held, width), F32)
    back_sent = spread(back_parts, no_bias, capacity)
    back_sent, result_part = lax.optimization_barrier((back_sent, result_part))
    back_got = exchanged(back_sent)
    result_columns = [
        lax.dynamic_slice_in_dim(result_part, (tp_at + PARTS - s) % PARTS * width, width, 2) for s in range(PARTS)
    ]
    result_parts = swapped(result_columns, -1)
    bias_columns = lax.dynamic_slice_in_dim(down_bias, tp_at * width, width, 1).astype(F32)
    result_sent = spread([[p[e] for p in result_parts] for e in range(held)], bias_columns, capacity)
    back_got, w_down_grad, w_up_grad = lax.optimization_barrier((back_got, w_down_grad, w_up_grad))
    grad_columns = to_tokens(target, back_got.reshape(slots, width))
    result_got = exchanged(after(result_sent, grad_columns))
    grad_blocks = swapped(jnp.split(grad_columns, PARTS), -1)
    second_grad = in_order([grad_blocks[-s % PARTS] for s in range(PARTS)], tp_at, 1).astype(F32)

    middle_grad = cot_part + norm_backward(second_grad, normed_two, inverse_two, gain_rows[1])
    branch_low = middle_grad.astype(BF)
    grad_rows_t = dot(out_all, branch_low, 0, 1).astype(BF)
    grad_t = jnp.concatenate(swapped(jnp.split(grad_rows_t, PARTS), -1), axis=1)

    dq_far, dk_far, dv_far = attend_backward(False, at, q_t, grad_t, exact_t, lse, start, k_far, v_far)
    kv_back = lax.ppermute(
        jnp.concatenate([dk_far[rows - REACH :], dv_far[rows - REACH :]], axis=1), "ctx", [(1, 0)]
    )
    dq, dk, dv = attend_backward(True, at, q_t, grad_t, exact_t, lse, start, k_low, v_low, dq_far)

    block_rel = (middle_columns.astype(F32) + to_tokens(target, result_got.reshape(slots, width)).astype(F32)).astype(BF)
    block_columns = in_order(jnp.split(block_rel, PARTS), tp_at, 0)
    block_out = placed(at, copied(block_columns), 1, -1)

    kv_grad = jnp.concatenate([dk, dv], axis=1).astype(F32) + jnp.pad(kv_back, ((rows - REACH, 0), (0, 0))).astype(F32)
    stacked = jnp.concatenate([dq, kv_grad.astype(BF)], axis=1)
    stacked, block_out = lax.optimization_barrier((stacked, block_out))
    first_part = dot(stacked, qkv_full, 1, 1).astype(BF)
    first_blocks = swapped(
        [lax.dynamic_slice_in_dim(first_part, (tp_at + s) % PARTS * part, part) for s in range(PARTS)], 1
    )
    first_grad = sum(b.astype(F32) for b in first_blocks)
    qkv_grad = dot(first_low, after(stacked, first_part), 0, 0).astype(BF)
    qkv_shard = jnp.moveaxis(summed_on_arrival(qkv_grad, FC, groups).reshape(shard, 3, channels), 1, 0)

    out_grad = dot(branch_low, mixed, 0, 1).astype(BF)
    out_sum = summed_on_arrival(after(out_grad, result_got), FC, groups).astype(BF)
    out_blocks = swapped(jnp.split(out_sum, PARTS, axis=1), -1)
    out_shard = sum(b.astype(F32) for b in out_blocks).T

    normed_one, inverse_one = normalized(inputs_part)
    tokens_part = (middle_grad + norm_backward(first_grad, normed_one, inverse_one, gain_rows[0])).astype(BF)
    tokens_grad = placed(at, copied(tokens_part), 0, -1)

    sums = jnp.stack([
        jnp.sum(first_grad * normed_one, axis=0),
        jnp.sum(second_grad * normed_two, axis=0),
        jnp.sum(first_grad, axis=0),
        jnp.sum(second_grad, axis=0),
        jnp.sum(branch_low.astype(F32), axis=0),
    ])
    stacked_sum = jnp.sum(stacked.astype(F32), axis=0)
    bias_sum = jnp.stack([stacked_sum[:channels], stacked_sum[2 * channels :]])
    bias_tiles = bias_sum.reshape(2, heads, groups, -1).transpose(2, 0, 1, 3).reshape(groups, -1)
    sum_tiles = sums.reshape(-1, groups, shard).transpose(1, 0, 2).reshape(groups, -1)
    tail = jnp.concatenate([sum_tiles, bias_tiles], axis=1)
    tail = jnp.pad(tail, ((0, 0), (0, 256 - tail.shape[1]))).reshape(groups, 1, 256)
    tail = jnp.sum(exchanged(tail), axis=0)[0]
    bias_shard = tail[5 * shard : 5 * shard + qv_bias.size].reshape(qv_bias.shape)
    norm_shard = sum(copied(tail[: 5 * shard].reshape(5, shard)))
    return (block_out, tokens_grad, qkv_shard, out_shard, norm_shard[:2], norm_shard[2:], bias_shard,
            w_up_grad, up_bias_grad, w_down_grad, down_bias_grad)


def solution(mesh):
    devices = mesh.devices.reshape(2, 4, 2, mesh.shape["ctx"], mesh.shape["tp"])
    chips = Mesh(devices, ("y_hi", "z", "core", "ctx", "tp"))
    token, weight = P(FC, None), P(None, FC)
    experts = P(FC, None, "tp"), P(FC, "tp"), P(FC, "tp", None), P(FC, None)
    shared = P(None, FC, "tp"), P("tp", FC), weight, weight, P(None, "tp", FC)
    return jax.shard_map(
        on_device,
        mesh=chips,
        in_specs=(token, token, token, P(FC[:3]), token, *shared, *experts),
        out_specs=(token, token, *shared, *experts),
        check_vma=False,
    )
```

```python
import functools

import jax
import jax.numpy as jnp
from jax import lax
from jax.experimental import pallas as pl
from jax.experimental.pallas import tpu as pltpu
from jax.sharding import Mesh, PartitionSpec as P

HD = 64
EPSILON = 1e-05
NEGATIVE = -1e30
REACH = 800
SIDE = 256
FC = ("y_hi", "z", "core", "ctx")
HALO = 1024
PARTS = 4
VMEM = 40 * 2**20
BF = jnp.bfloat16
F32 = jnp.float32


def dot(a, b, ca, cb):
    return lax.dot_general(a, b, (((ca,), (cb,)), ((), ())), preferred_element_type=F32)


def by_head(cols, heads):
    row = lax.broadcasted_iota(jnp.int32, cols.shape, 0) // HD
    zero = jnp.zeros_like(cols)
    return jnp.concatenate([jnp.where(row == h, cols, zero) for h in range(heads)], axis=1)


def pair_mask(start_row, q_first, k_first):
    k_pos = lax.broadcasted_iota(jnp.int32, (SIDE, SIDE), 0) + k_first
    q_pos = lax.broadcasted_iota(jnp.int32, (SIDE, SIDE), 1) + q_first
    return (k_pos >= start_row) & (k_pos <= q_pos)


def normalized(values):
    centre = values - jnp.mean(values, axis=-1, keepdims=True)
    variance = jnp.mean(centre * centre, axis=-1, keepdims=True)
    inverse = lax.rsqrt(variance + EPSILON)
    return centre * inverse, inverse


def small_kernel(small_ref, move_ref, rows_ref, bias_ref, column_ref):
    small = small_ref[...]
    rows_ref[...] = small.astype(F32).T[:8, :]
    column = dot(move_ref[...], small, 0, 0)
    column_ref[...] = column
    bias_ref[...] = column.T[:8, :]


def small_rows(packed, move):
    model, wide = packed.shape
    return pl.pallas_call(
        small_kernel,
        out_shape=(
            jax.ShapeDtypeStruct((8, model), F32),
            jax.ShapeDtypeStruct((8, move.shape[1]), F32),
            jax.ShapeDtypeStruct((move.shape[1], 128), F32),
        ),
        grid=(1,),
        in_specs=[
            pl.BlockSpec((model, 128), lambda i: (0, wide // 128 - 1)),
            pl.BlockSpec(move.shape, lambda i: (0, 0)),
        ],
        out_specs=(
            pl.BlockSpec((8, model), lambda i: (0, 0)),
            pl.BlockSpec((8, move.shape[1]), lambda i: (0, 0)),
            pl.BlockSpec((move.shape[1], 128), lambda i: (0, 0)),
        ),
        compiler_params=pltpu.CompilerParams(vmem_limit_bytes=VMEM),
        cost_estimate=pl.CostEstimate(flops=200_000_000, bytes_accessed=1_500_000, transcendentals=0),
        name="small_rows",
    )(packed, move)


def first_kernel(own_ref, w_ref, rows_ref, bias_ref, column_ref, q_ref, kv_ref, low_ref):
    channels = q_ref.shape[0]
    low = (normalized(own_ref[...].astype(F32))[0] * rows_ref[0:1, :] + rows_ref[2:3, :]).astype(BF)
    low_ref[...] = low
    q_ref[...] = (dot(low, w_ref[:, :channels], 1, 0).T + column_ref[:channels, 5:6]).astype(BF)
    kv = dot(low, w_ref[:, channels : 3 * channels], 1, 0)
    kv_ref[:, :channels] = kv[:, :channels].astype(BF)
    kv_ref[:, channels:] = (kv[:, channels:] + bias_ref[5:6, channels:]).astype(BF)


def first_projection(tokens, weights, rows_small, bias, column, channels):
    rows, model = tokens.shape

    def whole(a):
        return pl.BlockSpec(a.shape, lambda i: (0,) * a.ndim)

    return pl.pallas_call(
        first_kernel,
        out_shape=(
            jax.ShapeDtypeStruct((channels, rows), BF),
            jax.ShapeDtypeStruct((rows, 2 * channels), BF),
            jax.ShapeDtypeStruct((rows, model), BF),
        ),
        grid=(rows // SIDE,),
        in_specs=[
            pl.BlockSpec((SIDE, model), lambda i: (i, 0)),
            whole(weights), whole(rows_small), whole(bias), whole(column),
        ],
        out_specs=(
            pl.BlockSpec((channels, SIDE), lambda i: (0, i)),
            pl.BlockSpec((SIDE, 2 * channels), lambda i: (i, 0)),
            pl.BlockSpec((SIDE, model), lambda i: (i, 0)),
        ),
        compiler_params=pltpu.CompilerParams(vmem_limit_bytes=VMEM),
        cost_estimate=pl.CostEstimate(flops=1_900_000_000, bytes_accessed=6_000_000, transcendentals=0),
        name="first_projection",
    )(tokens, weights, rows_small, bias, column)


def part_rows(at_ref, s, n):
    return pl.ds(pl.multiple_of(lax.rem(at_ref[PARTS] + PARTS - s, PARTS) * n, n), n)


def branch_kernel(at_ref, *refs):
    mixed = refs[:PARTS]
    w_ref, tokens_ref, rows_ref, middle_ref, normed_ref, inverse_ref, second_ref, low_ref, held = refs[PARTS:]
    middle = tokens_ref[...].astype(F32) + rows_ref[4:5, :]
    model = middle.shape[1]
    for s in range(PARTS):
        middle += dot(mixed[s][...].T, w_ref[part_rows(at_ref, s, model), :], 1, 1)
    middle_ref[...] = middle
    normed, inverse = normalized(middle)
    normed_ref[...] = normed
    inverse_ref[...] = inverse
    n = second_ref.shape[2]
    held[0] = (normed * rows_ref[1:2, :] + rows_ref[3:4, :]).astype(BF)
    held[1] = middle.astype(BF)
    for s in range(PARTS):
        window = pl.ds(pl.multiple_of(lax.rem(at_ref[PARTS] + s, PARTS) * n, n), n)
        second_ref[s] = held[0, :, window]
        low_ref[s] = held[1, :, window]


def second_norm(at, mixed, w, tokens_part, rows_small):
    part, model = tokens_part.shape
    vmem = pl.BlockSpec(memory_space=pltpu.VMEM)
    blocks = jax.ShapeDtypeStruct((PARTS, part, model // PARTS), BF)
    return pl.pallas_call(
        branch_kernel,
        out_shape=(
            jax.ShapeDtypeStruct((part, model), F32), jax.ShapeDtypeStruct((part, model), F32),
            jax.ShapeDtypeStruct((part, 1), F32), blocks, blocks,
        ),
        in_specs=[pl.BlockSpec(memory_space=pltpu.SMEM)] + [vmem] * (PARTS + 3),
        out_specs=(vmem,) * 5,
        scratch_shapes=[pltpu.VMEM((2, part, model), BF)],
        compiler_params=pltpu.CompilerParams(vmem_limit_bytes=VMEM),
        cost_estimate=pl.CostEstimate(flops=600_000_000, bytes_accessed=6_000_000, transcendentals=0),
        name="second_norm",
    )(at, *mixed, w, tokens_part, rows_small)


def norm_backward(grad_out, normed, inverse, gain_row):
    scaled = grad_out * gain_row
    inner = jnp.mean(scaled, axis=-1, keepdims=True)
    along = jnp.mean(scaled * normed, axis=-1, keepdims=True)
    return inverse * (scaled - inner - normed * along)


def first_grad_kernel(near_ref, back_ref, w_ref, stacked_ref, o_ref):
    rows, n = near_ref.shape
    wide = back_ref.shape[1]
    stacked_ref[...] = near_ref[...]
    lower = slice(rows - back_ref.shape[0], rows)
    kept = near_ref[lower, n - wide :].astype(F32) + back_ref[...].astype(F32)
    stacked_ref[lower, n - wide :] = kept.astype(BF)
    for i in range(PARTS):
        at = slice(i * rows // PARTS, (i + 1) * rows // PARTS)
        o_ref[at, :] = dot(stacked_ref[at, :], w_ref[:, :n], 1, 1).astype(BF)


def first_gradient(near, back, weights):
    vmem = pl.BlockSpec(memory_space=pltpu.VMEM)
    return pl.pallas_call(
        first_grad_kernel,
        out_shape=(
            jax.ShapeDtypeStruct(near.shape, BF), jax.ShapeDtypeStruct((near.shape[0], weights.shape[0]), BF),
        ),
        in_specs=[vmem] * 3,
        out_specs=(vmem,) * 2,
        compiler_params=pltpu.CompilerParams(vmem_limit_bytes=VMEM),
        cost_estimate=pl.CostEstimate(flops=1_600_000_000, bytes_accessed=9_000_000, transcendentals=0),
        name="first_gradient",
    )(near, back, weights)


def total(values):
    return jnp.sum(values, axis=0, keepdims=True)


def second_back_kernel(at_ref, *refs):
    grads = refs[:PARTS]
    w_ref, cot_ref, normed_ref, inverse_ref, rows_ref, middle_ref, low_ref, sums_ref, blocks_ref, held = refs[PARTS:]
    n = grads[0].shape[1]
    for s in range(PARTS):
        window = pl.ds(pl.multiple_of(lax.rem(at_ref[PARTS] + s, PARTS) * n, n), n)
        held[:, window] = grads[s][...]
    grad = held[...].astype(F32)
    normed = normed_ref[...]
    middle = cot_ref[...].astype(F32) + norm_backward(grad, normed, inverse_ref[...], rows_ref[1:2, :])
    middle_ref[...] = middle
    low = middle.astype(BF)
    low_ref[...] = low
    for s in range(PARTS):
        blocks_ref[s] = dot(low, w_ref[part_rows(at_ref, s, low.shape[1]), :], 1, 0).T.astype(BF)
    sums_ref[...] = jnp.zeros_like(sums_ref)
    sums_ref[0:1, :] = total(grad * normed)
    sums_ref[1:2, :] = total(grad)
    sums_ref[2:3, :] = total(low.astype(F32))


def second_norm_back(at, grads, w, cot_part, normed, inverse, rows_small):
    part, model = cot_part.shape
    vmem = pl.BlockSpec(memory_space=pltpu.VMEM)
    return pl.pallas_call(
        second_back_kernel,
        out_shape=(
            jax.ShapeDtypeStruct((part, model), F32), jax.ShapeDtypeStruct((part, model), BF),
            jax.ShapeDtypeStruct((8, model), F32), jax.ShapeDtypeStruct((PARTS, w.shape[1], part), BF),
        ),
        in_specs=[pl.BlockSpec(memory_space=pltpu.SMEM)] + [vmem] * (PARTS + 5),
        out_specs=(vmem,) * 4,
        scratch_shapes=[pltpu.VMEM((part, model), BF)],
        compiler_params=pltpu.CompilerParams(vmem_limit_bytes=VMEM),
        cost_estimate=pl.CostEstimate(flops=600_000_000, bytes_accessed=6_000_000, transcendentals=0),
        name="second_norm_back",
    )(at, *grads, w, cot_part, normed, inverse, rows_small)


def first_back_kernel(grad_ref, tokens_ref, middle_ref, rows_ref, o_ref, sums_ref):
    grad = grad_ref[...].astype(F32)
    normed, inverse = normalized(tokens_ref[...].astype(F32))
    o_ref[...] = (middle_ref[...] + norm_backward(grad, normed, inverse, rows_ref[0:1, :])).astype(BF)
    sums_ref[...] = jnp.zeros_like(sums_ref)
    sums_ref[0:1, :] = total(grad * normed)
    sums_ref[1:2, :] = total(grad)


def first_norm_back(grad, tokens_part, middle_grad, rows_small):
    vmem = pl.BlockSpec(memory_space=pltpu.VMEM)
    return pl.pallas_call(
        first_back_kernel,
        out_shape=(
            jax.ShapeDtypeStruct(tokens_part.shape, BF), jax.ShapeDtypeStruct((8, tokens_part.shape[1]), F32),
        ),
        in_specs=[vmem] * 4,
        out_specs=(vmem,) * 2,
        compiler_params=pltpu.CompilerParams(vmem_limit_bytes=VMEM),
        cost_estimate=pl.CostEstimate(flops=8_000_000, bytes_accessed=5_000_000, transcendentals=0),
        name="first_norm_back",
    )(grad, tokens_part, middle_grad, rows_small)


def forward_kernel(at_ref, q_ref, start_ref, k_near, v_near, k_far, v_far, o_ref, exact_ref, lse_ref, q_heads, acc):
    heads = q_ref.shape[0] // HD
    i = pl.program_id(0)
    halo = PARTS
    own = halo + i
    short = PARTS - k_far.shape[0] // SIDE
    q_heads[...] = by_head(q_ref[...] * jnp.asarray(HD**-0.5, BF), heads)
    acc[...] = jnp.zeros_like(acc)
    start_row = start_ref[...]

    def step(k_ref, v_ref, first, n, carry):
        peak, total = carry
        j = own - n
        rows = pl.ds(pl.multiple_of((j - first) * SIDE, SIDE), SIDE)
        scores = dot(k_ref[rows, :], q_heads[...], 1, 0)
        allowed = pair_mask(start_row, own * SIDE, j * SIDE)
        scores = jnp.where(jnp.concatenate([allowed] * heads, axis=1), scores, NEGATIVE)
        new_peak = jnp.maximum(peak, jnp.max(scores, axis=0, keepdims=True))
        fade = jnp.exp(peak - new_peak)
        weights = jnp.exp(scores - new_peak)
        total = total * fade + jnp.sum(weights, axis=0, keepdims=True)
        low = weights.astype(BF)
        v_t = v_ref[rows, :].T
        for h in range(heads):
            at, cols = slice(h * HD, (h + 1) * HD), slice(h * SIDE, (h + 1) * SIDE)
            acc[at, :] = acc[at, :] * fade[:, cols] + dot(v_t[at, :], low[:, cols], 1, 0)
        return new_peak, total

    width = heads * SIDE
    last = own - at_ref[i] + 1
    carry = jnp.full((1, width), NEGATIVE, F32), jnp.zeros((1, width), F32)
    carry = lax.fori_loop(0, jnp.minimum(last, i + 1), functools.partial(step, k_near, v_near, halo), carry)
    peak, total = lax.fori_loop(i + 1, last, functools.partial(step, k_far, v_far, short), carry)
    scale = 1.0 / total
    for h in range(heads):
        at, cols = slice(h * HD, (h + 1) * HD), slice(h * SIDE, (h + 1) * SIDE)
        exact = acc[at, :] * scale[:, cols]
        exact_ref[at, :] = exact
        o_ref[at, :] = exact.astype(BF)
    lse_ref[0] = peak + jnp.log(total)


def turned(i, at):
    return lax.rem(i + PARTS - at[PARTS], PARTS)


def attend_forward(at, q_t, start, kv, kv_far):
    channels, rows = q_t.shape
    blocks = rows // SIDE
    width = channels // HD * SIDE
    column = pl.BlockSpec((channels, SIDE), lambda i, f: (0, i))
    return pl.pallas_call(
        forward_kernel,
        out_shape=(
            jax.ShapeDtypeStruct((channels, rows), BF),
            jax.ShapeDtypeStruct((channels, rows), F32),
            jax.ShapeDtypeStruct((blocks, 1, width), F32),
        ),
        grid_spec=pltpu.PrefetchScalarGridSpec(
            num_scalar_prefetch=1,
            grid=(blocks,),
            in_specs=[column, pl.BlockSpec((1, SIDE), lambda i, f: (0, i))]
            + [pl.BlockSpec((a.shape[0], channels), lambda i, f, c=c: (0, c)) for a in (kv, kv_far) for c in range(2)],
            out_specs=(
                pl.BlockSpec((channels, SIDE), lambda i, f: (0, turned(i, f))),
                column,
                pl.BlockSpec((1, 1, width), lambda i, f: (i, 0, 0)),
            ),
            scratch_shapes=[pltpu.VMEM((channels, width), BF), pltpu.VMEM((channels, SIDE), F32)],
        ),
        compiler_params=pltpu.CompilerParams(vmem_limit_bytes=VMEM),
        cost_estimate=pl.CostEstimate(flops=6_000_000_000, bytes_accessed=6_000_000, transcendentals=4_000_000),
        name="attend_forward",
    )(at, q_t, start, kv, kv, kv_far, kv_far)


def backward_kernel(low_block, at_ref, q_ref, g0, g1, g2, g3, exact_ref, lse_ref, start_ref, k_ref, v_ref, add_ref,
                    dq_ref, dkv_ref, q_heads, g_heads, dq_acc, dk_acc, dv_acc):
    heads = q_ref.shape[0] // HD
    i = pl.program_id(0)
    blocks = pl.num_programs(0)
    halo = PARTS
    own = halo + i
    q_heads[...] = by_head(q_ref[...] * jnp.asarray(HD**-0.5, BF), heads)
    place = turned(i, at_ref)
    grad = g0[...]
    for s, other in enumerate((g1, g2, g3)):
        grad = jnp.where(place == s + 1, other[...], grad)
    g_heads[...] = by_head(grad, heads)
    product = grad.astype(F32) * exact_ref[...]
    delta = jnp.concatenate(
        [jnp.sum(product[h * HD : (h + 1) * HD, :], axis=0, keepdims=True) for h in range(heads)], axis=1
    )
    dq_acc[...] = jnp.zeros_like(dq_acc)

    @pl.when(i == 0)
    def _():
        dk_acc[...] = jnp.zeros_like(dk_acc)
        dv_acc[...] = jnp.zeros_like(dv_acc)

    start_row = start_ref[...]
    lse = lse_ref[0]

    def step(j, carry):
        rows = pl.ds(pl.multiple_of((j - low_block) * SIDE, SIDE), SIDE)
        k_block = k_ref[rows, :]
        scores = dot(k_block, q_heads[...], 1, 0)
        allowed = pair_mask(start_row, own * SIDE, j * SIDE)
        scores = jnp.where(jnp.concatenate([allowed] * heads, axis=1), scores, NEGATIVE)
        weights = jnp.exp(scores - lse)
        grad_weights = dot(v_ref[rows, :], g_heads[...], 1, 0)
        grad_scores = (weights * (grad_weights - delta)).astype(BF)
        dv_acc[rows, :] += dot(weights.astype(BF), g_heads[...], 1, 1)
        dk_acc[rows, :] += dot(grad_scores, q_heads[...], 1, 1)
        k_t = k_block.T
        for h in range(heads):
            at, cols = slice(h * HD, (h + 1) * HD), slice(h * SIDE, (h + 1) * SIDE)
            dq_acc[at, :] += dot(k_t[at, :], grad_scores[:, cols], 1, 0)
        return carry

    first = at_ref[i]
    if low_block:
        lax.fori_loop(jnp.maximum(first, low_block), own + 1, step, 0)
        n = q_ref.shape[0]
        at = pl.ds(pl.multiple_of(i * SIDE, SIDE), SIDE)
        dkv_ref[at, :n] = (dq_acc[...] * HD**-0.5 + add_ref[...]).T.astype(BF)
    else:
        lax.fori_loop(first, halo, step, 0)
        dq_ref[...] = dq_acc[...] * HD**-0.5

    @pl.when(i == blocks - 1)
    def _():
        n = q_ref.shape[0]
        first_column = dkv_ref.shape[1] - 2 * n
        dkv_ref[:, first_column : first_column + n] = dk_acc[...].astype(BF)
        dkv_ref[:, first_column + n :] = dv_acc[...].astype(BF)


def far_kernel(at_ref, q_ref, g0, g1, g2, g3, exact_ref, lse_ref, start_ref, k_ref, v_ref, *rest):
    backward_kernel(0, at_ref, q_ref, g0, g1, g2, g3, exact_ref, lse_ref, start_ref, k_ref, v_ref, None, *rest)


def near_kernel(at_ref, q_ref, g0, g1, g2, g3, exact_ref, lse_ref, start_ref, k_ref, v_ref, add_ref, *rest):
    backward_kernel(PARTS, at_ref, q_ref, g0, g1, g2, g3, exact_ref, lse_ref, start_ref, k_ref, v_ref, add_ref,
                    None, *rest)


def attend_backward(near, at, q_t, grads, exact_t, lse, start, kv, add=None):
    channels, rows = q_t.shape
    blocks = rows // SIDE
    width = channels // HD * SIDE
    column = pl.BlockSpec((channels, SIDE), lambda i, f: (0, i))
    block = pl.BlockSpec((channels, SIDE), lambda i, f: (0, 0))
    in_specs = [
        column,
        *[block] * PARTS,
        column,
        pl.BlockSpec((1, 1, width), lambda i, f: (i, 0, 0)),
        pl.BlockSpec((1, SIDE), lambda i, f: (0, i)),
    ] + [pl.BlockSpec((kv.shape[0], channels), lambda i, f, c=c: (0, c)) for c in range(2)]
    args = [at, q_t, *grads, exact_t, lse, start, kv, kv]
    if near:
        in_specs.append(column)
        args.append(add)
        out_shape = (jax.ShapeDtypeStruct((rows, 3 * channels), BF),)
        out_specs = (pl.BlockSpec((rows, 3 * channels), lambda i, f: (0, 0)),)
    else:
        out_shape = jax.ShapeDtypeStruct((channels, rows), F32), jax.ShapeDtypeStruct(kv.shape, BF)
        out_specs = column, pl.BlockSpec(kv.shape, lambda i, f: (0, 0))
    return pl.pallas_call(
        near_kernel if near else far_kernel,
        out_shape=out_shape,
        grid_spec=pltpu.PrefetchScalarGridSpec(
            num_scalar_prefetch=1,
            grid=(blocks,),
            in_specs=in_specs,
            out_specs=out_specs,
            scratch_shapes=[
                pltpu.VMEM((channels, width), BF),
                pltpu.VMEM((channels, width), BF),
                pltpu.VMEM((channels, SIDE), F32),
                pltpu.VMEM((kv.shape[0], channels), F32),
                pltpu.VMEM((kv.shape[0], channels), F32),
            ],
        ),
        compiler_params=pltpu.CompilerParams(vmem_limit_bytes=VMEM),
        cost_estimate=pl.CostEstimate(flops=9_000_000_000, bytes_accessed=6_000_000, transcendentals=4_000_000),
        name="attend_near" if near else "attend_far",
    )(*args)


def slots_kernel(target_ref, x_ref, o_ref):
    place = lax.broadcasted_iota(jnp.int32, (o_ref.shape[0], x_ref.shape[0]), 0) + pl.program_id(0) * o_ref.shape[0]
    o_ref[...] = dot((place == target_ref[...]).astype(F32).astype(BF), x_ref[...], 1, 0).astype(BF)


def to_slots(target, x, slots):
    return pl.pallas_call(
        slots_kernel,
        out_shape=jax.ShapeDtypeStruct((slots, x.shape[1]), BF),
        grid=(slots // SIDE,),
        in_specs=[pl.BlockSpec((1, x.shape[0]), lambda i: (0, 0)), pl.BlockSpec(x.shape, lambda i: (0, 0))],
        out_specs=pl.BlockSpec((SIDE, x.shape[1]), lambda i: (i, 0)),
        compiler_params=pltpu.CompilerParams(vmem_limit_bytes=VMEM),
        cost_estimate=pl.CostEstimate(flops=1_200_000_000, bytes_accessed=2_000_000, transcendentals=0),
        name="to_slots",
    )(target[None, :], x)


def tokens_kernel(target_ref, x_ref, o_ref):
    place = lax.broadcasted_iota(jnp.int32, (o_ref.shape[0], x_ref.shape[0]), 1)
    o_ref[...] = dot((place == target_ref[...]).astype(F32).astype(BF), x_ref[...], 1, 0).astype(BF)


def to_tokens(target, x):
    rows = target.shape[0]
    return pl.pallas_call(
        tokens_kernel,
        out_shape=jax.ShapeDtypeStruct((rows, x.shape[1]), BF),
        grid=(rows // SIDE,),
        in_specs=[pl.BlockSpec((SIDE, 1), lambda i: (i, 0)), pl.BlockSpec(x.shape, lambda i: (0, 0))],
        out_specs=pl.BlockSpec((SIDE, x.shape[1]), lambda i: (i, 0)),
        compiler_params=pltpu.CompilerParams(vmem_limit_bytes=VMEM),
        cost_estimate=pl.CostEstimate(flops=1_200_000_000, bytes_accessed=2_000_000, transcendentals=0),
        name="to_tokens",
    )(target[:, None], x)


def join_kernel(got_ref, *refs):
    outs, held = refs[:-1], refs[-1]
    capacity = got_ref.shape[1] // len(outs)
    for f in range(got_ref.shape[0] // 2):
        both = got_ref[2 * f].astype(F32) + got_ref[2 * f + 1].astype(F32)
        for e in range(len(outs)):
            held[e, f * capacity : (f + 1) * capacity, :] = both[e * capacity : (e + 1) * capacity, :]
    for e, out in enumerate(outs):
        out[...] = held[e].astype(BF)


def join(got, experts):
    shape = (got.shape[0] // 2 * (got.shape[1] // experts), got.shape[2])
    return pl.pallas_call(
        join_kernel,
        out_shape=(jax.ShapeDtypeStruct(shape, BF),) * experts,
        scratch_shapes=[pltpu.VMEM((experts, *shape), F32)],
        compiler_params=pltpu.CompilerParams(vmem_limit_bytes=VMEM),
        cost_estimate=pl.CostEstimate(flops=600_000, bytes_accessed=2_000_000, transcendentals=0),
        name="join",
    )(got)


def spread_kernel(bias_ref, *refs):
    parts, (o_ref, held, piece) = refs[:-3], refs[-3:]
    experts, rows = held.shape[:2]
    capacity = o_ref.shape[1] // experts
    for e in range(experts):
        if len(parts) == 1:
            total = parts[0][e * rows : (e + 1) * rows, :].astype(F32)
        else:
            total = sum(part[...].astype(F32) for part in parts[e * PARTS : (e + 1) * PARTS])
        held[e] = total + bias_ref[e : e + 1, :]
    for f in range(o_ref.shape[0] // 2):
        for e in range(experts):
            piece[e * capacity : (e + 1) * capacity, :] = held[e, f * capacity : (f + 1) * capacity, :]
        low = piece[...].astype(BF)
        o_ref[2 * f] = low
        o_ref[2 * f + 1] = low


def spread(parts, bias, capacity):
    experts, n = bias.shape
    rows = parts[0].shape[0] // (experts if len(parts) == 1 else 1)
    return pl.pallas_call(
        spread_kernel,
        out_shape=jax.ShapeDtypeStruct((rows // capacity * 2, experts * capacity, n), BF),
        scratch_shapes=[pltpu.VMEM((experts, rows, n), F32), pltpu.VMEM((experts * capacity, n), F32)],
        compiler_params=pltpu.CompilerParams(vmem_limit_bytes=VMEM),
        cost_estimate=pl.CostEstimate(flops=2_400_000, bytes_accessed=4_000_000, transcendentals=0),
        name="spread",
    )(bias, *parts)


def expert_kernel(at_ref, r0, r1, r2, r3, w_ref, b_ref, g_ref, act_ref, hg_ref, rows_ref, *outs):
    parts = (r0, r1, r2, r3)
    n = r0.shape[1]
    windows = [
        pl.ds(pl.multiple_of(lax.rem(at_ref[PARTS] + PARTS - s, PARTS) * n, n), n) for s in range(PARTS)
    ]
    for s in range(PARTS):
        rows_ref[:, windows[s]] = parts[s][...]
    inner = w_ref.shape[2]
    for j in range(2):
        cols = slice(j * inner // 2, (j + 1) * inner // 2)
        hidden = dot(rows_ref[...], w_ref[0, :, cols], 1, 0) + b_ref[0, :, cols].astype(F32)
        gate = jax.nn.sigmoid(hidden)
        act_ref[:, cols] = (hidden * gate).astype(BF)
        hg_ref[:, cols] = (g_ref[:, cols] * (gate * (1.0 + hidden * (1.0 - gate)))).astype(BF)
    for s in range(PARTS):
        outs[s][...] = dot(hg_ref[...], w_ref[0, windows[s], :], 1, 1).astype(BF)


def run_expert(e, at, parts, w_up, up_bias, active_grad):
    rows, n = parts[0].shape
    model, inner = w_up.shape[1:]
    whole = pl.BlockSpec((rows, n), lambda j, f: (0, 0))
    full = pl.BlockSpec((rows, inner), lambda j, f: (0, 0))
    return pl.pallas_call(
        expert_kernel,
        out_shape=(
            jax.ShapeDtypeStruct((rows, inner), BF),
            jax.ShapeDtypeStruct((rows, inner), BF),
            jax.ShapeDtypeStruct((rows, model), BF),
            *[jax.ShapeDtypeStruct((rows, n), BF)] * PARTS,
        ),
        grid_spec=pltpu.PrefetchScalarGridSpec(
            num_scalar_prefetch=1,
            grid=(1,),
            in_specs=[whole] * PARTS + [
                pl.BlockSpec((1, model, inner), lambda j, f: (e, 0, 0)),
                pl.BlockSpec((1, 1, inner), lambda j, f: (e, 0, 0)),
                full,
            ],
            out_specs=(
                full, full,
                pl.BlockSpec((rows, model), lambda j, f: (0, 0)),
                *[whole] * PARTS,
            ),
        ),
        compiler_params=pltpu.CompilerParams(vmem_limit_bytes=VMEM),
        cost_estimate=pl.CostEstimate(flops=2_400_000_000, bytes_accessed=8_000_000, transcendentals=600_000),
        name="expert",
    )(at, *parts, w_up, up_bias[:, None, :], active_grad)


def result_kernel(a_ref, w_ref, o_ref):
    n = o_ref.shape[2]
    for t in range(o_ref.shape[0]):
        o_ref[t] = dot(a_ref[0], w_ref[0, :, t * n : (t + 1) * n], 1, 0).astype(BF)


def expert_results(active, w_down):
    held, rows, inner = active.shape
    model = w_down.shape[2]
    n = model // PARTS
    return pl.pallas_call(
        result_kernel,
        out_shape=jax.ShapeDtypeStruct((PARTS, held * rows, n), BF),
        grid=(held,),
        in_specs=[
            pl.BlockSpec((1, rows, inner), lambda e: (e, 0, 0)),
            pl.BlockSpec((1, inner, model), lambda e: (e, 0, 0)),
        ],
        out_specs=pl.BlockSpec((PARTS, rows, n), lambda e: (0, e, 0)),
        compiler_params=pltpu.CompilerParams(vmem_limit_bytes=VMEM),
        cost_estimate=pl.CostEstimate(flops=2_400_000_000, bytes_accessed=9_000_000, transcendentals=0),
        name="results",
    )(active, w_down)


def copy_kernel(x_ref, o_ref):
    o_ref[...] = x_ref[...]


def side_by_side(x):
    rows, n = x.shape[0] // PARTS, x.shape[1]
    return pl.pallas_call(
        copy_kernel,
        out_shape=jax.ShapeDtypeStruct((rows, PARTS * n), x.dtype),
        grid=(PARTS,),
        in_specs=[pl.BlockSpec((rows, n), lambda t: (t, 0))],
        out_specs=pl.BlockSpec((rows, n), lambda t: (0, t)),
        compiler_params=pltpu.CompilerParams(vmem_limit_bytes=VMEM),
        cost_estimate=pl.CostEstimate(flops=0, bytes_accessed=4_000_000, transcendentals=0),
        name="side_by_side",
    )(x)


def weight_kernel(x_ref, grads_ref, branch_ref, mixed_ref, o_ref):
    n = grads_ref.shape[1]
    o_ref[:, :n] = dot(x_ref[...].T, grads_ref[...], 1, 0).astype(BF)
    o_ref[:, n:] = dot(branch_ref[...].T, mixed_ref[...], 1, 1).astype(BF)


def weight_gradients(x, grads, branch, mixed):
    rows, model = x.shape
    n, channels = grads.shape[1], mixed.shape[0]
    block = pl.BlockSpec((rows, SIDE), lambda i: (0, i))
    return pl.pallas_call(
        weight_kernel,
        out_shape=jax.ShapeDtypeStruct((model, n + channels), BF),
        grid=(model // SIDE,),
        in_specs=[
            block, pl.BlockSpec((rows, n), lambda i: (0, 0)), block, pl.BlockSpec((channels, rows), lambda i: (0, 0)),
        ],
        out_specs=pl.BlockSpec((SIDE, n + channels), lambda i: (i, 0)),
        compiler_params=pltpu.CompilerParams(vmem_limit_bytes=VMEM),
        cost_estimate=pl.CostEstimate(flops=2_200_000_000, bytes_accessed=8_000_000, transcendentals=0),
        name="weight_gradients",
    )(x, grads, branch, mixed)


def after(value, *others):
    return lax.optimization_barrier((value, *others))[0]


def hops(axis, s):
    n = lax.axis_size(axis)
    return [(i, (i + s) % n) for i in range(n)]


def swapped(blocks, sign):
    return [blocks[0]] + [lax.ppermute(blocks[s], "tp", hops("tp", sign * s)) for s in range(1, PARTS)]


def copied(block):
    return swapped([block] * PARTS, 1)


def in_order(parts, start, axis):
    turned_parts = [parts[-k % PARTS] for k in range(PARTS)]
    size = parts[0].shape[axis]
    both = jnp.concatenate(turned_parts + turned_parts[:-1], axis=axis)
    return lax.dynamic_slice_in_dim(both, (PARTS - start) % PARTS * size, PARTS * size, axis)


def on_device(tokens, cotangent, expert_ids, segment_ids, priority, w_qkv, w_out, norm_gains, norm_shifts,
              qv_bias, w_up, up_bias, w_down, down_bias):
    rows, model = tokens.shape
    channels = w_qkv.shape[2]
    heads = channels // HD
    seq_len = segment_ids.shape[0]
    f_count, c_count = lax.axis_size(FC[:3]), lax.axis_size("ctx")
    groups = f_count * c_count
    ctx_at, tp_at = lax.axis_index("ctx"), lax.axis_index("tp")
    held = w_up.shape[0]
    experts = held * groups
    capacity = (9 * seq_len + 8 * experts - 1) // (8 * experts)
    slots = experts * capacity
    shard = model // groups
    part = rows // PARTS
    width = model // PARTS
    bias_size = qv_bias.size

    bias_column = jnp.pad(qv_bias.reshape(-1), (0, shard - bias_size))[None]
    small = jnp.concatenate([norm_gains, norm_shifts, bias_column], axis=0).T
    small = jnp.pad(small, ((0, 0), (0, 128 - small.shape[1])))
    pack = jnp.concatenate([jnp.moveaxis(w_qkv, 0, 1).reshape(shard, 3 * channels), w_out.T, small], axis=1)
    packed = lax.all_to_all(jnp.broadcast_to(pack[None], (groups, *pack.shape)), FC, 0, 0, tiled=True)
    packed = packed.reshape(model, -1)
    lane = lax.broadcasted_iota(jnp.int32, (model, 2 * channels), 1)
    line = lax.broadcasted_iota(jnp.int32, (model, 2 * channels), 0)
    inside, group = line % shard, line // shard
    ends = qv_bias.shape[2]
    goal = (inside // (heads * ends) * channels + inside // ends % heads * HD + group * ends + inside % ends)
    move = ((goal == lane) & (inside < bias_size)).astype(BF)
    owner = expert_ids[:, 0]
    rank = priority[0]
    earlier_ids = lax.ppermute(expert_ids + 1, "ctx", [(0, 1)])[:, 0]
    before = (owner[None, :] == owner[:, None]) & (rank[None, :] < rank[:, None])
    carried = earlier_ids[None, :] == owner[:, None] + 1
    slot = jnp.sum(before.astype(jnp.int32), axis=1) + jnp.sum(carried.astype(jnp.int32), axis=1)
    target = jnp.where(slot < capacity, owner * capacity + slot, slots)
    places = [(tp_at + PARTS - s) % PARTS for s in range(PARTS)]
    target = jnp.concatenate([lax.dynamic_slice_in_dim(target, p * part, part) for p in places])

    def exchanged(sent):
        return lax.all_to_all(sent, FC, 0, 0, tiled=True)

    def sent_rows(columns):
        return to_slots(target, columns, slots).reshape(groups, held * capacity, width)

    cot_columns = [lax.dynamic_slice(cotangent, (p * part, tp_at * width), (part, width)) for p in places]
    cot_sent = sent_rows(jnp.concatenate(cot_columns))

    seg_own = lax.dynamic_slice_in_dim(segment_ids, ctx_at * rows, rows)
    start = jnp.sum((segment_ids[None, :] < seg_own[:, None]).astype(jnp.int32), axis=1)
    start = start + jnp.where(ctx_at == 0, rows, 0)
    at = jnp.concatenate([start[::SIDE] // SIDE, tp_at[None]]).astype(jnp.int32)
    start = start[None, :]
    packed, start, at, move = lax.optimization_barrier((packed, start, at, move))
    rows_small, bias_row, bias_col = small_rows(packed, move)
    q_t, kv, first_low = first_projection(tokens, packed, rows_small, bias_row, bias_col, channels)
    kv_far = lax.ppermute(kv[rows - HALO :], "ctx", [(0, 1)])
    out_all = lax.all_gather(packed[:, 3 * channels : 4 * channels], "tp", axis=0, tiled=True)
    cot_got = exchanged(after(cot_sent, kv))
    mixed_t, exact_t, lse = attend_forward(at, q_t, start, kv, kv_far)
    mixed = swapped(jnp.split(mixed_t, PARTS, axis=1), 1)

    tokens_part = lax.dynamic_slice_in_dim(tokens, tp_at * part, part)
    cot_part = lax.dynamic_slice_in_dim(cotangent, tp_at * part, part)
    middle, normed_two, inverse_two, second_blocks, middle_blocks = second_norm(
        at, mixed, out_all, tokens_part, rows_small
    )
    second_sent = sent_rows(jnp.concatenate(swapped(list(second_blocks), 1)))

    cot_mine = jnp.concatenate(join(cot_got, held))
    middle_blocks, second_sent, cot_mine = lax.optimization_barrier((middle_blocks, second_sent, cot_mine))
    second_got = exchanged(second_sent)
    cot_all = lax.all_gather(cot_mine, "tp", axis=0, tiled=True)
    middle_columns = jnp.concatenate(swapped(list(middle_blocks), 1))
    mine = join(second_got, held)
    cot_all = after(cot_all, mine[0])
    parts = [copied(m) for m in mine]
    expert_grads = side_by_side(cot_all).reshape(held, -1, model)
    active_grad = jnp.einsum("emd,efd->emf", expert_grads, w_down, preferred_element_type=F32)
    done = [run_expert(e, at, parts[e], w_up, up_bias, active_grad[e]) for e in range(held)]
    back_parts = [p for d in done for p in swapped(d[3:], -1)]
    active_low = jnp.stack([d[0] for d in done])
    results = expert_results(active_low, w_down)
    back_sent = spread(back_parts, jnp.zeros((held, width), F32), capacity)
    back_sent, results = lax.optimization_barrier((back_sent, results))
    back_got = exchanged(back_sent)
    result_sum = lax.psum_scatter(results, "tp", scatter_dimension=0, tiled=True)
    active_late, grads_late = lax.optimization_barrier((active_low, expert_grads, back_sent))[:2]
    w_down_grad = jnp.einsum("emf,emd->efd", active_late, grads_late, preferred_element_type=F32)
    back_got, w_down_grad = lax.optimization_barrier((back_got, w_down_grad))
    grad_columns = to_tokens(target, back_got.reshape(slots, width))
    grad_blocks = swapped(jnp.split(grad_columns, PARTS), -1)
    grad_blocks[0], result_sum = lax.optimization_barrier((grad_blocks[0], result_sum))

    middle_grad, branch_low, second_sums, mixed_grads = second_norm_back(
        at, grad_blocks, out_all, cot_part, normed_two, inverse_two, rows_small
    )
    grads_t = swapped(list(mixed_grads), -1)
    branch_all = lax.all_gather(after(branch_low, grads_t[1]), "tp", axis=0, tiled=True)

    dq_far, dkv_far = attend_backward(False, at, q_t, grads_t, exact_t, lse, start, kv_far)
    kv_back = lax.ppermute(dkv_far[HALO - REACH :], "ctx", [(1, 0)])
    (near_grad,) = attend_backward(True, at, q_t, grads_t, exact_t, lse, start, kv, dq_far)
    stacked, first_part = first_gradient(near_grad, kv_back, packed)
    first_grad = lax.psum_scatter(first_part, "tp", scatter_dimension=0, tiled=True)

    result_sum, branch_all, first_part = lax.optimization_barrier((result_sum, branch_all, first_part))
    bias_columns = lax.dynamic_slice_in_dim(down_bias, tp_at * width, width, 1).astype(F32)
    result_got = exchanged(spread([result_sum.reshape(-1, width)], bias_columns, capacity))
    weight_tiles = weight_gradients(first_low, stacked, branch_all, exact_t.astype(BF))
    expert_rows = after(jnp.stack([d[2] for d in done]), first_part)
    hidden_grad = jnp.stack([d[1] for d in done])
    w_up_grad = jnp.einsum("emd,emf->edf", expert_rows, hidden_grad, preferred_element_type=F32)
    stacked_sum = jnp.sum(stacked.astype(F32), axis=0)
    first_grad, result_got, w_up_grad, weight_tiles, stacked_sum = lax.optimization_barrier(
        (first_grad, result_got, w_up_grad, weight_tiles, stacked_sum)
    )

    tokens_grad_part, first_sums = first_norm_back(first_grad, tokens_part, middle_grad, rows_small)
    tokens_grad = lax.all_gather(tokens_grad_part, "tp", axis=0, tiled=True)
    result_got = after(result_got, tokens_grad_part)
    block_rel = middle_columns.astype(F32) + to_tokens(target, result_got.reshape(slots, width)).astype(F32)
    block_columns = in_order(jnp.split(block_rel.astype(BF), PARTS), tp_at, 0)
    block_out = side_by_side(lax.all_gather(block_columns, "tp", axis=0, tiled=True))
    hidden_late, cot_late = lax.optimization_barrier((hidden_grad, expert_grads, tokens_grad_part))[:2]
    up_bias_grad = jnp.sum(hidden_late.astype(F32), axis=1)
    down_bias_grad = jnp.sum(cot_late.astype(F32), axis=1)
    sums = jnp.stack([first_sums[0], second_sums[0], first_sums[1], second_sums[1], second_sums[2]])
    bias_sum = jnp.stack([stacked_sum[:channels], stacked_sum[2 * channels :]])
    bias_tiles = bias_sum.reshape(2, heads, groups, -1).transpose(2, 0, 1, 3).reshape(groups, -1)
    sum_tiles = sums.reshape(-1, groups, shard).transpose(1, 0, 2).reshape(groups, -1)
    tail = jnp.concatenate([sum_tiles, bias_tiles], axis=1)
    tail = jnp.pad(tail, ((0, 0), (0, model - tail.shape[1])))[:, None, :].astype(BF)
    tail = jnp.pad(tail, ((0, 0), (0, 15), (0, 0)))
    sent = jnp.concatenate([weight_tiles.reshape(groups, shard, model), tail], axis=1)
    got = exchanged(sent).astype(F32).sum(axis=0)
    qkv_shard = jnp.moveaxis(got[:shard, : 3 * channels].reshape(shard, 3, channels), 1, 0)
    out_shard = got[:shard, 3 * channels :].T
    tail = got[shard]
    bias_shard = tail[5 * shard : 5 * shard + bias_size].reshape(qv_bias.shape)
    norm_shard = sum(copied(tail[: 5 * shard].reshape(5, shard)))
    return (block_out, tokens_grad, qkv_shard, out_shard, norm_shard[:2], norm_shard[2:], bias_shard,
            w_up_grad, up_bias_grad, w_down_grad, down_bias_grad)


def solution(mesh):
    devices = mesh.devices.reshape(2, 4, 2, mesh.shape["ctx"], mesh.shape["tp"])
    chips = Mesh(devices, ("y_hi", "z", "core", "ctx", "tp"))
    token, weight = P(FC, None), P(None, FC)
    experts = P(FC, None, "tp"), P(FC, "tp"), P(FC, "tp", None), P(FC, None)
    shared = P(None, FC, "tp"), P("tp", FC), weight, weight, P(None, "tp", FC)
    return jax.shard_map(
        on_device,
        mesh=chips,
        in_specs=(token, token, token, P(FC[:3]), token, *shared, *experts),
        out_specs=(token, token, *shared, *experts),
        check_vma=False,
    )
```

```python
import functools

import jax
import jax.numpy as jnp
from jax import lax
from jax.experimental import pallas as pl
from jax.experimental.pallas import tpu as pltpu
from jax.sharding import Mesh, PartitionSpec as P

HD = 64
EPSILON = 1e-05
NEGATIVE = -1e30
REACH = 800
SIDE = 256
FC = ("y_hi", "z", "core", "ctx")
HALO = 896
FAR = 128
PARTS = 4
VMEM = 40 * 2**20
BF = jnp.bfloat16
F32 = jnp.float32


def dot(a, b, ca, cb):
    return lax.dot_general(a, b, (((ca,), (cb,)), ((), ())), preferred_element_type=F32)


def by_head(cols, heads):
    row = lax.broadcasted_iota(jnp.int32, cols.shape, 0) // HD
    zero = jnp.zeros_like(cols)
    return jnp.concatenate([jnp.where(row == h, cols, zero) for h in range(heads)], axis=1)


def pair_mask(start_row, q_first, k_first, size):
    k_pos = lax.broadcasted_iota(jnp.int32, (size, SIDE), 0) + k_first
    q_pos = lax.broadcasted_iota(jnp.int32, (size, SIDE), 1) + q_first
    return (k_pos >= start_row) & (k_pos <= q_pos)


def normalized(values):
    centre = values - jnp.mean(values, axis=-1, keepdims=True)
    variance = jnp.mean(centre * centre, axis=-1, keepdims=True)
    inverse = lax.rsqrt(variance + EPSILON)
    return centre * inverse, inverse


def small_kernel(small_ref, move_ref, rows_ref, bias_ref, column_ref):
    small = small_ref[...]
    rows_ref[...] = small.astype(F32).T[:8, :]
    column = dot(move_ref[...], small, 0, 0)
    column_ref[...] = column
    bias_ref[...] = column.T[:8, :]


def small_rows(packed, move):
    model, wide = packed.shape
    return pl.pallas_call(
        small_kernel,
        out_shape=(
            jax.ShapeDtypeStruct((8, model), F32),
            jax.ShapeDtypeStruct((8, move.shape[1]), F32),
            jax.ShapeDtypeStruct((move.shape[1], 128), F32),
        ),
        grid=(1,),
        in_specs=[
            pl.BlockSpec((model, 128), lambda i: (0, wide // 128 - 1)),
            pl.BlockSpec(move.shape, lambda i: (0, 0)),
        ],
        out_specs=(
            pl.BlockSpec((8, model), lambda i: (0, 0)),
            pl.BlockSpec((8, move.shape[1]), lambda i: (0, 0)),
            pl.BlockSpec((move.shape[1], 128), lambda i: (0, 0)),
        ),
        compiler_params=pltpu.CompilerParams(vmem_limit_bytes=VMEM),
        cost_estimate=pl.CostEstimate(flops=200_000_000, bytes_accessed=1_500_000, transcendentals=0),
        name="small_rows",
    )(packed, move)


def first_kernel(own_ref, w_ref, rows_ref, bias_ref, column_ref, q_ref, kv_ref, low_ref, halo_ref):
    channels = q_ref.shape[0]
    low = (normalized(own_ref[...].astype(F32))[0] * rows_ref[0:1, :] + rows_ref[2:3, :]).astype(BF)
    low_ref[...] = low
    q_ref[...] = (dot(low, w_ref[:, :channels], 1, 0).T + column_ref[:channels, 5:6]).astype(BF)
    kv = dot(low, w_ref[:, channels : 3 * channels], 1, 0)
    kv_ref[:, :channels] = kv[:, :channels].astype(BF)
    kv_ref[:, channels:] = (kv[:, channels:] + bias_ref[5:6, channels:]).astype(BF)
    i = pl.program_id(0)
    skipped = PARTS * SIDE - HALO

    @pl.when(i == 0)
    def _():
        halo_ref[: SIDE - skipped, :] = kv_ref[skipped:, :]

    @pl.when(i > 0)
    def _():
        halo_ref[pl.ds(pl.multiple_of(i * SIDE - skipped, FAR), SIDE), :] = kv_ref[...]


def first_projection(tokens, weights, rows_small, bias, column, channels):
    rows, model = tokens.shape

    def whole(a):
        return pl.BlockSpec(a.shape, lambda i: (0,) * a.ndim)

    return pl.pallas_call(
        first_kernel,
        out_shape=(
            jax.ShapeDtypeStruct((channels, rows), BF),
            jax.ShapeDtypeStruct((rows, 2 * channels), BF),
            jax.ShapeDtypeStruct((rows, model), BF),
            jax.ShapeDtypeStruct((HALO, 2 * channels), BF),
        ),
        grid=(rows // SIDE,),
        in_specs=[
            pl.BlockSpec((SIDE, model), lambda i: (i, 0)),
            whole(weights), whole(rows_small), whole(bias), whole(column),
        ],
        out_specs=(
            pl.BlockSpec((channels, SIDE), lambda i: (0, i)),
            pl.BlockSpec((SIDE, 2 * channels), lambda i: (i, 0)),
            pl.BlockSpec((SIDE, model), lambda i: (i, 0)),
            pl.BlockSpec((HALO, 2 * channels), lambda i: (0, 0)),
        ),
        compiler_params=pltpu.CompilerParams(vmem_limit_bytes=VMEM),
        cost_estimate=pl.CostEstimate(flops=1_900_000_000, bytes_accessed=6_000_000, transcendentals=0),
        name="first_projection",
    )(tokens, weights, rows_small, bias, column)


def part_rows(at_ref, s, n):
    return pl.ds(pl.multiple_of(lax.rem(at_ref[PARTS] + PARTS - s, PARTS) * n, n), n)


def branch_kernel(at_ref, *refs):
    mixed = refs[:PARTS]
    w_ref, tokens_ref, rows_ref, middle_ref = refs[PARTS : PARTS + 4]
    second, held = refs[PARTS + 4 : -1], refs[-1]
    middle = tokens_ref[...].astype(F32) + rows_ref[4:5, :]
    model = middle.shape[1]
    for s in range(PARTS):
        middle += dot(mixed[s][...].T, w_ref[part_rows(at_ref, s, model), :], 1, 1)
    middle_ref[...] = middle.astype(BF)
    n = second[0].shape[1]
    held[...] = (normalized(middle)[0] * rows_ref[1:2, :] + rows_ref[3:4, :]).astype(BF)
    for s in range(PARTS):
        window = pl.ds(pl.multiple_of(lax.rem(at_ref[PARTS] + s, PARTS) * n, n), n)
        second[s][...] = held[:, window]


def second_norm(at, mixed, w, tokens_part, rows_small):
    part, model = tokens_part.shape
    vmem = pl.BlockSpec(memory_space=pltpu.VMEM)
    return pl.pallas_call(
        branch_kernel,
        out_shape=(
            jax.ShapeDtypeStruct((part, model), BF), *[jax.ShapeDtypeStruct((part, model // PARTS), BF)] * PARTS,
        ),
        in_specs=[pl.BlockSpec(memory_space=pltpu.SMEM)] + [vmem] * (PARTS + 3),
        out_specs=(vmem,) * (1 + PARTS),
        scratch_shapes=[pltpu.VMEM((part, model), BF)],
        compiler_params=pltpu.CompilerParams(vmem_limit_bytes=VMEM),
        cost_estimate=pl.CostEstimate(flops=600_000_000, bytes_accessed=6_000_000, transcendentals=0),
        name="second_norm",
    )(at, *mixed, w, tokens_part, rows_small)


def norm_backward(grad_out, normed, inverse, gain_row):
    scaled = grad_out * gain_row
    inner = jnp.mean(scaled, axis=-1, keepdims=True)
    along = jnp.mean(scaled * normed, axis=-1, keepdims=True)
    return inverse * (scaled - inner - normed * along)


def first_grad_kernel(at_ref, near_ref, back_ref, w_ref, stacked_ref, o0, o1, o2, o3):
    rows, n = near_ref.shape
    wide = back_ref.shape[1]
    stacked_ref[...] = near_ref[...]
    lower = slice(rows - back_ref.shape[0], rows)
    kept = near_ref[lower, n - wide :].astype(F32) + back_ref[...].astype(F32)
    stacked_ref[lower, n - wide :] = kept.astype(BF)
    part = o0.shape[0]
    for s in (2, 1, 3, 0):
        window = pl.ds(pl.multiple_of(lax.rem(at_ref[PARTS] + s, PARTS) * part, part), part)
        (o0, o1, o2, o3)[s][...] = dot(stacked_ref[window, :], w_ref[:, :n], 1, 1).astype(BF)


def first_gradient(at, near, back, weights):
    rows = near.shape[0]
    model = weights.shape[0]
    vmem = pl.BlockSpec(memory_space=pltpu.VMEM)
    return pl.pallas_call(
        first_grad_kernel,
        out_shape=(
            jax.ShapeDtypeStruct(near.shape, BF), *[jax.ShapeDtypeStruct((rows // PARTS, model), BF)] * PARTS,
        ),
        in_specs=[pl.BlockSpec(memory_space=pltpu.SMEM)] + [vmem] * 3,
        out_specs=(vmem,) * (PARTS + 1),
        compiler_params=pltpu.CompilerParams(vmem_limit_bytes=VMEM),
        cost_estimate=pl.CostEstimate(flops=1_600_000_000, bytes_accessed=9_000_000, transcendentals=0),
        name="first_gradient",
    )(at, near, back, weights)


def total(values):
    return jnp.sum(values, axis=0, keepdims=True)


def second_back_kernel(at_ref, *refs):
    grads = refs[:PARTS]
    w_ref, cot_ref, middle_ref, rows_ref, low_ref, sums_ref = refs[PARTS : PARTS + 6]
    blocks, held = refs[PARTS + 6 : -1], refs[-1]
    n = grads[0].shape[1]
    for s in range(PARTS):
        window = pl.ds(pl.multiple_of(lax.rem(at_ref[PARTS] + s, PARTS) * n, n), n)
        held[:, window] = grads[s][...]
    grad = held[...].astype(F32)
    normed, inverse = normalized(middle_ref[...].astype(F32))
    low = (cot_ref[...].astype(F32) + norm_backward(grad, normed, inverse, rows_ref[1:2, :])).astype(BF)
    low_ref[...] = low
    for s in range(PARTS):
        blocks[s][...] = dot(low, w_ref[part_rows(at_ref, s, low.shape[1]), :], 1, 0).T.astype(BF)
    sums_ref[...] = jnp.zeros_like(sums_ref)
    sums_ref[0:1, :] = total(grad * normed)
    sums_ref[1:2, :] = total(grad)
    sums_ref[2:3, :] = total(low.astype(F32))


def second_norm_back(at, grads, w, cot_part, middle, rows_small):
    part, model = cot_part.shape
    vmem = pl.BlockSpec(memory_space=pltpu.VMEM)
    return pl.pallas_call(
        second_back_kernel,
        out_shape=(
            jax.ShapeDtypeStruct((part, model), BF), jax.ShapeDtypeStruct((8, model), F32),
            *[jax.ShapeDtypeStruct((w.shape[1], part), BF)] * PARTS,
        ),
        in_specs=[pl.BlockSpec(memory_space=pltpu.SMEM)] + [vmem] * (PARTS + 4),
        out_specs=(vmem,) * (2 + PARTS),
        scratch_shapes=[pltpu.VMEM((part, model), BF)],
        compiler_params=pltpu.CompilerParams(vmem_limit_bytes=VMEM),
        cost_estimate=pl.CostEstimate(flops=600_000_000, bytes_accessed=6_000_000, transcendentals=0),
        name="second_norm_back",
    )(at, *grads, w, cot_part, middle, rows_small)


def first_back_kernel(*refs):
    tokens_ref, middle_ref, rows_ref, o_ref, sums_ref = refs[PARTS:]
    grad = sum(ref[...].astype(F32) for ref in refs[:PARTS])
    normed, inverse = normalized(tokens_ref[...].astype(F32))
    o_ref[...] = (middle_ref[...].astype(F32) + norm_backward(grad, normed, inverse, rows_ref[0:1, :])).astype(BF)
    sums_ref[...] = jnp.zeros_like(sums_ref)
    sums_ref[0:1, :] = total(grad * normed)
    sums_ref[1:2, :] = total(grad)


def first_norm_back(grads, tokens_part, middle_grad, rows_small):
    vmem = pl.BlockSpec(memory_space=pltpu.VMEM)
    return pl.pallas_call(
        first_back_kernel,
        out_shape=(
            jax.ShapeDtypeStruct(tokens_part.shape, BF), jax.ShapeDtypeStruct((8, tokens_part.shape[1]), F32),
        ),
        in_specs=[vmem] * (PARTS + 3),
        out_specs=(vmem,) * 2,
        compiler_params=pltpu.CompilerParams(vmem_limit_bytes=VMEM),
        cost_estimate=pl.CostEstimate(flops=8_000_000, bytes_accessed=5_000_000, transcendentals=0),
        name="first_norm_back",
    )(*grads, tokens_part, middle_grad, rows_small)


def forward_kernel(at_ref, q_ref, start_ref, k_near, v_near, k_far, v_far, o0, o1, o2, o3,
                   exact_ref, lse_ref, q_heads, acc):
    heads = q_ref.shape[0] // HD
    i = pl.program_id(0)
    half = pl.num_programs(0) * SIDE
    q_heads[...] = by_head(q_ref[...] * jnp.asarray(HD**-0.5, BF), heads)
    acc[...] = jnp.zeros_like(acc)
    start_row = start_ref[...]

    def step(k_ref, v_ref, size, top, base, n, carry):
        peak, total = carry
        first_row = (top - n) * size
        rows = pl.ds(pl.multiple_of(first_row, size), size)
        scores = dot(k_ref[rows, :], q_heads[...], 1, 0)
        allowed = pair_mask(start_row, half + i * SIDE, base + first_row, size)
        scores = jnp.where(jnp.concatenate([allowed] * heads, axis=1), scores, NEGATIVE)
        new_peak = jnp.maximum(peak, jnp.max(scores, axis=0, keepdims=True))
        fade = jnp.exp(peak - new_peak)
        weights = jnp.exp(scores - new_peak)
        total = total * fade + jnp.sum(weights, axis=0, keepdims=True)
        low = weights.astype(BF)
        v_t = v_ref[rows, :].T
        for h in range(heads):
            at, cols = slice(h * HD, (h + 1) * HD), slice(h * SIDE, (h + 1) * SIDE)
            acc[at, :] = acc[at, :] * fade[:, cols] + dot(v_t[at, :], low[:, cols], 1, 0)
        return new_peak, total

    width = heads * SIDE
    near = functools.partial(step, k_near, v_near, SIDE, i, half)
    blocks = k_far.shape[0] // FAR
    far = functools.partial(step, k_far, v_far, FAR, blocks - 1, half - k_far.shape[0])
    carry = jnp.full((1, width), NEGATIVE, F32), jnp.zeros((1, width), F32)
    carry = lax.fori_loop(0, jnp.minimum(PARTS + i - at_ref[i], i) + 1, near, carry)
    peak, total = lax.fori_loop(0, blocks - at_ref[PARTS + 1 + i], far, carry)
    scale = 1.0 / total
    for h in range(heads):
        at, cols = slice(h * HD, (h + 1) * HD), slice(h * SIDE, (h + 1) * SIDE)
        exact = acc[at, :] * scale[:, cols]
        exact_ref[at, :] = exact.astype(BF)
    lse_ref[0] = peak + jnp.log(total)
    place = turned(i, at_ref)
    for s, out in enumerate((o0, o1, o2, o3)):
        @pl.when(place == s)
        def _():
            out[...] = exact_ref[...]


def turned(i, at):
    return lax.rem(i + PARTS - at[PARTS], PARTS)


def attend_forward(at, q_t, start, kv, kv_far):
    channels, rows = q_t.shape
    blocks = rows // SIDE
    width = channels // HD * SIDE
    column = pl.BlockSpec((channels, SIDE), lambda i, f: (0, i))
    return pl.pallas_call(
        forward_kernel,
        out_shape=(
            *[jax.ShapeDtypeStruct((channels, SIDE), BF)] * PARTS,
            jax.ShapeDtypeStruct((channels, rows), BF),
            jax.ShapeDtypeStruct((blocks, 1, width), F32),
        ),
        grid_spec=pltpu.PrefetchScalarGridSpec(
            num_scalar_prefetch=1,
            grid=(blocks,),
            in_specs=[column, pl.BlockSpec((1, SIDE), lambda i, f: (0, i))]
            + [pl.BlockSpec((a.shape[0], channels), lambda i, f, c=c: (0, c)) for a in (kv, kv_far) for c in range(2)],
            out_specs=(
                *[pl.BlockSpec((channels, SIDE), lambda i, f: (0, 0))] * PARTS,
                column,
                pl.BlockSpec((1, 1, width), lambda i, f: (i, 0, 0)),
            ),
            scratch_shapes=[pltpu.VMEM((channels, width), BF), pltpu.VMEM((channels, SIDE), F32)],
        ),
        compiler_params=pltpu.CompilerParams(vmem_limit_bytes=VMEM),
        cost_estimate=pl.CostEstimate(flops=6_000_000_000, bytes_accessed=6_000_000, transcendentals=4_000_000),
        name="attend_forward",
    )(at, q_t, start, kv, kv, kv_far, kv_far)


def backward_kernel(near, at_ref, q_ref, g0, g1, g2, g3, exact_ref, lse_ref, start_ref, k_ref, v_ref, add_ref,
                    dq_ref, dkv_ref, q_heads, g_heads, dq_acc, dk_acc, dv_acc):
    heads = q_ref.shape[0] // HD
    i = pl.program_id(0)
    blocks = pl.num_programs(0)
    half = blocks * SIDE
    size, base = (SIDE, half) if near else (FAR, half - k_ref.shape[0])
    q_heads[...] = by_head(q_ref[...] * jnp.asarray(HD**-0.5, BF), heads)
    place = turned(i, at_ref)
    grad = g0[...]
    for s, other in enumerate((g1, g2, g3)):
        grad = jnp.where(place == s + 1, other[...], grad)
    g_heads[...] = by_head(grad, heads)
    product = grad.astype(F32) * exact_ref[...].astype(F32)
    delta = jnp.concatenate(
        [jnp.sum(product[h * HD : (h + 1) * HD, :], axis=0, keepdims=True) for h in range(heads)], axis=1
    )
    dq_acc[...] = jnp.zeros_like(dq_acc)

    @pl.when(i == 0)
    def _():
        dk_acc[...] = jnp.zeros_like(dk_acc)
        dv_acc[...] = jnp.zeros_like(dv_acc)

    start_row = start_ref[...]
    lse = lse_ref[0]

    def step(j, carry):
        rows = pl.ds(pl.multiple_of(j * size, size), size)
        k_block = k_ref[rows, :]
        scores = dot(k_block, q_heads[...], 1, 0)
        allowed = pair_mask(start_row, half + i * SIDE, base + j * size, size)
        scores = jnp.where(jnp.concatenate([allowed] * heads, axis=1), scores, NEGATIVE)
        weights = jnp.exp(scores - lse)
        grad_weights = dot(v_ref[rows, :], g_heads[...], 1, 0)
        grad_scores = (weights * (grad_weights - delta)).astype(BF)
        dv_acc[rows, :] += dot(weights.astype(BF), g_heads[...], 1, 1)
        dk_acc[rows, :] += dot(grad_scores, q_heads[...], 1, 1)
        k_t = k_block.T
        for h in range(heads):
            at, cols = slice(h * HD, (h + 1) * HD), slice(h * SIDE, (h + 1) * SIDE)
            dq_acc[at, :] += dot(k_t[at, :], grad_scores[:, cols], 1, 0)
        return carry

    if near:
        lax.fori_loop(jnp.maximum(at_ref[i] - PARTS, 0), i + 1, step, 0)
        n = q_ref.shape[0]
        at = pl.ds(pl.multiple_of(i * SIDE, SIDE), SIDE)
        dkv_ref[at, :n] = (dq_acc[...] * HD**-0.5 + add_ref[...]).T.astype(BF)
    else:
        lax.fori_loop(at_ref[PARTS + 1 + i], k_ref.shape[0] // FAR, step, 0)
        dq_ref[...] = dq_acc[...] * HD**-0.5

    @pl.when(i == blocks - 1)
    def _():
        n = q_ref.shape[0]
        first_column = dkv_ref.shape[1] - 2 * n
        skipped = dk_acc.shape[0] - dkv_ref.shape[0]
        dkv_ref[:, first_column : first_column + n] = dk_acc[skipped:, :].astype(BF)
        dkv_ref[:, first_column + n :] = dv_acc[skipped:, :].astype(BF)


def far_kernel(at_ref, q_ref, g0, g1, g2, g3, exact_ref, lse_ref, start_ref, k_ref, v_ref, *rest):
    backward_kernel(False, at_ref, q_ref, g0, g1, g2, g3, exact_ref, lse_ref, start_ref, k_ref, v_ref, None, *rest)


def near_kernel(at_ref, q_ref, g0, g1, g2, g3, exact_ref, lse_ref, start_ref, k_ref, v_ref, add_ref, *rest):
    backward_kernel(True, at_ref, q_ref, g0, g1, g2, g3, exact_ref, lse_ref, start_ref, k_ref, v_ref, add_ref,
                    None, *rest)


def attend_backward(near, at, q_t, grads, exact_t, lse, start, kv, add=None):
    channels, rows = q_t.shape
    blocks = rows // SIDE
    width = channels // HD * SIDE
    column = pl.BlockSpec((channels, SIDE), lambda i, f: (0, i))
    block = pl.BlockSpec((channels, SIDE), lambda i, f: (0, 0))
    in_specs = [
        column,
        *[block] * PARTS,
        column,
        pl.BlockSpec((1, 1, width), lambda i, f: (i, 0, 0)),
        pl.BlockSpec((1, SIDE), lambda i, f: (0, i)),
    ] + [pl.BlockSpec((kv.shape[0], channels), lambda i, f, c=c: (0, c)) for c in range(2)]
    args = [at, q_t, *grads, exact_t, lse, start, kv, kv]
    if near:
        in_specs.append(column)
        args.append(add)
        out_shape = (jax.ShapeDtypeStruct((rows, 3 * channels), BF),)
        out_specs = (pl.BlockSpec((rows, 3 * channels), lambda i, f: (0, 0)),)
    else:
        out_shape = jax.ShapeDtypeStruct((channels, rows), F32), jax.ShapeDtypeStruct((REACH, 2 * channels), BF)
        out_specs = column, pl.BlockSpec((REACH, 2 * channels), lambda i, f: (0, 0))
    return pl.pallas_call(
        near_kernel if near else far_kernel,
        out_shape=out_shape,
        grid_spec=pltpu.PrefetchScalarGridSpec(
            num_scalar_prefetch=1,
            grid=(blocks,),
            in_specs=in_specs,
            out_specs=out_specs,
            scratch_shapes=[
                pltpu.VMEM((channels, width), BF),
                pltpu.VMEM((channels, width), BF),
                pltpu.VMEM((channels, SIDE), F32),
                pltpu.VMEM((kv.shape[0], channels), F32),
                pltpu.VMEM((kv.shape[0], channels), F32),
            ],
        ),
        compiler_params=pltpu.CompilerParams(vmem_limit_bytes=VMEM),
        cost_estimate=pl.CostEstimate(flops=9_000_000_000, bytes_accessed=6_000_000, transcendentals=4_000_000),
        name="attend_near" if near else "attend_far",
    )(*args)


def slots_kernel(target_ref, x_ref, o_ref):
    place = lax.broadcasted_iota(jnp.int32, (o_ref.shape[0], x_ref.shape[0]), 0) + pl.program_id(0) * o_ref.shape[0]
    o_ref[...] = dot((place == target_ref[...]).astype(F32).astype(BF), x_ref[...], 1, 0).astype(BF)


def to_slots(target, x, slots):
    return pl.pallas_call(
        slots_kernel,
        out_shape=jax.ShapeDtypeStruct((slots, x.shape[1]), BF),
        grid=(slots // SIDE,),
        in_specs=[pl.BlockSpec((1, x.shape[0]), lambda i: (0, 0)), pl.BlockSpec(x.shape, lambda i: (0, 0))],
        out_specs=pl.BlockSpec((SIDE, x.shape[1]), lambda i: (i, 0)),
        compiler_params=pltpu.CompilerParams(vmem_limit_bytes=VMEM),
        cost_estimate=pl.CostEstimate(flops=1_200_000_000, bytes_accessed=2_000_000, transcendentals=0),
        name="to_slots",
    )(target[None, :], x)


def tokens_kernel(target_ref, x_ref, *outs):
    place = lax.broadcasted_iota(jnp.int32, (SIDE, x_ref.shape[0]), 1)
    for s, out in enumerate(outs):
        rows = slice(s * SIDE, (s + 1) * SIDE)
        out[...] = dot((place == target_ref[rows, :]).astype(F32).astype(BF), x_ref[...], 1, 0).astype(BF)


def to_tokens(target, x):
    blocks = target.shape[0] // SIDE
    vmem = pl.BlockSpec(memory_space=pltpu.VMEM)
    return pl.pallas_call(
        tokens_kernel,
        out_shape=(jax.ShapeDtypeStruct((SIDE, x.shape[1]), BF),) * blocks,
        in_specs=[vmem] * 2,
        out_specs=(vmem,) * blocks,
        compiler_params=pltpu.CompilerParams(vmem_limit_bytes=VMEM),
        cost_estimate=pl.CostEstimate(flops=1_200_000_000, bytes_accessed=2_000_000, transcendentals=0),
        name="to_tokens",
    )(target[:, None], x)


def sum_kernel(at_ref, target_ref, x_ref, *refs):
    middle, o_ref = refs[:-1], refs[-1]
    n = SIDE
    place = lax.broadcasted_iota(jnp.int32, (n, x_ref.shape[0]), 1)
    for s, part in enumerate(middle):
        one = (place == target_ref[s * n : (s + 1) * n, :]).astype(F32).astype(BF)
        o_ref[part_rows(at_ref, s, n), :] = (part[...].astype(F32) + dot(one, x_ref[...], 1, 0)).astype(BF)


def block_output(at, target, x, middle):
    vmem = pl.BlockSpec(memory_space=pltpu.VMEM)
    return pl.pallas_call(
        sum_kernel,
        out_shape=jax.ShapeDtypeStruct((target.shape[0], x.shape[1]), BF),
        in_specs=[pl.BlockSpec(memory_space=pltpu.SMEM)] + [vmem] * (2 + len(middle)),
        out_specs=vmem,
        compiler_params=pltpu.CompilerParams(vmem_limit_bytes=VMEM),
        cost_estimate=pl.CostEstimate(flops=1_200_000_000, bytes_accessed=2_000_000, transcendentals=0),
        name="block_output",
    )(at, target[:, None], x, *middle)


def join_kernel(got_ref, *refs):
    outs, held = refs[:-1], refs[-1]
    capacity = got_ref.shape[1] // len(outs)
    for f in range(got_ref.shape[0] // 2):
        both = got_ref[2 * f].astype(F32) + got_ref[2 * f + 1].astype(F32)
        for e in range(len(outs)):
            held[e, f * capacity : (f + 1) * capacity, :] = both[e * capacity : (e + 1) * capacity, :]
    for e, out in enumerate(outs):
        out[...] = held[e].astype(BF)


def join(got, experts):
    shape = (got.shape[0] // 2 * (got.shape[1] // experts), got.shape[2])
    return pl.pallas_call(
        join_kernel,
        out_shape=(jax.ShapeDtypeStruct(shape, BF),) * experts,
        scratch_shapes=[pltpu.VMEM((experts, *shape), F32)],
        compiler_params=pltpu.CompilerParams(vmem_limit_bytes=VMEM),
        cost_estimate=pl.CostEstimate(flops=600_000, bytes_accessed=2_000_000, transcendentals=0),
        name="join",
    )(got)


def spread_kernel(bias_ref, *refs):
    parts, (o_ref, held, piece) = refs[:-3], refs[-3:]
    experts, rows = held.shape[:2]
    capacity = o_ref.shape[1] // experts
    for e in range(experts):
        if len(parts) == 1:
            total = parts[0][e * rows : (e + 1) * rows, :].astype(F32)
        else:
            total = sum(part[...].astype(F32) for part in parts[e * PARTS : (e + 1) * PARTS])
        held[e] = total + bias_ref[e : e + 1, :]
    for f in range(o_ref.shape[0] // 2):
        for e in range(experts):
            piece[e * capacity : (e + 1) * capacity, :] = held[e, f * capacity : (f + 1) * capacity, :]
        low = piece[...].astype(BF)
        o_ref[2 * f] = low
        o_ref[2 * f + 1] = low


def spread(parts, bias, capacity):
    experts, n = bias.shape
    rows = parts[0].shape[0] // (experts if len(parts) == 1 else 1)
    return pl.pallas_call(
        spread_kernel,
        out_shape=jax.ShapeDtypeStruct((rows // capacity * 2, experts * capacity, n), BF),
        scratch_shapes=[pltpu.VMEM((experts, rows, n), F32), pltpu.VMEM((experts * capacity, n), F32)],
        compiler_params=pltpu.CompilerParams(vmem_limit_bytes=VMEM),
        cost_estimate=pl.CostEstimate(flops=2_400_000, bytes_accessed=4_000_000, transcendentals=0),
        name="spread",
    )(bias, *parts)


def expert_kernel(at_ref, r0, r1, r2, r3, w_ref, b_ref, g_ref, act_ref, hg_ref, rows_ref, *outs):
    parts = (r0, r1, r2, r3)
    n = r0.shape[1]
    windows = [
        pl.ds(pl.multiple_of(lax.rem(at_ref[PARTS] + PARTS - s, PARTS) * n, n), n) for s in range(PARTS)
    ]
    for s in range(PARTS):
        rows_ref[:, windows[s]] = parts[s][...]
    inner = w_ref.shape[2]
    for j in range(2):
        cols = slice(j * inner // 2, (j + 1) * inner // 2)
        hidden = dot(rows_ref[...], w_ref[0, :, cols], 1, 0) + b_ref[0, :, cols].astype(F32)
        gate = jax.nn.sigmoid(hidden)
        act_ref[:, cols] = (hidden * gate).astype(BF)
        hg_ref[:, cols] = (g_ref[0, :, cols] * (gate * (1.0 + hidden * (1.0 - gate)))).astype(BF)
    for s in range(PARTS):
        outs[s][...] = dot(hg_ref[...], w_ref[0, windows[s], :], 1, 1).astype(BF)


def run_expert(e, at, parts, w_up, up_bias, active_grad):
    rows, n = parts[0].shape
    model, inner = w_up.shape[1:]
    whole = pl.BlockSpec((rows, n), lambda j, f: (0, 0))
    full = pl.BlockSpec((rows, inner), lambda j, f: (0, 0))
    return pl.pallas_call(
        expert_kernel,
        out_shape=(
            jax.ShapeDtypeStruct((rows, inner), BF),
            jax.ShapeDtypeStruct((rows, inner), BF),
            jax.ShapeDtypeStruct((rows, model), BF),
            *[jax.ShapeDtypeStruct((rows, n), BF)] * PARTS,
        ),
        grid_spec=pltpu.PrefetchScalarGridSpec(
            num_scalar_prefetch=1,
            grid=(1,),
            in_specs=[whole] * PARTS + [
                pl.BlockSpec((1, model, inner), lambda j, f: (e, 0, 0)),
                pl.BlockSpec((1, 1, inner), lambda j, f: (e, 0, 0)),
                pl.BlockSpec((1, rows, inner), lambda j, f: (e, 0, 0)),
            ],
            out_specs=(
                full, full,
                pl.BlockSpec((rows, model), lambda j, f: (0, 0)),
                *[whole] * PARTS,
            ),
        ),
        compiler_params=pltpu.CompilerParams(vmem_limit_bytes=VMEM),
        cost_estimate=pl.CostEstimate(flops=2_400_000_000, bytes_accessed=8_000_000, transcendentals=600_000),
        name="expert",
    )(at, *parts, w_up, up_bias[:, None, :], active_grad)


def result_kernel(a_ref, w_ref, o_ref):
    n = o_ref.shape[2]
    for t in range(o_ref.shape[0]):
        o_ref[t] = dot(a_ref[0], w_ref[0, :, t * n : (t + 1) * n], 1, 0).astype(BF)


def expert_results(active, w_down):
    held, rows, inner = active.shape
    model = w_down.shape[2]
    n = model // PARTS
    return pl.pallas_call(
        result_kernel,
        out_shape=jax.ShapeDtypeStruct((PARTS, held * rows, n), BF),
        grid=(held,),
        in_specs=[
            pl.BlockSpec((1, rows, inner), lambda e: (e, 0, 0)),
            pl.BlockSpec((1, inner, model), lambda e: (e, 0, 0)),
        ],
        out_specs=pl.BlockSpec((PARTS, rows, n), lambda e: (0, e, 0)),
        compiler_params=pltpu.CompilerParams(vmem_limit_bytes=VMEM),
        cost_estimate=pl.CostEstimate(flops=2_400_000_000, bytes_accessed=9_000_000, transcendentals=0),
        name="results",
    )(active, w_down)


def copy_kernel(x_ref, o_ref):
    o_ref[...] = x_ref[...]


def side_by_side(x):
    rows, n = x.shape[0] // PARTS, x.shape[1]
    return pl.pallas_call(
        copy_kernel,
        out_shape=jax.ShapeDtypeStruct((rows, PARTS * n), x.dtype),
        grid=(PARTS,),
        in_specs=[pl.BlockSpec((rows, n), lambda t: (t, 0))],
        out_specs=pl.BlockSpec((rows, n), lambda t: (0, t)),
        compiler_params=pltpu.CompilerParams(vmem_limit_bytes=VMEM),
        cost_estimate=pl.CostEstimate(flops=0, bytes_accessed=4_000_000, transcendentals=0),
        name="side_by_side",
    )(x)


def weight_kernel(x_ref, grads_ref, branch_ref, mixed_ref, o_ref):
    n = grads_ref.shape[1]
    groups, shard, _ = o_ref.shape
    grads = dot(x_ref[...].T, grads_ref[...], 1, 0).astype(BF)
    branch = dot(branch_ref[...].T, mixed_ref[...], 1, 1).astype(BF)
    for g in range(groups):
        rows = slice(g * shard, (g + 1) * shard)
        o_ref[g, :shard, :n] = grads[rows, :]
        o_ref[g, :shard, n:] = branch[rows, :]


def weight_gradients(x, grads, branch, mixed, groups):
    rows, model = x.shape
    n, channels = grads.shape[1], mixed.shape[0]
    block = pl.BlockSpec((rows, SIDE), lambda i: (0, i))
    shape = (groups, model // groups, n + channels)
    return pl.pallas_call(
        weight_kernel,
        out_shape=jax.ShapeDtypeStruct(shape, BF),
        grid=(model // SIDE,),
        in_specs=[
            block, pl.BlockSpec((rows, n), lambda i: (0, 0)), block, pl.BlockSpec((channels, rows), lambda i: (0, 0)),
        ],
        out_specs=pl.BlockSpec((groups * SIDE // model, *shape[1:]), lambda i: (i, 0, 0)),
        compiler_params=pltpu.CompilerParams(vmem_limit_bytes=VMEM),
        cost_estimate=pl.CostEstimate(flops=2_200_000_000, bytes_accessed=8_000_000, transcendentals=0),
        name="weight_gradients",
    )(x, grads, branch, mixed)


def after(value, *others):
    return lax.optimization_barrier((value, *others))[0]


def hops(axis, s):
    n = lax.axis_size(axis)
    return [(i, (i + s) % n) for i in range(n)]


def swapped(blocks, sign, name):
    with jax.named_scope("x_" + name):
        return [blocks[0]] + [lax.ppermute(blocks[s], "tp", hops("tp", sign * s)) for s in range(1, PARTS)]


def copied(block, name):
    return swapped([block] * PARTS, 1, name)


def in_order(parts, start, axis):
    turned_parts = [parts[-k % PARTS] for k in range(PARTS)]
    size = parts[0].shape[axis]
    both = jnp.concatenate(turned_parts + turned_parts[:-1], axis=axis)
    return lax.dynamic_slice_in_dim(both, (PARTS - start) % PARTS * size, PARTS * size, axis)


def on_device(tokens, cotangent, expert_ids, segment_ids, priority, w_qkv, w_out, norm_gains, norm_shifts,
              qv_bias, w_up, up_bias, w_down, down_bias):
    rows, model = tokens.shape
    channels = w_qkv.shape[2]
    heads = channels // HD
    seq_len = segment_ids.shape[0]
    f_count, c_count = lax.axis_size(FC[:3]), lax.axis_size("ctx")
    groups = f_count * c_count
    ctx_at, tp_at = lax.axis_index("ctx"), lax.axis_index("tp")
    held = w_up.shape[0]
    experts = held * groups
    capacity = (9 * seq_len + 8 * experts - 1) // (8 * experts)
    slots = experts * capacity
    shard = model // groups
    part = rows // PARTS
    width = model // PARTS
    bias_size = qv_bias.size

    bias_column = jnp.pad(qv_bias.reshape(-1), (0, shard - bias_size))[None]
    small = jnp.concatenate([norm_gains, norm_shifts, bias_column], axis=0).T
    small = jnp.pad(small, ((0, 0), (0, 128 - small.shape[1])))
    pack = jnp.concatenate([jnp.moveaxis(w_qkv, 0, 1).reshape(shard, 3 * channels), w_out.T, small], axis=1)
    packed = lax.all_to_all(jnp.broadcast_to(pack[None], (groups, *pack.shape)), FC, 0, 0, tiled=True)
    packed = packed.reshape(model, -1)
    lane = lax.broadcasted_iota(jnp.int32, (model, 2 * channels), 1)
    line = lax.broadcasted_iota(jnp.int32, (model, 2 * channels), 0)
    inside, group = line % shard, line // shard
    ends = qv_bias.shape[2]
    goal = (inside // (heads * ends) * channels + inside // ends % heads * HD + group * ends + inside % ends)
    move = ((goal == lane) & (inside < bias_size)).astype(BF)
    owner = expert_ids[:, 0]
    rank = priority[0]
    earlier_ids = lax.ppermute(after(expert_ids, pack) + 1, "ctx", [(0, 1)])[:, 0]
    before = (owner[None, :] == owner[:, None]) & (rank[None, :] < rank[:, None])
    carried = earlier_ids[None, :] == owner[:, None] + 1
    slot = jnp.sum(before.astype(jnp.int32), axis=1) + jnp.sum(carried.astype(jnp.int32), axis=1)
    target = jnp.where(slot < capacity, owner * capacity + slot, slots)
    places = [(tp_at + PARTS - s) % PARTS for s in range(PARTS)]
    target = jnp.concatenate([lax.dynamic_slice_in_dim(target, p * part, part) for p in places])

    def exchanged(sent, name):
        with jax.named_scope("x_" + name):
            return lax.all_to_all(sent, FC, 0, 0, tiled=True)

    def sent_rows(columns):
        return to_slots(target, columns, slots).reshape(groups, held * capacity, width)

    seg_own = lax.dynamic_slice_in_dim(segment_ids, ctx_at * rows, rows)
    start = jnp.sum((segment_ids[None, :] < seg_own[:, None]).astype(jnp.int32), axis=1)
    start = start + jnp.where(ctx_at == 0, rows, 0)
    first = start[::SIDE]
    at = jnp.concatenate([first // SIDE, tp_at[None], (first - (rows - HALO)) // FAR]).astype(jnp.int32)
    start = start[None, :]
    packed, start, at, move, target = lax.optimization_barrier((packed, start, at, move, target))
    rows_small, bias_row, bias_col = small_rows(packed, move)
    q_t, kv, first_low, halo = first_projection(tokens, packed, rows_small, bias_row, bias_col, channels)
    kv_far = lax.ppermute(halo, "ctx", [(0, 1)])
    out_all = lax.all_gather(packed[:, 3 * channels : 4 * channels], "tp", axis=0, tiled=True)
    cot_columns = [lax.dynamic_slice(cotangent, (p * part, tp_at * width), (part, width)) for p in places]
    cot_sent = sent_rows(jnp.concatenate(cot_columns))
    cot_got = exchanged(after(cot_sent, kv), "cot")
    *mixed, exact_t, lse = attend_forward(at, q_t, start, kv, kv_far)
    mixed = swapped(mixed, 1, "mixed")

    tokens_part = lax.dynamic_slice_in_dim(tokens, tp_at * part, part)
    cot_part = lax.dynamic_slice_in_dim(cotangent, tp_at * part, part)
    cot_mine = jnp.concatenate(join(after(cot_got, *mixed[1:]), held))
    cot_all = lax.all_gather(cot_mine, "tp", axis=0, tiled=True)
    middle, *blocks = second_norm(at, mixed, out_all, after(tokens_part, cot_mine), rows_small)
    second_sent = sent_rows(jnp.concatenate(swapped(blocks, 1, "second")))

    second_got = exchanged(second_sent, "rows")
    middle_late = after(middle, second_sent)
    middle_parts = swapped(
        [lax.dynamic_slice_in_dim(middle_late, (tp_at + s) % PARTS * width, width, 1) for s in range(PARTS)], 1, "middle"
    )
    second_got, middle_parts = lax.optimization_barrier((second_got, middle_parts))
    mine = join(second_got, held)
    parts = [copied(m, "rows") for m in mine]
    expert_grads = side_by_side(after(cot_all, mine[0])).reshape(held, -1, model)
    active_grad = jnp.einsum("emd,efd->emf", expert_grads, w_down, preferred_element_type=F32)
    done = [run_expert(e, at, parts[e], w_up, up_bias, active_grad) for e in range(held)]
    back_parts = [p for d in done for p in swapped(d[3:], -1, "back")]
    active_low = jnp.stack([d[0] for d in done])
    results = expert_results(active_low, w_down)
    back_sent = spread(back_parts, jnp.zeros((held, width), F32), capacity)
    back_sent, results = lax.optimization_barrier((back_sent, results))
    back_got = exchanged(back_sent, "back")
    result_sum = lax.psum_scatter(results, "tp", scatter_dimension=0, tiled=True)
    active_late, rows_late, hidden_late, grads_late = lax.optimization_barrier(
        (active_low, [d[2] for d in done], [d[1] for d in done], expert_grads, back_sent)
    )[:4]
    w_down_grad = jnp.einsum("emf,emd->efd", active_late, grads_late, preferred_element_type=F32)
    w_up_grad = jnp.einsum(
        "emd,emf->edf", jnp.stack(rows_late), jnp.stack(hidden_late), preferred_element_type=F32
    )
    back_got, w_down_grad, w_up_grad = lax.optimization_barrier((back_got, w_down_grad, w_up_grad))
    grad_blocks = swapped(to_tokens(target, back_got.reshape(slots, width)), -1, "grads")
    grad_blocks[0], result_sum = lax.optimization_barrier((grad_blocks[0], result_sum))
    bias_columns = lax.dynamic_slice_in_dim(down_bias, tp_at * width, width, 1).astype(F32)
    result_sent = spread([result_sum.reshape(-1, width)], bias_columns, capacity)
    result_got = exchanged(result_sent, "result")

    branch_low, second_sums, *mixed_grads = second_norm_back(at, grad_blocks, out_all, cot_part, middle, rows_small)
    grads_t = swapped(mixed_grads, -1, "mixedgrads")
    branch_all = lax.all_gather(branch_low, "tp", axis=0, tiled=True)

    dq_far, dkv_far = attend_backward(False, at, q_t, grads_t, exact_t, lse, start, kv_far)
    kv_back = lax.ppermute(dkv_far, "ctx", [(1, 0)])
    (near_grad,) = attend_backward(True, at, q_t, grads_t, exact_t, lse, start, kv, dq_far)

    result_got = after(result_got, near_grad, kv_back)
    block_columns = block_output(at, target, result_got.reshape(slots, width), middle_parts)
    block_all = lax.all_gather(block_columns, "tp", axis=0, tiled=True)
    near_grad, block_columns = lax.optimization_barrier((near_grad, block_columns))
    stacked, *first_blocks = first_gradient(at, near_grad, kv_back, packed)
    first_parts = swapped(first_blocks, 1, "firstsum")

    weight_tiles = weight_gradients(first_low, stacked, branch_all, exact_t, groups)
    weight_got = exchanged(weight_tiles, "weights")
    first_parts, block_all = lax.optimization_barrier((first_parts, block_all))

    tokens_grad_part, first_sums = first_norm_back(first_parts, tokens_part, branch_low, rows_small)
    tokens_grad = lax.all_gather(tokens_grad_part, "tp", axis=0, tiled=True)
    block_out = side_by_side(after(block_all, tokens_grad_part))
    stacked, second_sums = lax.optimization_barrier((stacked, second_sums, tokens_grad_part))[:2]
    sums = jnp.concatenate([first_sums[:2], second_sums[:3]])
    stacked_sum = jnp.sum(stacked.astype(F32), axis=0)
    bias_sum = jnp.stack([stacked_sum[:channels], stacked_sum[2 * channels :]])
    bias_tiles = bias_sum.reshape(2, heads, groups, -1).transpose(2, 0, 1, 3).reshape(groups, -1)
    sum_tiles = sums.reshape(5, groups, shard).transpose(1, 0, 2).reshape(groups, -1)
    tail = jnp.concatenate([sum_tiles, bias_tiles], axis=1)
    tail = jnp.pad(tail, ((0, 0), (0, 256 - tail.shape[1]))).reshape(groups, 1, 256)
    tail, weight_got = lax.optimization_barrier((tail, weight_got))
    tail = exchanged(tail, "sums").sum(axis=0)[0]
    got = weight_got.astype(F32).sum(axis=0)
    qkv_shard = jnp.moveaxis(got[:, : 3 * channels].reshape(shard, 3, channels), 1, 0)
    out_shard = got[:, 3 * channels :].T
    bias_shard = tail[5 * shard : 5 * shard + bias_size].reshape(qv_bias.shape)
    norms = sum(copied(tail[: 5 * shard].reshape(5, shard), "norms"))

    hidden_late, cot_late = lax.optimization_barrier((jnp.stack(hidden_late), expert_grads, tokens_grad_part))[:2]
    up_bias_grad = jnp.sum(hidden_late.astype(F32), axis=1)
    down_bias_grad = jnp.sum(cot_late.astype(F32), axis=1)
    gain_shard = jnp.stack([norms[0], norms[2]])
    shift_shard = jnp.stack([norms[1], norms[3], norms[4]])
    return (block_out, tokens_grad, qkv_shard, out_shard, gain_shard, shift_shard, bias_shard,
            w_up_grad, up_bias_grad, w_down_grad, down_bias_grad)


def solution(mesh):
    devices = mesh.devices.reshape(2, 4, 2, mesh.shape["ctx"], mesh.shape["tp"])
    chips = Mesh(devices, ("y_hi", "z", "core", "ctx", "tp"))
    token, weight = P(FC, None), P(None, FC)
    experts = P(FC, None, "tp"), P(FC, "tp"), P(FC, "tp", None), P(FC, None)
    shared = P(None, FC, "tp"), P("tp", FC), weight, weight, P(None, "tp", FC)
    return jax.shard_map(
        on_device,
        mesh=chips,
        in_specs=(token, token, token, P(FC[:3]), token, *shared, *experts),
        out_specs=(token, token, *shared, *experts),
        check_vma=False,
    )
```

```python
import functools

import jax
import jax.numpy as jnp
from jax import lax
from jax.experimental import pallas as pl
from jax.experimental.pallas import tpu as pltpu
from jax.sharding import Mesh, PartitionSpec as P

HD = 64
EPSILON = 1e-05
NEGATIVE = -1e30
REACH = 800
SIDE = 256
FC = ("y_hi", "z", "core", "ctx")
HALO = 896
FAR = 128
PARTS = 4
VMEM = 40 * 2**20
BF = jnp.bfloat16
F32 = jnp.float32


def dot(a, b, ca, cb):
    return lax.dot_general(a, b, (((ca,), (cb,)), ((), ())), preferred_element_type=F32)


def by_head(cols, heads):
    row = lax.broadcasted_iota(jnp.int32, cols.shape, 0) // HD
    zero = jnp.zeros_like(cols)
    return jnp.concatenate([jnp.where(row == h, cols, zero) for h in range(heads)], axis=1)


def pair_mask(start_row, q_first, k_first, size):
    k_pos = lax.broadcasted_iota(jnp.int32, (size, SIDE), 0) + k_first
    q_pos = lax.broadcasted_iota(jnp.int32, (size, SIDE), 1) + q_first
    return (k_pos >= start_row) & (k_pos <= q_pos)


def normalized(values):
    centre = values - jnp.mean(values, axis=-1, keepdims=True)
    variance = jnp.mean(centre * centre, axis=-1, keepdims=True)
    inverse = lax.rsqrt(variance + EPSILON)
    return centre * inverse, inverse


def small_kernel(small_ref, move_ref, rows_ref, bias_ref, column_ref):
    small = small_ref[...]
    rows_ref[...] = small.astype(F32).T[:8, :]
    column = dot(move_ref[...], small, 0, 0)
    column_ref[...] = column
    bias_ref[...] = column.T[:8, :]


def small_rows(packed, move):
    model, wide = packed.shape
    return pl.pallas_call(
        small_kernel,
        out_shape=(
            jax.ShapeDtypeStruct((8, model), F32),
            jax.ShapeDtypeStruct((8, move.shape[1]), F32),
            jax.ShapeDtypeStruct((move.shape[1], 128), F32),
        ),
        grid=(1,),
        in_specs=[
            pl.BlockSpec((model, 128), lambda i: (0, wide // 128 - 1)),
            pl.BlockSpec(move.shape, lambda i: (0, 0)),
        ],
        out_specs=(
            pl.BlockSpec((8, model), lambda i: (0, 0)),
            pl.BlockSpec((8, move.shape[1]), lambda i: (0, 0)),
            pl.BlockSpec((move.shape[1], 128), lambda i: (0, 0)),
        ),
        compiler_params=pltpu.CompilerParams(vmem_limit_bytes=VMEM),
        cost_estimate=pl.CostEstimate(flops=200_000_000, bytes_accessed=1_500_000, transcendentals=0),
        name="small_rows",
    )(packed, move)


def first_kernel(own_ref, w_ref, rows_ref, bias_ref, column_ref, q_ref, kv_ref, low_ref, halo_ref):
    channels = q_ref.shape[0]
    low = (normalized(own_ref[...].astype(F32))[0] * rows_ref[0:1, :] + rows_ref[2:3, :]).astype(BF)
    low_ref[...] = low
    q_ref[...] = (dot(low, w_ref[:, :channels], 1, 0).T + column_ref[:channels, 5:6]).astype(BF)
    kv = dot(low, w_ref[:, channels : 3 * channels], 1, 0)
    kv_ref[:, :channels] = kv[:, :channels].astype(BF)
    kv_ref[:, channels:] = (kv[:, channels:] + bias_ref[5:6, channels:]).astype(BF)
    i = pl.program_id(0)
    skipped = PARTS * SIDE - HALO

    @pl.when(i == 0)
    def _():
        halo_ref[: SIDE - skipped, :] = kv_ref[skipped:, :]

    @pl.when(i > 0)
    def _():
        halo_ref[pl.ds(pl.multiple_of(i * SIDE - skipped, FAR), SIDE), :] = kv_ref[...]


def first_projection(tokens, weights, rows_small, bias, column, channels):
    rows, model = tokens.shape

    def whole(a):
        return pl.BlockSpec(a.shape, lambda i: (0,) * a.ndim)

    return pl.pallas_call(
        first_kernel,
        out_shape=(
            jax.ShapeDtypeStruct((channels, rows), BF),
            jax.ShapeDtypeStruct((rows, 2 * channels), BF),
            jax.ShapeDtypeStruct((rows, model), BF),
            jax.ShapeDtypeStruct((HALO, 2 * channels), BF),
        ),
        grid=(rows // SIDE,),
        in_specs=[
            pl.BlockSpec((SIDE, model), lambda i: (i, 0)),
            whole(weights), whole(rows_small), whole(bias), whole(column),
        ],
        out_specs=(
            pl.BlockSpec((channels, SIDE), lambda i: (0, i)),
            pl.BlockSpec((SIDE, 2 * channels), lambda i: (i, 0)),
            pl.BlockSpec((SIDE, model), lambda i: (i, 0)),
            pl.BlockSpec((HALO, 2 * channels), lambda i: (0, 0)),
        ),
        compiler_params=pltpu.CompilerParams(vmem_limit_bytes=VMEM),
        cost_estimate=pl.CostEstimate(flops=1_900_000_000, bytes_accessed=6_000_000, transcendentals=0),
        name="first_projection",
    )(tokens, weights, rows_small, bias, column)


def part_rows(at_ref, s, n):
    return pl.ds(pl.multiple_of(lax.rem(at_ref[PARTS] + PARTS - s, PARTS) * n, n), n)


def branch_kernel(at_ref, *refs):
    mixed = refs[:PARTS]
    w_ref, tokens_ref, rows_ref, middle_ref = refs[PARTS : PARTS + 4]
    second, held = refs[PARTS + 4 : -1], refs[-1]
    middle = tokens_ref[...].astype(F32) + rows_ref[4:5, :]
    model = middle.shape[1]
    for s in range(PARTS):
        middle += dot(mixed[s][...].T, w_ref[part_rows(at_ref, s, model), :], 1, 1)
    middle_ref[...] = middle.astype(BF)
    n = second[0].shape[1]
    held[...] = (normalized(middle)[0] * rows_ref[1:2, :] + rows_ref[3:4, :]).astype(BF)
    for s in range(PARTS):
        window = pl.ds(pl.multiple_of(lax.rem(at_ref[PARTS] + s, PARTS) * n, n), n)
        second[s][...] = held[:, window]


def second_norm(at, mixed, w, tokens_part, rows_small):
    part, model = tokens_part.shape
    vmem = pl.BlockSpec(memory_space=pltpu.VMEM)
    return pl.pallas_call(
        branch_kernel,
        out_shape=(
            jax.ShapeDtypeStruct((part, model), BF), *[jax.ShapeDtypeStruct((part, model // PARTS), BF)] * PARTS,
        ),
        in_specs=[pl.BlockSpec(memory_space=pltpu.SMEM)] + [vmem] * (PARTS + 3),
        out_specs=(vmem,) * (1 + PARTS),
        scratch_shapes=[pltpu.VMEM((part, model), BF)],
        compiler_params=pltpu.CompilerParams(vmem_limit_bytes=VMEM),
        cost_estimate=pl.CostEstimate(flops=600_000_000, bytes_accessed=6_000_000, transcendentals=0),
        name="second_norm",
    )(at, *mixed, w, tokens_part, rows_small)


def norm_backward(grad_out, normed, inverse, gain_row):
    scaled = grad_out * gain_row
    inner = jnp.mean(scaled, axis=-1, keepdims=True)
    along = jnp.mean(scaled * normed, axis=-1, keepdims=True)
    return inverse * (scaled - inner - normed * along)


def first_grad_kernel(at_ref, near_ref, back_ref, w_ref, stacked_ref, o0, o1, o2, o3):
    rows, n = near_ref.shape
    wide = back_ref.shape[1]
    stacked_ref[...] = near_ref[...]
    lower = slice(rows - back_ref.shape[0], rows)
    kept = near_ref[lower, n - wide :].astype(F32) + back_ref[...].astype(F32)
    stacked_ref[lower, n - wide :] = kept.astype(BF)
    part = o0.shape[0]
    for s in (2, 1, 3, 0):
        window = pl.ds(pl.multiple_of(lax.rem(at_ref[PARTS] + s, PARTS) * part, part), part)
        (o0, o1, o2, o3)[s][...] = dot(stacked_ref[window, :], w_ref[:, :n], 1, 1).astype(BF)


def first_gradient(at, near, back, weights):
    rows = near.shape[0]
    model = weights.shape[0]
    vmem = pl.BlockSpec(memory_space=pltpu.VMEM)
    return pl.pallas_call(
        first_grad_kernel,
        out_shape=(
            jax.ShapeDtypeStruct(near.shape, BF), *[jax.ShapeDtypeStruct((rows // PARTS, model), BF)] * PARTS,
        ),
        in_specs=[pl.BlockSpec(memory_space=pltpu.SMEM)] + [vmem] * 3,
        out_specs=(vmem,) * (PARTS + 1),
        compiler_params=pltpu.CompilerParams(vmem_limit_bytes=VMEM),
        cost_estimate=pl.CostEstimate(flops=1_600_000_000, bytes_accessed=9_000_000, transcendentals=0),
        name="first_gradient",
    )(at, near, back, weights)


def total(values):
    return jnp.sum(values, axis=0, keepdims=True)


def second_back_kernel(at_ref, *refs):
    grads = refs[:PARTS]
    w_ref, cot_ref, middle_ref, rows_ref, low_ref, sums_ref = refs[PARTS : PARTS + 6]
    blocks, held = refs[PARTS + 6 : -1], refs[-1]
    n = grads[0].shape[1]
    for s in range(PARTS):
        window = pl.ds(pl.multiple_of(lax.rem(at_ref[PARTS] + s, PARTS) * n, n), n)
        held[:, window] = grads[s][...]
    grad = held[...].astype(F32)
    normed, inverse = normalized(middle_ref[...].astype(F32))
    low = (cot_ref[...].astype(F32) + norm_backward(grad, normed, inverse, rows_ref[1:2, :])).astype(BF)
    low_ref[...] = low
    for s in range(PARTS):
        blocks[s][...] = dot(low, w_ref[part_rows(at_ref, s, low.shape[1]), :], 1, 0).T.astype(BF)
    sums_ref[...] = jnp.zeros_like(sums_ref)
    sums_ref[0:1, :] = total(grad * normed)
    sums_ref[1:2, :] = total(grad)
    sums_ref[2:3, :] = total(low.astype(F32))


def second_norm_back(at, grads, w, cot_part, middle, rows_small):
    part, model = cot_part.shape
    vmem = pl.BlockSpec(memory_space=pltpu.VMEM)
    return pl.pallas_call(
        second_back_kernel,
        out_shape=(
            jax.ShapeDtypeStruct((part, model), BF), jax.ShapeDtypeStruct((8, model), F32),
            *[jax.ShapeDtypeStruct((w.shape[1], part), BF)] * PARTS,
        ),
        in_specs=[pl.BlockSpec(memory_space=pltpu.SMEM)] + [vmem] * (PARTS + 4),
        out_specs=(vmem,) * (2 + PARTS),
        scratch_shapes=[pltpu.VMEM((part, model), BF)],
        compiler_params=pltpu.CompilerParams(vmem_limit_bytes=VMEM),
        cost_estimate=pl.CostEstimate(flops=600_000_000, bytes_accessed=6_000_000, transcendentals=0),
        name="second_norm_back",
    )(at, *grads, w, cot_part, middle, rows_small)


def first_back_kernel(*refs):
    tokens_ref, middle_ref, rows_ref, o_ref, sums_ref = refs[PARTS:]
    grad = sum(ref[...].astype(F32) for ref in refs[:PARTS])
    normed, inverse = normalized(tokens_ref[...].astype(F32))
    o_ref[...] = (middle_ref[...].astype(F32) + norm_backward(grad, normed, inverse, rows_ref[0:1, :])).astype(BF)
    sums_ref[...] = jnp.zeros_like(sums_ref)
    sums_ref[0:1, :] = total(grad * normed)
    sums_ref[1:2, :] = total(grad)


def first_norm_back(grads, tokens_part, middle_grad, rows_small):
    vmem = pl.BlockSpec(memory_space=pltpu.VMEM)
    return pl.pallas_call(
        first_back_kernel,
        out_shape=(
            jax.ShapeDtypeStruct(tokens_part.shape, BF), jax.ShapeDtypeStruct((8, tokens_part.shape[1]), F32),
        ),
        in_specs=[vmem] * (PARTS + 3),
        out_specs=(vmem,) * 2,
        compiler_params=pltpu.CompilerParams(vmem_limit_bytes=VMEM),
        cost_estimate=pl.CostEstimate(flops=8_000_000, bytes_accessed=5_000_000, transcendentals=0),
        name="first_norm_back",
    )(*grads, tokens_part, middle_grad, rows_small)


def forward_kernel(at_ref, q_ref, start_ref, k_near, v_near, k_far, v_far, o0, o1, o2, o3,
                   exact_ref, lse_ref, q_heads, acc):
    heads = q_ref.shape[0] // HD
    i = pl.program_id(0)
    half = pl.num_programs(0) * SIDE
    q_heads[...] = by_head(q_ref[...] * jnp.asarray(HD**-0.5, BF), heads)
    acc[...] = jnp.zeros_like(acc)
    start_row = start_ref[...]

    def step(k_ref, v_ref, size, top, base, n, carry):
        peak, total = carry
        first_row = (top - n) * size
        rows = pl.ds(pl.multiple_of(first_row, size), size)
        scores = dot(k_ref[rows, :], q_heads[...], 1, 0)
        allowed = pair_mask(start_row, half + i * SIDE, base + first_row, size)
        scores = jnp.where(jnp.concatenate([allowed] * heads, axis=1), scores, NEGATIVE)
        new_peak = jnp.maximum(peak, jnp.max(scores, axis=0, keepdims=True))
        fade = jnp.exp(peak - new_peak)
        weights = jnp.exp(scores - new_peak)
        total = total * fade + jnp.sum(weights, axis=0, keepdims=True)
        low = weights.astype(BF)
        v_t = v_ref[rows, :].T
        for h in range(heads):
            at, cols = slice(h * HD, (h + 1) * HD), slice(h * SIDE, (h + 1) * SIDE)
            acc[at, :] = acc[at, :] * fade[:, cols] + dot(v_t[at, :], low[:, cols], 1, 0)
        return new_peak, total

    width = heads * SIDE
    near = functools.partial(step, k_near, v_near, SIDE, i, half)
    blocks = k_far.shape[0] // FAR
    far = functools.partial(step, k_far, v_far, FAR, blocks - 1, half - k_far.shape[0])
    carry = jnp.full((1, width), NEGATIVE, F32), jnp.zeros((1, width), F32)
    carry = lax.fori_loop(0, jnp.minimum(PARTS + i - at_ref[i], i) + 1, near, carry)
    peak, total = lax.fori_loop(0, blocks - at_ref[PARTS + 1 + i], far, carry)
    scale = 1.0 / total
    for h in range(heads):
        at, cols = slice(h * HD, (h + 1) * HD), slice(h * SIDE, (h + 1) * SIDE)
        exact = acc[at, :] * scale[:, cols]
        exact_ref[at, :] = exact.astype(BF)
    lse_ref[0] = peak + jnp.log(total)
    place = turned(i, at_ref)
    for s, out in enumerate((o0, o1, o2, o3)):
        @pl.when(place == s)
        def _():
            out[...] = exact_ref[...]


def turned(i, at):
    return lax.rem(i + PARTS - at[PARTS], PARTS)


def attend_forward(at, q_t, start, kv, kv_far):
    channels, rows = q_t.shape
    blocks = rows // SIDE
    width = channels // HD * SIDE
    column = pl.BlockSpec((channels, SIDE), lambda i, f: (0, i))
    return pl.pallas_call(
        forward_kernel,
        out_shape=(
            *[jax.ShapeDtypeStruct((channels, SIDE), BF)] * PARTS,
            jax.ShapeDtypeStruct((channels, rows), BF),
            jax.ShapeDtypeStruct((blocks, 1, width), F32),
        ),
        grid_spec=pltpu.PrefetchScalarGridSpec(
            num_scalar_prefetch=1,
            grid=(blocks,),
            in_specs=[column, pl.BlockSpec((1, SIDE), lambda i, f: (0, i))]
            + [pl.BlockSpec((a.shape[0], channels), lambda i, f, c=c: (0, c)) for a in (kv, kv_far) for c in range(2)],
            out_specs=(
                *[pl.BlockSpec((channels, SIDE), lambda i, f: (0, 0))] * PARTS,
                column,
                pl.BlockSpec((1, 1, width), lambda i, f: (i, 0, 0)),
            ),
            scratch_shapes=[pltpu.VMEM((channels, width), BF), pltpu.VMEM((channels, SIDE), F32)],
        ),
        compiler_params=pltpu.CompilerParams(vmem_limit_bytes=VMEM),
        cost_estimate=pl.CostEstimate(flops=6_000_000_000, bytes_accessed=6_000_000, transcendentals=4_000_000),
        name="attend_forward",
    )(at, q_t, start, kv, kv, kv_far, kv_far)


def backward_kernel(near, at_ref, q_ref, g0, g1, g2, g3, exact_ref, lse_ref, start_ref, k_ref, v_ref, add_ref,
                    dq_ref, dkv_ref, q_heads, g_heads, dq_acc, dk_acc, dv_acc):
    heads = q_ref.shape[0] // HD
    i = pl.program_id(0)
    blocks = pl.num_programs(0)
    half = blocks * SIDE
    size, base = (SIDE, half) if near else (FAR, half - k_ref.shape[0])
    q_heads[...] = by_head(q_ref[...] * jnp.asarray(HD**-0.5, BF), heads)
    place = turned(i, at_ref)
    grad = g0[...]
    for s, other in enumerate((g1, g2, g3)):
        grad = jnp.where(place == s + 1, other[...], grad)
    g_heads[...] = by_head(grad, heads)
    product = grad.astype(F32) * exact_ref[...].astype(F32)
    delta = jnp.concatenate(
        [jnp.sum(product[h * HD : (h + 1) * HD, :], axis=0, keepdims=True) for h in range(heads)], axis=1
    )
    dq_acc[...] = jnp.zeros_like(dq_acc)

    @pl.when(i == 0)
    def _():
        dk_acc[...] = jnp.zeros_like(dk_acc)
        dv_acc[...] = jnp.zeros_like(dv_acc)

    start_row = start_ref[...]
    lse = lse_ref[0]

    def step(j, carry):
        rows = pl.ds(pl.multiple_of(j * size, size), size)
        k_block = k_ref[rows, :]
        scores = dot(k_block, q_heads[...], 1, 0)
        allowed = pair_mask(start_row, half + i * SIDE, base + j * size, size)
        scores = jnp.where(jnp.concatenate([allowed] * heads, axis=1), scores, NEGATIVE)
        weights = jnp.exp(scores - lse)
        grad_weights = dot(v_ref[rows, :], g_heads[...], 1, 0)
        grad_scores = (weights * (grad_weights - delta)).astype(BF)
        dv_acc[rows, :] += dot(weights.astype(BF), g_heads[...], 1, 1)
        dk_acc[rows, :] += dot(grad_scores, q_heads[...], 1, 1)
        k_t = k_block.T
        for h in range(heads):
            at, cols = slice(h * HD, (h + 1) * HD), slice(h * SIDE, (h + 1) * SIDE)
            dq_acc[at, :] += dot(k_t[at, :], grad_scores[:, cols], 1, 0)
        return carry

    if near:
        lax.fori_loop(jnp.maximum(at_ref[i] - PARTS, 0), i + 1, step, 0)
        n = q_ref.shape[0]
        at = pl.ds(pl.multiple_of(i * SIDE, SIDE), SIDE)
        dkv_ref[at, :n] = (dq_acc[...] * HD**-0.5 + add_ref[...]).T.astype(BF)
    else:
        lax.fori_loop(at_ref[PARTS + 1 + i], k_ref.shape[0] // FAR, step, 0)
        dq_ref[...] = dq_acc[...] * HD**-0.5

    @pl.when(i == blocks - 1)
    def _():
        n = q_ref.shape[0]
        first_column = dkv_ref.shape[1] - 2 * n
        skipped = dk_acc.shape[0] - dkv_ref.shape[0]
        dkv_ref[:, first_column : first_column + n] = dk_acc[skipped:, :].astype(BF)
        dkv_ref[:, first_column + n :] = dv_acc[skipped:, :].astype(BF)


def far_kernel(at_ref, q_ref, g0, g1, g2, g3, exact_ref, lse_ref, start_ref, k_ref, v_ref, *rest):
    backward_kernel(False, at_ref, q_ref, g0, g1, g2, g3, exact_ref, lse_ref, start_ref, k_ref, v_ref, None, *rest)


def near_kernel(at_ref, q_ref, g0, g1, g2, g3, exact_ref, lse_ref, start_ref, k_ref, v_ref, add_ref, *rest):
    backward_kernel(True, at_ref, q_ref, g0, g1, g2, g3, exact_ref, lse_ref, start_ref, k_ref, v_ref, add_ref,
                    None, *rest)


def attend_backward(near, at, q_t, grads, exact_t, lse, start, kv, add=None):
    channels, rows = q_t.shape
    blocks = rows // SIDE
    width = channels // HD * SIDE
    column = pl.BlockSpec((channels, SIDE), lambda i, f: (0, i))
    block = pl.BlockSpec((channels, SIDE), lambda i, f: (0, 0))
    in_specs = [
        column,
        *[block] * PARTS,
        column,
        pl.BlockSpec((1, 1, width), lambda i, f: (i, 0, 0)),
        pl.BlockSpec((1, SIDE), lambda i, f: (0, i)),
    ] + [pl.BlockSpec((kv.shape[0], channels), lambda i, f, c=c: (0, c)) for c in range(2)]
    args = [at, q_t, *grads, exact_t, lse, start, kv, kv]
    if near:
        in_specs.append(column)
        args.append(add)
        out_shape = (jax.ShapeDtypeStruct((rows, 3 * channels), BF),)
        out_specs = (pl.BlockSpec((rows, 3 * channels), lambda i, f: (0, 0)),)
    else:
        out_shape = jax.ShapeDtypeStruct((channels, rows), F32), jax.ShapeDtypeStruct((REACH, 2 * channels), BF)
        out_specs = column, pl.BlockSpec((REACH, 2 * channels), lambda i, f: (0, 0))
    return pl.pallas_call(
        near_kernel if near else far_kernel,
        out_shape=out_shape,
        grid_spec=pltpu.PrefetchScalarGridSpec(
            num_scalar_prefetch=1,
            grid=(blocks,),
            in_specs=in_specs,
            out_specs=out_specs,
            scratch_shapes=[
                pltpu.VMEM((channels, width), BF),
                pltpu.VMEM((channels, width), BF),
                pltpu.VMEM((channels, SIDE), F32),
                pltpu.VMEM((kv.shape[0], channels), F32),
                pltpu.VMEM((kv.shape[0], channels), F32),
            ],
        ),
        compiler_params=pltpu.CompilerParams(vmem_limit_bytes=VMEM),
        cost_estimate=pl.CostEstimate(flops=9_000_000_000, bytes_accessed=6_000_000, transcendentals=4_000_000),
        name="attend_near" if near else "attend_far",
    )(*args)


def slots_kernel(target_ref, x_ref, o_ref):
    place = lax.broadcasted_iota(jnp.int32, (o_ref.shape[0], x_ref.shape[0]), 0) + pl.program_id(0) * o_ref.shape[0]
    o_ref[...] = dot((place == target_ref[...]).astype(F32).astype(BF), x_ref[...], 1, 0).astype(BF)


def to_slots(target, x, slots):
    return pl.pallas_call(
        slots_kernel,
        out_shape=jax.ShapeDtypeStruct((slots, x.shape[1]), BF),
        grid=(slots // SIDE,),
        in_specs=[pl.BlockSpec((1, x.shape[0]), lambda i: (0, 0)), pl.BlockSpec(x.shape, lambda i: (0, 0))],
        out_specs=pl.BlockSpec((SIDE, x.shape[1]), lambda i: (i, 0)),
        compiler_params=pltpu.CompilerParams(vmem_limit_bytes=VMEM),
        cost_estimate=pl.CostEstimate(flops=1_200_000_000, bytes_accessed=2_000_000, transcendentals=0),
        name="to_slots",
    )(target[None, :], x)


def tokens_kernel(target_ref, x_ref, *outs):
    place = lax.broadcasted_iota(jnp.int32, (SIDE, x_ref.shape[0]), 1)
    for s, out in enumerate(outs):
        rows = slice(s * SIDE, (s + 1) * SIDE)
        out[...] = dot((place == target_ref[rows, :]).astype(F32).astype(BF), x_ref[...], 1, 0).astype(BF)


def to_tokens(target, x):
    blocks = target.shape[0] // SIDE
    vmem = pl.BlockSpec(memory_space=pltpu.VMEM)
    return pl.pallas_call(
        tokens_kernel,
        out_shape=(jax.ShapeDtypeStruct((SIDE, x.shape[1]), BF),) * blocks,
        in_specs=[vmem] * 2,
        out_specs=(vmem,) * blocks,
        compiler_params=pltpu.CompilerParams(vmem_limit_bytes=VMEM),
        cost_estimate=pl.CostEstimate(flops=1_200_000_000, bytes_accessed=2_000_000, transcendentals=0),
        name="to_tokens",
    )(target[:, None], x)


def sum_kernel(at_ref, target_ref, x_ref, *refs):
    middle, o_ref = refs[:-1], refs[-1]
    n = SIDE
    place = lax.broadcasted_iota(jnp.int32, (n, x_ref.shape[0]), 1)
    for s, part in enumerate(middle):
        one = (place == target_ref[s * n : (s + 1) * n, :]).astype(F32).astype(BF)
        o_ref[part_rows(at_ref, s, n), :] = (part[...].astype(F32) + dot(one, x_ref[...], 1, 0)).astype(BF)


def block_output(at, target, x, middle):
    vmem = pl.BlockSpec(memory_space=pltpu.VMEM)
    return pl.pallas_call(
        sum_kernel,
        out_shape=jax.ShapeDtypeStruct((target.shape[0], x.shape[1]), BF),
        in_specs=[pl.BlockSpec(memory_space=pltpu.SMEM)] + [vmem] * (2 + len(middle)),
        out_specs=vmem,
        compiler_params=pltpu.CompilerParams(vmem_limit_bytes=VMEM),
        cost_estimate=pl.CostEstimate(flops=1_200_000_000, bytes_accessed=2_000_000, transcendentals=0),
        name="block_output",
    )(at, target[:, None], x, *middle)


def join_kernel(got_ref, *refs):
    outs, held = refs[:-1], refs[-1]
    capacity = got_ref.shape[1] // len(outs)
    for f in range(got_ref.shape[0] // 2):
        both = got_ref[2 * f].astype(F32) + got_ref[2 * f + 1].astype(F32)
        for e in range(len(outs)):
            held[e, f * capacity : (f + 1) * capacity, :] = both[e * capacity : (e + 1) * capacity, :]
    for e, out in enumerate(outs):
        out[...] = held[e].astype(BF)


def join(got, experts):
    shape = (got.shape[0] // 2 * (got.shape[1] // experts), got.shape[2])
    return pl.pallas_call(
        join_kernel,
        out_shape=(jax.ShapeDtypeStruct(shape, BF),) * experts,
        scratch_shapes=[pltpu.VMEM((experts, *shape), F32)],
        compiler_params=pltpu.CompilerParams(vmem_limit_bytes=VMEM),
        cost_estimate=pl.CostEstimate(flops=600_000, bytes_accessed=2_000_000, transcendentals=0),
        name="join",
    )(got)


def spread_kernel(bias_ref, *refs):
    parts, (o_ref, held, piece) = refs[:-3], refs[-3:]
    experts, rows = held.shape[:2]
    capacity = o_ref.shape[1] // experts
    for e in range(experts):
        if len(parts) == 1:
            total = parts[0][e * rows : (e + 1) * rows, :].astype(F32)
        else:
            total = sum(part[...].astype(F32) for part in parts[e * PARTS : (e + 1) * PARTS])
        held[e] = total + bias_ref[e : e + 1, :]
    for f in range(o_ref.shape[0] // 2):
        for e in range(experts):
            piece[e * capacity : (e + 1) * capacity, :] = held[e, f * capacity : (f + 1) * capacity, :]
        low = piece[...].astype(BF)
        o_ref[2 * f] = low
        o_ref[2 * f + 1] = low


def spread(parts, bias, capacity):
    experts, n = bias.shape
    rows = parts[0].shape[0] // (experts if len(parts) == 1 else 1)
    return pl.pallas_call(
        spread_kernel,
        out_shape=jax.ShapeDtypeStruct((rows // capacity * 2, experts * capacity, n), BF),
        scratch_shapes=[pltpu.VMEM((experts, rows, n), F32), pltpu.VMEM((experts * capacity, n), F32)],
        compiler_params=pltpu.CompilerParams(vmem_limit_bytes=VMEM),
        cost_estimate=pl.CostEstimate(flops=2_400_000, bytes_accessed=4_000_000, transcendentals=0),
        name="spread",
    )(bias, *parts)


def expert_kernel(at_ref, r0, r1, r2, r3, w_ref, b_ref, g_ref, act_ref, hg_ref, rows_ref, *outs):
    parts = (r0, r1, r2, r3)
    n = r0.shape[1]
    windows = [
        pl.ds(pl.multiple_of(lax.rem(at_ref[PARTS] + PARTS - s, PARTS) * n, n), n) for s in range(PARTS)
    ]
    for s in range(PARTS):
        rows_ref[:, windows[s]] = parts[s][...]
    inner = w_ref.shape[2]
    for j in range(2):
        cols = slice(j * inner // 2, (j + 1) * inner // 2)
        hidden = dot(rows_ref[...], w_ref[0, :, cols], 1, 0) + b_ref[0, :, cols].astype(F32)
        gate = jax.nn.sigmoid(hidden)
        act_ref[:, cols] = (hidden * gate).astype(BF)
        hg_ref[:, cols] = (g_ref[0, :, cols] * (gate * (1.0 + hidden * (1.0 - gate)))).astype(BF)
    for s in range(PARTS):
        outs[s][...] = dot(hg_ref[...], w_ref[0, windows[s], :], 1, 1).astype(BF)


def run_expert(e, at, parts, w_up, up_bias, active_grad):
    rows, n = parts[0].shape
    model, inner = w_up.shape[1:]
    whole = pl.BlockSpec((rows, n), lambda j, f: (0, 0))
    full = pl.BlockSpec((rows, inner), lambda j, f: (0, 0))
    return pl.pallas_call(
        expert_kernel,
        out_shape=(
            jax.ShapeDtypeStruct((rows, inner), BF),
            jax.ShapeDtypeStruct((rows, inner), BF),
            jax.ShapeDtypeStruct((rows, model), BF),
            *[jax.ShapeDtypeStruct((rows, n), BF)] * PARTS,
        ),
        grid_spec=pltpu.PrefetchScalarGridSpec(
            num_scalar_prefetch=1,
            grid=(1,),
            in_specs=[whole] * PARTS + [
                pl.BlockSpec((1, model, inner), lambda j, f: (e, 0, 0)),
                pl.BlockSpec((1, 1, inner), lambda j, f: (e, 0, 0)),
                pl.BlockSpec((1, rows, inner), lambda j, f: (e, 0, 0)),
            ],
            out_specs=(
                full, full,
                pl.BlockSpec((rows, model), lambda j, f: (0, 0)),
                *[whole] * PARTS,
            ),
        ),
        compiler_params=pltpu.CompilerParams(vmem_limit_bytes=VMEM),
        cost_estimate=pl.CostEstimate(flops=2_400_000_000, bytes_accessed=8_000_000, transcendentals=600_000),
        name="expert",
    )(at, *parts, w_up, up_bias[:, None, :], active_grad)


def result_kernel(a_ref, w_ref, o_ref):
    n = o_ref.shape[2]
    for t in range(o_ref.shape[0]):
        o_ref[t] = dot(a_ref[0], w_ref[0, :, t * n : (t + 1) * n], 1, 0).astype(BF)


def expert_results(active, w_down):
    held, rows, inner = active.shape
    model = w_down.shape[2]
    n = model // PARTS
    return pl.pallas_call(
        result_kernel,
        out_shape=jax.ShapeDtypeStruct((PARTS, held * rows, n), BF),
        grid=(held,),
        in_specs=[
            pl.BlockSpec((1, rows, inner), lambda e: (e, 0, 0)),
            pl.BlockSpec((1, inner, model), lambda e: (e, 0, 0)),
        ],
        out_specs=pl.BlockSpec((PARTS, rows, n), lambda e: (0, e, 0)),
        compiler_params=pltpu.CompilerParams(vmem_limit_bytes=VMEM),
        cost_estimate=pl.CostEstimate(flops=2_400_000_000, bytes_accessed=9_000_000, transcendentals=0),
        name="results",
    )(active, w_down)


def copy_kernel(x_ref, o_ref):
    o_ref[...] = x_ref[...]


def side_by_side(x):
    rows, n = x.shape[0] // PARTS, x.shape[1]
    return pl.pallas_call(
        copy_kernel,
        out_shape=jax.ShapeDtypeStruct((rows, PARTS * n), x.dtype),
        grid=(PARTS,),
        in_specs=[pl.BlockSpec((rows, n), lambda t: (t, 0))],
        out_specs=pl.BlockSpec((rows, n), lambda t: (0, t)),
        compiler_params=pltpu.CompilerParams(vmem_limit_bytes=VMEM),
        cost_estimate=pl.CostEstimate(flops=0, bytes_accessed=4_000_000, transcendentals=0),
        name="side_by_side",
    )(x)


def weight_kernel(x_ref, grads_ref, branch_ref, mixed_ref, o_ref):
    n = grads_ref.shape[1]
    groups, shard, _ = o_ref.shape
    grads = dot(x_ref[...].T, grads_ref[...], 1, 0).astype(BF)
    branch = dot(branch_ref[...].T, mixed_ref[...], 1, 1).astype(BF)
    for g in range(groups):
        rows = slice(g * shard, (g + 1) * shard)
        o_ref[g, :shard, :n] = grads[rows, :]
        o_ref[g, :shard, n:] = branch[rows, :]


def weight_gradients(x, grads, branch, mixed, groups):
    rows, model = x.shape
    n, channels = grads.shape[1], mixed.shape[0]
    block = pl.BlockSpec((rows, SIDE), lambda i: (0, i))
    shape = (groups, model // groups, n + channels)
    return pl.pallas_call(
        weight_kernel,
        out_shape=jax.ShapeDtypeStruct(shape, BF),
        grid=(model // SIDE,),
        in_specs=[
            block, pl.BlockSpec((rows, n), lambda i: (0, 0)), block, pl.BlockSpec((channels, rows), lambda i: (0, 0)),
        ],
        out_specs=pl.BlockSpec((groups * SIDE // model, *shape[1:]), lambda i: (i, 0, 0)),
        compiler_params=pltpu.CompilerParams(vmem_limit_bytes=VMEM),
        cost_estimate=pl.CostEstimate(flops=2_200_000_000, bytes_accessed=8_000_000, transcendentals=0),
        name="weight_gradients",
    )(x, grads, branch, mixed)


def after(value, *others):
    return lax.optimization_barrier((value, *others))[0]


def hops(axis, s):
    n = lax.axis_size(axis)
    return [(i, (i + s) % n) for i in range(n)]


def swapped(blocks, sign, name):
    with jax.named_scope("x_" + name):
        return [blocks[0]] + [lax.ppermute(blocks[s], "tp", hops("tp", sign * s)) for s in range(1, PARTS)]


def copied(block, name):
    return swapped([block] * PARTS, 1, name)


def in_order(parts, start, axis):
    turned_parts = [parts[-k % PARTS] for k in range(PARTS)]
    size = parts[0].shape[axis]
    both = jnp.concatenate(turned_parts + turned_parts[:-1], axis=axis)
    return lax.dynamic_slice_in_dim(both, (PARTS - start) % PARTS * size, PARTS * size, axis)


def on_device(tokens, cotangent, expert_ids, segment_ids, priority, w_qkv, w_out, norm_gains, norm_shifts,
              qv_bias, w_up, up_bias, w_down, down_bias):
    rows, model = tokens.shape
    channels = w_qkv.shape[2]
    heads = channels // HD
    seq_len = segment_ids.shape[0]
    f_count, c_count = lax.axis_size(FC[:3]), lax.axis_size("ctx")
    groups = f_count * c_count
    ctx_at, tp_at = lax.axis_index("ctx"), lax.axis_index("tp")
    held = w_up.shape[0]
    experts = held * groups
    capacity = (9 * seq_len + 8 * experts - 1) // (8 * experts)
    slots = experts * capacity
    shard = model // groups
    part = rows // PARTS
    width = model // PARTS
    bias_size = qv_bias.size

    bias_column = jnp.pad(qv_bias.reshape(-1), (0, shard - bias_size))[None]
    small = jnp.concatenate([norm_gains, norm_shifts, bias_column], axis=0).T
    small = jnp.pad(small, ((0, 0), (0, 128 - small.shape[1])))
    pack = jnp.concatenate([jnp.moveaxis(w_qkv, 0, 1).reshape(shard, 3 * channels), w_out.T, small], axis=1)
    packed = lax.all_to_all(jnp.broadcast_to(pack[None], (groups, *pack.shape)), FC, 0, 0, tiled=True)
    packed = packed.reshape(model, -1)
    lane = lax.broadcasted_iota(jnp.int32, (model, 2 * channels), 1)
    line = lax.broadcasted_iota(jnp.int32, (model, 2 * channels), 0)
    inside, group = line % shard, line // shard
    ends = qv_bias.shape[2]
    goal = (inside // (heads * ends) * channels + inside // ends % heads * HD + group * ends + inside % ends)
    move = ((goal == lane) & (inside < bias_size)).astype(BF)
    owner = expert_ids[:, 0]
    rank = priority[0]
    earlier_ids = lax.ppermute(after(expert_ids, pack) + 1, "ctx", [(0, 1)])[:, 0]
    before = (owner[None, :] == owner[:, None]) & (rank[None, :] < rank[:, None])
    carried = earlier_ids[None, :] == owner[:, None] + 1
    slot = jnp.sum(before.astype(jnp.int32), axis=1) + jnp.sum(carried.astype(jnp.int32), axis=1)
    target = jnp.where(slot < capacity, owner * capacity + slot, slots)
    places = [(tp_at + PARTS - s) % PARTS for s in range(PARTS)]
    target = jnp.concatenate([lax.dynamic_slice_in_dim(target, p * part, part) for p in places])

    def exchanged(sent, name):
        with jax.named_scope("x_" + name):
            return lax.all_to_all(sent, FC, 0, 0, tiled=True)

    def sent_rows(columns):
        return to_slots(target, columns, slots).reshape(groups, held * capacity, width)

    seg_own = lax.dynamic_slice_in_dim(segment_ids, ctx_at * rows, rows)
    start = jnp.sum((segment_ids[None, :] < seg_own[:, None]).astype(jnp.int32), axis=1)
    start = start + jnp.where(ctx_at == 0, rows, 0)
    first = start[::SIDE]
    at = jnp.concatenate([first // SIDE, tp_at[None], (first - (rows - HALO)) // FAR]).astype(jnp.int32)
    start = start[None, :]
    packed, start, at, move, target = lax.optimization_barrier((packed, start, at, move, target))
    rows_small, bias_row, bias_col = small_rows(packed, move)
    q_t, kv, first_low, halo = first_projection(tokens, packed, rows_small, bias_row, bias_col, channels)
    kv_far = lax.ppermute(halo, "ctx", [(0, 1)])
    out_all = lax.all_gather(packed[:, 3 * channels : 4 * channels], "tp", axis=0, tiled=True)
    cot_columns = [lax.dynamic_slice(cotangent, (p * part, tp_at * width), (part, width)) for p in places]
    cot_sent = sent_rows(jnp.concatenate(cot_columns))
    cot_got = exchanged(after(cot_sent, kv), "cot")
    *mixed, exact_t, lse = attend_forward(at, q_t, start, kv, kv_far)
    mixed = swapped(mixed, 1, "mixed")

    tokens_part = lax.dynamic_slice_in_dim(tokens, tp_at * part, part)
    cot_part = lax.dynamic_slice_in_dim(cotangent, tp_at * part, part)
    cot_mine = jnp.concatenate(join(after(cot_got, *mixed[1:]), held))
    cot_all = lax.all_gather(cot_mine, "tp", axis=0, tiled=True)
    middle, *blocks = second_norm(at, mixed, out_all, after(tokens_part, cot_mine), rows_small)
    second_sent = sent_rows(jnp.concatenate(swapped(blocks, 1, "second")))

    second_got = exchanged(second_sent, "rows")
    middle_late = after(middle, second_sent)
    middle_parts = swapped(
        [lax.dynamic_slice_in_dim(middle_late, (tp_at + s) % PARTS * width, width, 1) for s in range(PARTS)], 1, "middle"
    )
    second_got, middle_parts = lax.optimization_barrier((second_got, middle_parts))
    mine = join(second_got, held)
    parts = [copied(m, "rows") for m in mine]
    expert_grads = side_by_side(after(cot_all, mine[0])).reshape(held, -1, model)
    active_grad = jnp.einsum("emd,efd->emf", expert_grads, w_down, preferred_element_type=F32)
    done = [run_expert(e, at, parts[e], w_up, up_bias, active_grad) for e in range(held)]
    back_parts = [p for d in done for p in swapped(d[3:], -1, "back")]
    active_low = jnp.stack([d[0] for d in done])
    results = expert_results(active_low, w_down)
    back_sent = spread(back_parts, jnp.zeros((held, width), F32), capacity)
    back_sent, results = lax.optimization_barrier((back_sent, results))
    back_got = exchanged(back_sent, "back")
    result_sum = lax.psum_scatter(results, "tp", scatter_dimension=0, tiled=True)
    active_late, rows_late, hidden_late, grads_late = lax.optimization_barrier(
        (active_low, [d[2] for d in done], [d[1] for d in done], expert_grads, back_sent)
    )[:4]
    w_down_grad = jnp.einsum("emf,emd->efd", active_late, grads_late, preferred_element_type=F32)
    w_up_grad = jnp.einsum(
        "emd,emf->edf", jnp.stack(rows_late), jnp.stack(hidden_late), preferred_element_type=F32
    )
    back_got, w_down_grad, w_up_grad = lax.optimization_barrier((back_got, w_down_grad, w_up_grad))
    grad_blocks = swapped(to_tokens(target, back_got.reshape(slots, width)), -1, "grads")
    grad_blocks[0], result_sum = lax.optimization_barrier((grad_blocks[0], result_sum))
    bias_columns = lax.dynamic_slice_in_dim(down_bias, tp_at * width, width, 1).astype(F32)
    result_sent = spread([result_sum.reshape(-1, width)], bias_columns, capacity)
    result_got = exchanged(result_sent, "result")

    branch_low, second_sums, *mixed_grads = second_norm_back(at, grad_blocks, out_all, cot_part, middle, rows_small)
    grads_t = swapped(mixed_grads, -1, "mixedgrads")
    branch_all = lax.all_gather(branch_low, "tp", axis=0, tiled=True)

    dq_far, dkv_far = attend_backward(False, at, q_t, grads_t, exact_t, lse, start, kv_far)
    kv_back = lax.ppermute(dkv_far, "ctx", [(1, 0)])
    (near_grad,) = attend_backward(True, at, q_t, grads_t, exact_t, lse, start, kv, dq_far)

    result_got = after(result_got, near_grad, kv_back)
    block_columns = block_output(at, target, result_got.reshape(slots, width), middle_parts)
    block_all = lax.all_gather(block_columns, "tp", axis=0, tiled=True)
    near_grad, block_columns = lax.optimization_barrier((near_grad, block_columns))
    stacked, *first_blocks = first_gradient(at, near_grad, kv_back, packed)
    first_parts = swapped(first_blocks, 1, "firstsum")

    weight_tiles = weight_gradients(first_low, stacked, branch_all, exact_t, groups)
    weight_got = exchanged(weight_tiles, "weights")
    first_parts, block_all = lax.optimization_barrier((first_parts, block_all))

    tokens_grad_part, first_sums = first_norm_back(first_parts, tokens_part, branch_low, rows_small)
    tokens_grad = lax.all_gather(tokens_grad_part, "tp", axis=0, tiled=True)
    stacked, second_sums = lax.optimization_barrier((stacked, second_sums, tokens_grad_part))[:2]
    sums = jnp.concatenate([first_sums[:2], second_sums[:3]])
    stacked_sum = jnp.sum(stacked.astype(F32), axis=0)
    bias_sum = jnp.stack([stacked_sum[:channels], stacked_sum[2 * channels :]])
    bias_tiles = bias_sum.reshape(2, heads, groups, -1).transpose(2, 0, 1, 3).reshape(groups, -1)
    sum_tiles = sums.reshape(5, groups, shard).transpose(1, 0, 2).reshape(groups, -1)
    tail = jnp.concatenate([sum_tiles, bias_tiles], axis=1)
    tail = jnp.pad(tail, ((0, 0), (0, 256 - tail.shape[1]))).reshape(groups, 1, 256)
    tail, weight_got = lax.optimization_barrier((tail, weight_got))
    tail = exchanged(tail, "sums").sum(axis=0)[0]
    block_out = side_by_side(after(block_all, tail))
    got = weight_got.astype(F32).sum(axis=0)
    qkv_shard = jnp.moveaxis(got[:, : 3 * channels].reshape(shard, 3, channels), 1, 0)
    out_shard = got[:, 3 * channels :].T
    bias_shard = tail[5 * shard : 5 * shard + bias_size].reshape(qv_bias.shape)
    norms = sum(copied(tail[: 5 * shard].reshape(5, shard), "norms"))

    hidden_late, cot_late = lax.optimization_barrier((hidden_late, expert_grads, tail))[:2]
    up_bias_grad = jnp.stack([jnp.sum(h.astype(F32), axis=0) for h in hidden_late])
    down_bias_grad = jnp.sum(cot_late.astype(F32), axis=1)
    gain_shard = jnp.stack([norms[0], norms[2]])
    shift_shard = jnp.stack([norms[1], norms[3], norms[4]])
    return (block_out, tokens_grad, qkv_shard, out_shard, gain_shard, shift_shard, bias_shard,
            w_up_grad, up_bias_grad, w_down_grad, down_bias_grad)


def solution(mesh):
    devices = mesh.devices.reshape(2, 4, 2, mesh.shape["ctx"], mesh.shape["tp"])
    chips = Mesh(devices, ("y_hi", "z", "core", "ctx", "tp"))
    token, weight = P(FC, None), P(None, FC)
    experts = P(FC, None, "tp"), P(FC, "tp"), P(FC, "tp", None), P(FC, None)
    shared = P(None, FC, "tp"), P("tp", FC), weight, weight, P(None, "tp", FC)
    return jax.shard_map(
        on_device,
        mesh=chips,
        in_specs=(token, token, token, P(FC[:3]), token, *shared, *experts),
        out_specs=(token, token, *shared, *experts),
        check_vma=False,
    )
```

```python
import functools

import jax
import jax.numpy as jnp
from jax import lax
from jax.experimental import pallas as pl
from jax.experimental.pallas import tpu as pltpu
from jax.sharding import Mesh, PartitionSpec as P

HD = 64
EPSILON = 1e-05
NEGATIVE = -1e30
REACH = 800
SIDE = 256
FC = ("y_hi", "z", "core", "ctx")
HALO = 896
FAR = 128
PARTS = 4
VMEM = 40 * 2**20
BF = jnp.bfloat16
F32 = jnp.float32


def dot(a, b, ca, cb):
    return lax.dot_general(a, b, (((ca,), (cb,)), ((), ())), preferred_element_type=F32)


def by_head(cols, heads):
    row = lax.broadcasted_iota(jnp.int32, cols.shape, 0) // HD
    zero = jnp.zeros_like(cols)
    return jnp.concatenate([jnp.where(row == h, cols, zero) for h in range(heads)], axis=1)


def pair_mask(start_row, q_first, k_first, size):
    k_pos = lax.broadcasted_iota(jnp.int32, (size, SIDE), 0) + k_first
    q_pos = lax.broadcasted_iota(jnp.int32, (size, SIDE), 1) + q_first
    return (k_pos >= start_row) & (k_pos <= q_pos)


def normalized(values):
    centre = values - jnp.mean(values, axis=-1, keepdims=True)
    variance = jnp.mean(centre * centre, axis=-1, keepdims=True)
    inverse = lax.rsqrt(variance + EPSILON)
    return centre * inverse, inverse


def small_kernel(small_ref, move_ref, rows_ref, bias_ref, column_ref):
    small = small_ref[...]
    rows_ref[...] = small.astype(F32).T[:8, :]
    column = dot(move_ref[...], small, 0, 0)
    column_ref[...] = column
    bias_ref[...] = column.T[:8, :]


def small_rows(packed, move):
    model, wide = packed.shape
    return pl.pallas_call(
        small_kernel,
        out_shape=(
            jax.ShapeDtypeStruct((8, model), F32),
            jax.ShapeDtypeStruct((8, move.shape[1]), F32),
            jax.ShapeDtypeStruct((move.shape[1], 128), F32),
        ),
        grid=(1,),
        in_specs=[
            pl.BlockSpec((model, 128), lambda i: (0, wide // 128 - 1)),
            pl.BlockSpec(move.shape, lambda i: (0, 0)),
        ],
        out_specs=(
            pl.BlockSpec((8, model), lambda i: (0, 0)),
            pl.BlockSpec((8, move.shape[1]), lambda i: (0, 0)),
            pl.BlockSpec((move.shape[1], 128), lambda i: (0, 0)),
        ),
        compiler_params=pltpu.CompilerParams(vmem_limit_bytes=VMEM),
        cost_estimate=pl.CostEstimate(flops=200_000_000, bytes_accessed=1_500_000, transcendentals=0),
        name="small_rows",
    )(packed, move)


def first_kernel(own_ref, w_ref, rows_ref, bias_ref, column_ref, q_ref, kv_ref, low_ref, halo_ref):
    channels = q_ref.shape[0]
    low = (normalized(own_ref[...].astype(F32))[0] * rows_ref[0:1, :] + rows_ref[2:3, :]).astype(BF)
    low_ref[...] = low
    q_ref[...] = (dot(low, w_ref[:, :channels], 1, 0).T + column_ref[:channels, 5:6]).astype(BF)
    kv = dot(low, w_ref[:, channels : 3 * channels], 1, 0)
    kv_ref[:, :channels] = kv[:, :channels].astype(BF)
    kv_ref[:, channels:] = (kv[:, channels:] + bias_ref[5:6, channels:]).astype(BF)
    i = pl.program_id(0)
    skipped = PARTS * SIDE - HALO

    @pl.when(i == 0)
    def _():
        halo_ref[: SIDE - skipped, :] = kv_ref[skipped:, :]

    @pl.when(i > 0)
    def _():
        halo_ref[pl.ds(pl.multiple_of(i * SIDE - skipped, FAR), SIDE), :] = kv_ref[...]


def first_projection(tokens, weights, rows_small, bias, column, channels):
    rows, model = tokens.shape

    def whole(a):
        return pl.BlockSpec(a.shape, lambda i: (0,) * a.ndim)

    return pl.pallas_call(
        first_kernel,
        out_shape=(
            jax.ShapeDtypeStruct((channels, rows), BF),
            jax.ShapeDtypeStruct((rows, 2 * channels), BF),
            jax.ShapeDtypeStruct((rows, model), BF),
            jax.ShapeDtypeStruct((HALO, 2 * channels), BF),
        ),
        grid=(rows // SIDE,),
        in_specs=[
            pl.BlockSpec((SIDE, model), lambda i: (i, 0)),
            whole(weights), whole(rows_small), whole(bias), whole(column),
        ],
        out_specs=(
            pl.BlockSpec((channels, SIDE), lambda i: (0, i)),
            pl.BlockSpec((SIDE, 2 * channels), lambda i: (i, 0)),
            pl.BlockSpec((SIDE, model), lambda i: (i, 0)),
            pl.BlockSpec((HALO, 2 * channels), lambda i: (0, 0)),
        ),
        compiler_params=pltpu.CompilerParams(vmem_limit_bytes=VMEM),
        cost_estimate=pl.CostEstimate(flops=1_900_000_000, bytes_accessed=6_000_000, transcendentals=0),
        name="first_projection",
    )(tokens, weights, rows_small, bias, column)


def part_rows(at_ref, s, n):
    return pl.ds(pl.multiple_of(lax.rem(at_ref[PARTS] + PARTS - s, PARTS) * n, n), n)


def branch_kernel(at_ref, *refs):
    mixed = refs[:PARTS]
    w_ref, tokens_ref, rows_ref, middle_ref = refs[PARTS : PARTS + 4]
    second, held = refs[PARTS + 4 : -1], refs[-1]
    middle = tokens_ref[...].astype(F32) + rows_ref[4:5, :]
    model = middle.shape[1]
    for s in range(PARTS):
        middle += dot(mixed[s][...].T, w_ref[part_rows(at_ref, s, model), :], 1, 1)
    middle_ref[...] = middle.astype(BF)
    n = second[0].shape[1]
    held[...] = (normalized(middle)[0] * rows_ref[1:2, :] + rows_ref[3:4, :]).astype(BF)
    for s in range(PARTS):
        window = pl.ds(pl.multiple_of(lax.rem(at_ref[PARTS] + s, PARTS) * n, n), n)
        second[s][...] = held[:, window]


def second_norm(at, mixed, w, tokens_part, rows_small):
    part, model = tokens_part.shape
    vmem = pl.BlockSpec(memory_space=pltpu.VMEM)
    return pl.pallas_call(
        branch_kernel,
        out_shape=(
            jax.ShapeDtypeStruct((part, model), BF), *[jax.ShapeDtypeStruct((part, model // PARTS), BF)] * PARTS,
        ),
        in_specs=[pl.BlockSpec(memory_space=pltpu.SMEM)] + [vmem] * (PARTS + 3),
        out_specs=(vmem,) * (1 + PARTS),
        scratch_shapes=[pltpu.VMEM((part, model), BF)],
        compiler_params=pltpu.CompilerParams(vmem_limit_bytes=VMEM),
        cost_estimate=pl.CostEstimate(flops=600_000_000, bytes_accessed=6_000_000, transcendentals=0),
        name="second_norm",
    )(at, *mixed, w, tokens_part, rows_small)


def norm_backward(grad_out, normed, inverse, gain_row):
    scaled = grad_out * gain_row
    inner = jnp.mean(scaled, axis=-1, keepdims=True)
    along = jnp.mean(scaled * normed, axis=-1, keepdims=True)
    return inverse * (scaled - inner - normed * along)


def first_grad_kernel(at_ref, near_ref, back_ref, w_ref, stacked_ref, o0, o1, o2, o3):
    rows, n = near_ref.shape
    wide = back_ref.shape[1]
    stacked_ref[...] = near_ref[...]
    lower = slice(rows - back_ref.shape[0], rows)
    kept = near_ref[lower, n - wide :].astype(F32) + back_ref[...].astype(F32)
    stacked_ref[lower, n - wide :] = kept.astype(BF)
    part = o0.shape[0]
    for s in (2, 1, 3, 0):
        window = pl.ds(pl.multiple_of(lax.rem(at_ref[PARTS] + s, PARTS) * part, part), part)
        (o0, o1, o2, o3)[s][...] = dot(stacked_ref[window, :], w_ref[:, :n], 1, 1).astype(BF)


def first_gradient(at, near, back, weights):
    rows = near.shape[0]
    model = weights.shape[0]
    vmem = pl.BlockSpec(memory_space=pltpu.VMEM)
    return pl.pallas_call(
        first_grad_kernel,
        out_shape=(
            jax.ShapeDtypeStruct(near.shape, BF), *[jax.ShapeDtypeStruct((rows // PARTS, model), BF)] * PARTS,
        ),
        in_specs=[pl.BlockSpec(memory_space=pltpu.SMEM)] + [vmem] * 3,
        out_specs=(vmem,) * (PARTS + 1),
        compiler_params=pltpu.CompilerParams(vmem_limit_bytes=VMEM),
        cost_estimate=pl.CostEstimate(flops=1_600_000_000, bytes_accessed=9_000_000, transcendentals=0),
        name="first_gradient",
    )(at, near, back, weights)


def total(values):
    return jnp.sum(values, axis=0, keepdims=True)


def second_back_kernel(at_ref, *refs):
    grads = refs[:PARTS]
    w_ref, cot_ref, middle_ref, rows_ref, low_ref, sums_ref = refs[PARTS : PARTS + 6]
    blocks, held = refs[PARTS + 6 : -1], refs[-1]
    n = grads[0].shape[1]
    for s in range(PARTS):
        window = pl.ds(pl.multiple_of(lax.rem(at_ref[PARTS] + s, PARTS) * n, n), n)
        held[:, window] = grads[s][...]
    grad = held[...].astype(F32)
    normed, inverse = normalized(middle_ref[...].astype(F32))
    low = (cot_ref[...].astype(F32) + norm_backward(grad, normed, inverse, rows_ref[1:2, :])).astype(BF)
    low_ref[...] = low
    for s in range(PARTS):
        blocks[s][...] = dot(low, w_ref[part_rows(at_ref, s, low.shape[1]), :], 1, 0).T.astype(BF)
    sums_ref[...] = jnp.zeros_like(sums_ref)
    sums_ref[0:1, :] = total(grad * normed)
    sums_ref[1:2, :] = total(grad)
    sums_ref[2:3, :] = total(low.astype(F32))


def second_norm_back(at, grads, w, cot_part, middle, rows_small):
    part, model = cot_part.shape
    vmem = pl.BlockSpec(memory_space=pltpu.VMEM)
    return pl.pallas_call(
        second_back_kernel,
        out_shape=(
            jax.ShapeDtypeStruct((part, model), BF), jax.ShapeDtypeStruct((8, model), F32),
            *[jax.ShapeDtypeStruct((w.shape[1], part), BF)] * PARTS,
        ),
        in_specs=[pl.BlockSpec(memory_space=pltpu.SMEM)] + [vmem] * (PARTS + 4),
        out_specs=(vmem,) * (2 + PARTS),
        scratch_shapes=[pltpu.VMEM((part, model), BF)],
        compiler_params=pltpu.CompilerParams(vmem_limit_bytes=VMEM),
        cost_estimate=pl.CostEstimate(flops=600_000_000, bytes_accessed=6_000_000, transcendentals=0),
        name="second_norm_back",
    )(at, *grads, w, cot_part, middle, rows_small)


def first_back_kernel(*refs):
    tokens_ref, middle_ref, rows_ref, o_ref, sums_ref = refs[PARTS:]
    grad = sum(ref[...].astype(F32) for ref in refs[:PARTS])
    normed, inverse = normalized(tokens_ref[...].astype(F32))
    o_ref[...] = (middle_ref[...].astype(F32) + norm_backward(grad, normed, inverse, rows_ref[0:1, :])).astype(BF)
    sums_ref[...] = jnp.zeros_like(sums_ref)
    sums_ref[0:1, :] = total(grad * normed)
    sums_ref[1:2, :] = total(grad)


def first_norm_back(grads, tokens_part, middle_grad, rows_small):
    vmem = pl.BlockSpec(memory_space=pltpu.VMEM)
    return pl.pallas_call(
        first_back_kernel,
        out_shape=(
            jax.ShapeDtypeStruct(tokens_part.shape, BF), jax.ShapeDtypeStruct((8, tokens_part.shape[1]), F32),
        ),
        in_specs=[vmem] * (PARTS + 3),
        out_specs=(vmem,) * 2,
        compiler_params=pltpu.CompilerParams(vmem_limit_bytes=VMEM),
        cost_estimate=pl.CostEstimate(flops=8_000_000, bytes_accessed=5_000_000, transcendentals=0),
        name="first_norm_back",
    )(*grads, tokens_part, middle_grad, rows_small)


def forward_kernel(at_ref, q_ref, start_ref, k_near, v_near, k_far, v_far, o0, o1, o2, o3,
                   exact_ref, lse_ref, q_heads, acc):
    heads = q_ref.shape[0] // HD
    i = pl.program_id(0)
    half = pl.num_programs(0) * SIDE
    q_heads[...] = by_head(q_ref[...] * jnp.asarray(HD**-0.5, BF), heads)
    acc[...] = jnp.zeros_like(acc)
    start_row = start_ref[...]

    def step(k_ref, v_ref, size, top, base, n, carry):
        peak, total = carry
        first_row = (top - n) * size
        rows = pl.ds(pl.multiple_of(first_row, size), size)
        scores = dot(k_ref[rows, :], q_heads[...], 1, 0)
        allowed = pair_mask(start_row, half + i * SIDE, base + first_row, size)
        scores = jnp.where(jnp.concatenate([allowed] * heads, axis=1), scores, NEGATIVE)
        new_peak = jnp.maximum(peak, jnp.max(scores, axis=0, keepdims=True))
        fade = jnp.exp(peak - new_peak)
        weights = jnp.exp(scores - new_peak)
        total = total * fade + jnp.sum(weights, axis=0, keepdims=True)
        low = weights.astype(BF)
        v_t = v_ref[rows, :].T
        for h in range(heads):
            at, cols = slice(h * HD, (h + 1) * HD), slice(h * SIDE, (h + 1) * SIDE)
            acc[at, :] = acc[at, :] * fade[:, cols] + dot(v_t[at, :], low[:, cols], 1, 0)
        return new_peak, total

    width = heads * SIDE
    near = functools.partial(step, k_near, v_near, SIDE, i, half)
    blocks = k_far.shape[0] // FAR
    far = functools.partial(step, k_far, v_far, FAR, blocks - 1, half - k_far.shape[0])
    carry = jnp.full((1, width), NEGATIVE, F32), jnp.zeros((1, width), F32)
    carry = lax.fori_loop(0, jnp.minimum(PARTS + i - at_ref[i], i) + 1, near, carry)
    peak, total = lax.fori_loop(0, blocks - at_ref[PARTS + 1 + i], far, carry)
    scale = 1.0 / total
    for h in range(heads):
        at, cols = slice(h * HD, (h + 1) * HD), slice(h * SIDE, (h + 1) * SIDE)
        exact = acc[at, :] * scale[:, cols]
        exact_ref[at, :] = exact.astype(BF)
    lse_ref[0] = peak + jnp.log(total)
    place = turned(i, at_ref)
    for s, out in enumerate((o0, o1, o2, o3)):
        @pl.when(place == s)
        def _():
            out[...] = exact_ref[...]


def turned(i, at):
    return lax.rem(i + PARTS - at[PARTS], PARTS)


def attend_forward(at, q_t, start, kv, kv_far):
    channels, rows = q_t.shape
    blocks = rows // SIDE
    width = channels // HD * SIDE
    column = pl.BlockSpec((channels, SIDE), lambda i, f: (0, i))
    return pl.pallas_call(
        forward_kernel,
        out_shape=(
            *[jax.ShapeDtypeStruct((channels, SIDE), BF)] * PARTS,
            jax.ShapeDtypeStruct((channels, rows), BF),
            jax.ShapeDtypeStruct((blocks, 1, width), F32),
        ),
        grid_spec=pltpu.PrefetchScalarGridSpec(
            num_scalar_prefetch=1,
            grid=(blocks,),
            in_specs=[column, pl.BlockSpec((1, SIDE), lambda i, f: (0, i))]
            + [pl.BlockSpec((a.shape[0], channels), lambda i, f, c=c: (0, c)) for a in (kv, kv_far) for c in range(2)],
            out_specs=(
                *[pl.BlockSpec((channels, SIDE), lambda i, f: (0, 0))] * PARTS,
                column,
                pl.BlockSpec((1, 1, width), lambda i, f: (i, 0, 0)),
            ),
            scratch_shapes=[pltpu.VMEM((channels, width), BF), pltpu.VMEM((channels, SIDE), F32)],
        ),
        compiler_params=pltpu.CompilerParams(vmem_limit_bytes=VMEM),
        cost_estimate=pl.CostEstimate(flops=6_000_000_000, bytes_accessed=6_000_000, transcendentals=4_000_000),
        name="attend_forward",
    )(at, q_t, start, kv, kv, kv_far, kv_far)


def backward_kernel(near, at_ref, q_ref, g0, g1, g2, g3, exact_ref, lse_ref, start_ref, k_ref, v_ref, add_ref,
                    dq_ref, dkv_ref, q_heads, g_heads, dq_acc, dk_acc, dv_acc):
    heads = q_ref.shape[0] // HD
    i = pl.program_id(0)
    blocks = pl.num_programs(0)
    half = blocks * SIDE
    size, base = (SIDE, half) if near else (FAR, half - k_ref.shape[0])
    q_heads[...] = by_head(q_ref[...] * jnp.asarray(HD**-0.5, BF), heads)
    place = turned(i, at_ref)
    grad = g0[...]
    for s, other in enumerate((g1, g2, g3)):
        grad = jnp.where(place == s + 1, other[...], grad)
    g_heads[...] = by_head(grad, heads)
    product = grad.astype(F32) * exact_ref[...].astype(F32)
    delta = jnp.concatenate(
        [jnp.sum(product[h * HD : (h + 1) * HD, :], axis=0, keepdims=True) for h in range(heads)], axis=1
    )
    dq_acc[...] = jnp.zeros_like(dq_acc)

    @pl.when(i == 0)
    def _():
        dk_acc[...] = jnp.zeros_like(dk_acc)
        dv_acc[...] = jnp.zeros_like(dv_acc)

    start_row = start_ref[...]
    lse = lse_ref[0]

    def step(j, carry):
        rows = pl.ds(pl.multiple_of(j * size, size), size)
        k_block = k_ref[rows, :]
        scores = dot(k_block, q_heads[...], 1, 0)
        allowed = pair_mask(start_row, half + i * SIDE, base + j * size, size)
        scores = jnp.where(jnp.concatenate([allowed] * heads, axis=1), scores, NEGATIVE)
        weights = jnp.exp(scores - lse)
        grad_weights = dot(v_ref[rows, :], g_heads[...], 1, 0)
        grad_scores = (weights * (grad_weights - delta)).astype(BF)
        dv_acc[rows, :] += dot(weights.astype(BF), g_heads[...], 1, 1)
        dk_acc[rows, :] += dot(grad_scores, q_heads[...], 1, 1)
        k_t = k_block.T
        for h in range(heads):
            at, cols = slice(h * HD, (h + 1) * HD), slice(h * SIDE, (h + 1) * SIDE)
            dq_acc[at, :] += dot(k_t[at, :], grad_scores[:, cols], 1, 0)
        return carry

    if near:
        lax.fori_loop(jnp.maximum(at_ref[i] - PARTS, 0), i + 1, step, 0)
        n = q_ref.shape[0]
        at = pl.ds(pl.multiple_of(i * SIDE, SIDE), SIDE)
        dkv_ref[at, :n] = (dq_acc[...] * HD**-0.5 + add_ref[...]).T.astype(BF)
    else:
        lax.fori_loop(at_ref[PARTS + 1 + i], k_ref.shape[0] // FAR, step, 0)
        dq_ref[...] = dq_acc[...] * HD**-0.5

    @pl.when(i == blocks - 1)
    def _():
        n = q_ref.shape[0]
        first_column = dkv_ref.shape[1] - 2 * n
        skipped = dk_acc.shape[0] - dkv_ref.shape[0]
        dkv_ref[:, first_column : first_column + n] = dk_acc[skipped:, :].astype(BF)
        dkv_ref[:, first_column + n :] = dv_acc[skipped:, :].astype(BF)


def far_kernel(at_ref, q_ref, g0, g1, g2, g3, exact_ref, lse_ref, start_ref, k_ref, v_ref, *rest):
    backward_kernel(False, at_ref, q_ref, g0, g1, g2, g3, exact_ref, lse_ref, start_ref, k_ref, v_ref, None, *rest)


def near_kernel(at_ref, q_ref, g0, g1, g2, g3, exact_ref, lse_ref, start_ref, k_ref, v_ref, add_ref, *rest):
    backward_kernel(True, at_ref, q_ref, g0, g1, g2, g3, exact_ref, lse_ref, start_ref, k_ref, v_ref, add_ref,
                    None, *rest)


def attend_backward(near, at, q_t, grads, exact_t, lse, start, kv, add=None):
    channels, rows = q_t.shape
    blocks = rows // SIDE
    width = channels // HD * SIDE
    column = pl.BlockSpec((channels, SIDE), lambda i, f: (0, i))
    block = pl.BlockSpec((channels, SIDE), lambda i, f: (0, 0))
    in_specs = [
        column,
        *[block] * PARTS,
        column,
        pl.BlockSpec((1, 1, width), lambda i, f: (i, 0, 0)),
        pl.BlockSpec((1, SIDE), lambda i, f: (0, i)),
    ] + [pl.BlockSpec((kv.shape[0], channels), lambda i, f, c=c: (0, c)) for c in range(2)]
    args = [at, q_t, *grads, exact_t, lse, start, kv, kv]
    if near:
        in_specs.append(column)
        args.append(add)
        out_shape = (jax.ShapeDtypeStruct((rows, 3 * channels), BF),)
        out_specs = (pl.BlockSpec((rows, 3 * channels), lambda i, f: (0, 0)),)
    else:
        out_shape = jax.ShapeDtypeStruct((channels, rows), F32), jax.ShapeDtypeStruct((REACH, 2 * channels), BF)
        out_specs = column, pl.BlockSpec((REACH, 2 * channels), lambda i, f: (0, 0))
    return pl.pallas_call(
        near_kernel if near else far_kernel,
        out_shape=out_shape,
        grid_spec=pltpu.PrefetchScalarGridSpec(
            num_scalar_prefetch=1,
            grid=(blocks,),
            in_specs=in_specs,
            out_specs=out_specs,
            scratch_shapes=[
                pltpu.VMEM((channels, width), BF),
                pltpu.VMEM((channels, width), BF),
                pltpu.VMEM((channels, SIDE), F32),
                pltpu.VMEM((kv.shape[0], channels), F32),
                pltpu.VMEM((kv.shape[0], channels), F32),
            ],
        ),
        compiler_params=pltpu.CompilerParams(vmem_limit_bytes=VMEM),
        cost_estimate=pl.CostEstimate(flops=1000, bytes_accessed=1000, transcendentals=0),
        name="attend_near" if near else "attend_far",
    )(*args)


def slots_kernel(target_ref, x_ref, o_ref):
    place = lax.broadcasted_iota(jnp.int32, (o_ref.shape[0], x_ref.shape[0]), 0) + pl.program_id(0) * o_ref.shape[0]
    o_ref[...] = dot((place == target_ref[...]).astype(F32).astype(BF), x_ref[...], 1, 0).astype(BF)


def to_slots(target, x, slots):
    return pl.pallas_call(
        slots_kernel,
        out_shape=jax.ShapeDtypeStruct((slots, x.shape[1]), BF),
        grid=(slots // SIDE,),
        in_specs=[pl.BlockSpec((1, x.shape[0]), lambda i: (0, 0)), pl.BlockSpec(x.shape, lambda i: (0, 0))],
        out_specs=pl.BlockSpec((SIDE, x.shape[1]), lambda i: (i, 0)),
        compiler_params=pltpu.CompilerParams(vmem_limit_bytes=VMEM),
        cost_estimate=pl.CostEstimate(flops=1_200_000_000, bytes_accessed=2_000_000, transcendentals=0),
        name="to_slots",
    )(target[None, :], x)


def tokens_kernel(target_ref, x_ref, *outs):
    place = lax.broadcasted_iota(jnp.int32, (SIDE, x_ref.shape[0]), 1)
    for s, out in enumerate(outs):
        rows = slice(s * SIDE, (s + 1) * SIDE)
        out[...] = dot((place == target_ref[rows, :]).astype(F32).astype(BF), x_ref[...], 1, 0).astype(BF)


def to_tokens(target, x):
    blocks = target.shape[0] // SIDE
    vmem = pl.BlockSpec(memory_space=pltpu.VMEM)
    return pl.pallas_call(
        tokens_kernel,
        out_shape=(jax.ShapeDtypeStruct((SIDE, x.shape[1]), BF),) * blocks,
        in_specs=[vmem] * 2,
        out_specs=(vmem,) * blocks,
        compiler_params=pltpu.CompilerParams(vmem_limit_bytes=VMEM),
        cost_estimate=pl.CostEstimate(flops=1_200_000_000, bytes_accessed=2_000_000, transcendentals=0),
        name="to_tokens",
    )(target[:, None], x)


def sum_kernel(at_ref, target_ref, x_ref, *refs):
    middle, o_ref = refs[:-1], refs[-1]
    n = SIDE
    place = lax.broadcasted_iota(jnp.int32, (n, x_ref.shape[0]), 1)
    for s, part in enumerate(middle):
        one = (place == target_ref[s * n : (s + 1) * n, :]).astype(F32).astype(BF)
        o_ref[part_rows(at_ref, s, n), :] = (part[...].astype(F32) + dot(one, x_ref[...], 1, 0)).astype(BF)


def block_output(at, target, x, middle):
    vmem = pl.BlockSpec(memory_space=pltpu.VMEM)
    return pl.pallas_call(
        sum_kernel,
        out_shape=jax.ShapeDtypeStruct((target.shape[0], x.shape[1]), BF),
        in_specs=[pl.BlockSpec(memory_space=pltpu.SMEM)] + [vmem] * (2 + len(middle)),
        out_specs=vmem,
        compiler_params=pltpu.CompilerParams(vmem_limit_bytes=VMEM),
        cost_estimate=pl.CostEstimate(flops=1_200_000_000, bytes_accessed=2_000_000, transcendentals=0),
        name="block_output",
    )(at, target[:, None], x, *middle)


def join_kernel(got_ref, *refs):
    outs, held = refs[:-1], refs[-1]
    capacity = got_ref.shape[1] // len(outs)
    for f in range(got_ref.shape[0] // 2):
        both = got_ref[2 * f].astype(F32) + got_ref[2 * f + 1].astype(F32)
        for e in range(len(outs)):
            held[e, f * capacity : (f + 1) * capacity, :] = both[e * capacity : (e + 1) * capacity, :]
    for e, out in enumerate(outs):
        out[...] = held[e].astype(BF)


def join(got, experts):
    shape = (got.shape[0] // 2 * (got.shape[1] // experts), got.shape[2])
    return pl.pallas_call(
        join_kernel,
        out_shape=(jax.ShapeDtypeStruct(shape, BF),) * experts,
        scratch_shapes=[pltpu.VMEM((experts, *shape), F32)],
        compiler_params=pltpu.CompilerParams(vmem_limit_bytes=VMEM),
        cost_estimate=pl.CostEstimate(flops=600_000, bytes_accessed=2_000_000, transcendentals=0),
        name="join",
    )(got)


def spread_kernel(bias_ref, *refs):
    parts, (o_ref, held, piece) = refs[:-3], refs[-3:]
    experts, rows = held.shape[:2]
    capacity = o_ref.shape[1] // experts
    for e in range(experts):
        if len(parts) == 1:
            total = parts[0][e * rows : (e + 1) * rows, :].astype(F32)
        else:
            total = sum(part[...].astype(F32) for part in parts[e * PARTS : (e + 1) * PARTS])
        held[e] = total + bias_ref[e : e + 1, :]
    for f in range(o_ref.shape[0] // 2):
        for e in range(experts):
            piece[e * capacity : (e + 1) * capacity, :] = held[e, f * capacity : (f + 1) * capacity, :]
        low = piece[...].astype(BF)
        o_ref[2 * f] = low
        o_ref[2 * f + 1] = low


def spread(parts, bias, capacity):
    experts, n = bias.shape
    rows = parts[0].shape[0] // (experts if len(parts) == 1 else 1)
    return pl.pallas_call(
        spread_kernel,
        out_shape=jax.ShapeDtypeStruct((rows // capacity * 2, experts * capacity, n), BF),
        scratch_shapes=[pltpu.VMEM((experts, rows, n), F32), pltpu.VMEM((experts * capacity, n), F32)],
        compiler_params=pltpu.CompilerParams(vmem_limit_bytes=VMEM),
        cost_estimate=pl.CostEstimate(flops=2_400_000, bytes_accessed=4_000_000, transcendentals=0),
        name="spread",
    )(bias, *parts)


def expert_kernel(at_ref, r0, r1, r2, r3, w_ref, b_ref, g_ref, act_ref, hg_ref, rows_ref, *outs):
    parts = (r0, r1, r2, r3)
    n = r0.shape[1]
    windows = [
        pl.ds(pl.multiple_of(lax.rem(at_ref[PARTS] + PARTS - s, PARTS) * n, n), n) for s in range(PARTS)
    ]
    for s in range(PARTS):
        rows_ref[:, windows[s]] = parts[s][...]
    inner = w_ref.shape[2]
    for j in range(2):
        cols = slice(j * inner // 2, (j + 1) * inner // 2)
        hidden = dot(rows_ref[...], w_ref[0, :, cols], 1, 0) + b_ref[0, :, cols].astype(F32)
        gate = jax.nn.sigmoid(hidden)
        act_ref[:, cols] = (hidden * gate).astype(BF)
        hg_ref[:, cols] = (g_ref[0, :, cols] * (gate * (1.0 + hidden * (1.0 - gate)))).astype(BF)
    for s in range(PARTS):
        outs[s][...] = dot(hg_ref[...], w_ref[0, windows[s], :], 1, 1).astype(BF)


def run_expert(e, at, parts, w_up, up_bias, active_grad):
    rows, n = parts[0].shape
    model, inner = w_up.shape[1:]
    whole = pl.BlockSpec((rows, n), lambda j, f: (0, 0))
    full = pl.BlockSpec((rows, inner), lambda j, f: (0, 0))
    return pl.pallas_call(
        expert_kernel,
        out_shape=(
            jax.ShapeDtypeStruct((rows, inner), BF),
            jax.ShapeDtypeStruct((rows, inner), BF),
            jax.ShapeDtypeStruct((rows, model), BF),
            *[jax.ShapeDtypeStruct((rows, n), BF)] * PARTS,
        ),
        grid_spec=pltpu.PrefetchScalarGridSpec(
            num_scalar_prefetch=1,
            grid=(1,),
            in_specs=[whole] * PARTS + [
                pl.BlockSpec((1, model, inner), lambda j, f: (e, 0, 0)),
                pl.BlockSpec((1, 1, inner), lambda j, f: (e, 0, 0)),
                pl.BlockSpec((1, rows, inner), lambda j, f: (e, 0, 0)),
            ],
            out_specs=(
                full, full,
                pl.BlockSpec((rows, model), lambda j, f: (0, 0)),
                *[whole] * PARTS,
            ),
        ),
        compiler_params=pltpu.CompilerParams(vmem_limit_bytes=VMEM),
        cost_estimate=pl.CostEstimate(flops=2_400_000_000, bytes_accessed=8_000_000, transcendentals=600_000),
        name="expert",
    )(at, *parts, w_up, up_bias[:, None, :], active_grad)


def result_kernel(a_ref, w_ref, o_ref):
    n = o_ref.shape[2]
    for t in range(o_ref.shape[0]):
        o_ref[t] = dot(a_ref[0], w_ref[0, :, t * n : (t + 1) * n], 1, 0).astype(BF)


def expert_results(active, w_down):
    held, rows, inner = active.shape
    model = w_down.shape[2]
    n = model // PARTS
    return pl.pallas_call(
        result_kernel,
        out_shape=jax.ShapeDtypeStruct((PARTS, held * rows, n), BF),
        grid=(held,),
        in_specs=[
            pl.BlockSpec((1, rows, inner), lambda e: (e, 0, 0)),
            pl.BlockSpec((1, inner, model), lambda e: (e, 0, 0)),
        ],
        out_specs=pl.BlockSpec((PARTS, rows, n), lambda e: (0, e, 0)),
        compiler_params=pltpu.CompilerParams(vmem_limit_bytes=VMEM),
        cost_estimate=pl.CostEstimate(flops=2_400_000_000, bytes_accessed=9_000_000, transcendentals=0),
        name="results",
    )(active, w_down)


def copy_kernel(x_ref, o_ref):
    o_ref[...] = x_ref[...]


def side_by_side(x):
    rows, n = x.shape[0] // PARTS, x.shape[1]
    return pl.pallas_call(
        copy_kernel,
        out_shape=jax.ShapeDtypeStruct((rows, PARTS * n), x.dtype),
        grid=(PARTS,),
        in_specs=[pl.BlockSpec((rows, n), lambda t: (t, 0))],
        out_specs=pl.BlockSpec((rows, n), lambda t: (0, t)),
        compiler_params=pltpu.CompilerParams(vmem_limit_bytes=VMEM),
        cost_estimate=pl.CostEstimate(flops=0, bytes_accessed=4_000_000, transcendentals=0),
        name="side_by_side",
    )(x)


def weight_kernel(x_ref, grads_ref, branch_ref, mixed_ref, o_ref):
    n = grads_ref.shape[1]
    groups, shard, _ = o_ref.shape
    grads = dot(x_ref[...].T, grads_ref[...], 1, 0).astype(BF)
    branch = dot(branch_ref[...].T, mixed_ref[...], 1, 1).astype(BF)
    for g in range(groups):
        rows = slice(g * shard, (g + 1) * shard)
        o_ref[g, :shard, :n] = grads[rows, :]
        o_ref[g, :shard, n:] = branch[rows, :]


def weight_gradients(x, grads, branch, mixed, groups):
    rows, model = x.shape
    n, channels = grads.shape[1], mixed.shape[0]
    block = pl.BlockSpec((rows, SIDE), lambda i: (0, i))
    shape = (groups, model // groups, n + channels)
    return pl.pallas_call(
        weight_kernel,
        out_shape=jax.ShapeDtypeStruct(shape, BF),
        grid=(model // SIDE,),
        in_specs=[
            block, pl.BlockSpec((rows, n), lambda i: (0, 0)), block, pl.BlockSpec((channels, rows), lambda i: (0, 0)),
        ],
        out_specs=pl.BlockSpec((groups * SIDE // model, *shape[1:]), lambda i: (i, 0, 0)),
        compiler_params=pltpu.CompilerParams(vmem_limit_bytes=VMEM),
        cost_estimate=pl.CostEstimate(flops=2_200_000_000, bytes_accessed=8_000_000, transcendentals=0),
        name="weight_gradients",
    )(x, grads, branch, mixed)


def after(value, *others):
    return lax.optimization_barrier((value, *others))[0]


def hops(axis, s):
    n = lax.axis_size(axis)
    return [(i, (i + s) % n) for i in range(n)]


def swapped(blocks, sign, name):
    with jax.named_scope("x_" + name):
        return [blocks[0]] + [lax.ppermute(blocks[s], "tp", hops("tp", sign * s)) for s in range(1, PARTS)]


def copied(block, name):
    return swapped([block] * PARTS, 1, name)


def in_order(parts, start, axis):
    turned_parts = [parts[-k % PARTS] for k in range(PARTS)]
    size = parts[0].shape[axis]
    both = jnp.concatenate(turned_parts + turned_parts[:-1], axis=axis)
    return lax.dynamic_slice_in_dim(both, (PARTS - start) % PARTS * size, PARTS * size, axis)


def on_device(tokens, cotangent, expert_ids, segment_ids, priority, w_qkv, w_out, norm_gains, norm_shifts,
              qv_bias, w_up, up_bias, w_down, down_bias):
    rows, model = tokens.shape
    channels = w_qkv.shape[2]
    heads = channels // HD
    seq_len = segment_ids.shape[0]
    f_count, c_count = lax.axis_size(FC[:3]), lax.axis_size("ctx")
    groups = f_count * c_count
    ctx_at, tp_at = lax.axis_index("ctx"), lax.axis_index("tp")
    held = w_up.shape[0]
    experts = held * groups
    capacity = (9 * seq_len + 8 * experts - 1) // (8 * experts)
    slots = experts * capacity
    shard = model // groups
    part = rows // PARTS
    width = model // PARTS
    bias_size = qv_bias.size

    bias_column = jnp.pad(qv_bias.reshape(-1), (0, shard - bias_size))[None]
    small = jnp.concatenate([norm_gains, norm_shifts, bias_column], axis=0).T
    small = jnp.pad(small, ((0, 0), (0, 128 - small.shape[1])))
    pack = jnp.concatenate([jnp.moveaxis(w_qkv, 0, 1).reshape(shard, 3 * channels), w_out.T, small], axis=1)
    packed = lax.all_to_all(jnp.broadcast_to(pack[None], (groups, *pack.shape)), FC, 0, 0, tiled=True)
    packed = packed.reshape(model, -1)
    lane = lax.broadcasted_iota(jnp.int32, (model, 2 * channels), 1)
    line = lax.broadcasted_iota(jnp.int32, (model, 2 * channels), 0)
    inside, group = line % shard, line // shard
    ends = qv_bias.shape[2]
    goal = (inside // (heads * ends) * channels + inside // ends % heads * HD + group * ends + inside % ends)
    move = ((goal == lane) & (inside < bias_size)).astype(BF)
    owner = expert_ids[:, 0]
    rank = priority[0]
    earlier_ids = lax.ppermute(after(expert_ids, pack) + 1, "ctx", [(0, 1)])[:, 0]
    before = (owner[None, :] == owner[:, None]) & (rank[None, :] < rank[:, None])
    carried = earlier_ids[None, :] == owner[:, None] + 1
    slot = jnp.sum(before.astype(jnp.int32), axis=1) + jnp.sum(carried.astype(jnp.int32), axis=1)
    target = jnp.where(slot < capacity, owner * capacity + slot, slots)
    places = [(tp_at + PARTS - s) % PARTS for s in range(PARTS)]
    target = jnp.concatenate([lax.dynamic_slice_in_dim(target, p * part, part) for p in places])

    def exchanged(sent, name):
        with jax.named_scope("x_" + name):
            return lax.all_to_all(sent, FC, 0, 0, tiled=True)

    def sent_rows(columns):
        return to_slots(target, columns, slots).reshape(groups, held * capacity, width)

    seg_own = lax.dynamic_slice_in_dim(segment_ids, ctx_at * rows, rows)
    start = jnp.sum((segment_ids[None, :] < seg_own[:, None]).astype(jnp.int32), axis=1)
    start = start + jnp.where(ctx_at == 0, rows, 0)
    first = start[::SIDE]
    at = jnp.concatenate([first // SIDE, tp_at[None], (first - (rows - HALO)) // FAR]).astype(jnp.int32)
    start = start[None, :]
    packed, start, at, move, target = lax.optimization_barrier((packed, start, at, move, target))
    rows_small, bias_row, bias_col = small_rows(packed, move)
    q_t, kv, first_low, halo = first_projection(tokens, packed, rows_small, bias_row, bias_col, channels)
    kv_far = lax.ppermute(halo, "ctx", [(0, 1)])
    out_all = lax.all_gather(packed[:, 3 * channels : 4 * channels], "tp", axis=0, tiled=True)
    cot_columns = [lax.dynamic_slice(cotangent, (p * part, tp_at * width), (part, width)) for p in places]
    cot_sent = sent_rows(jnp.concatenate(cot_columns))
    cot_got = exchanged(after(cot_sent, kv), "cot")
    *mixed, exact_t, lse = attend_forward(at, q_t, start, kv, kv_far)
    mixed = swapped(mixed, 1, "mixed")

    tokens_part = lax.dynamic_slice_in_dim(tokens, tp_at * part, part)
    cot_part = lax.dynamic_slice_in_dim(cotangent, tp_at * part, part)
    cot_mine = jnp.concatenate(join(after(cot_got, *mixed[1:]), held))
    cot_all = lax.all_gather(cot_mine, "tp", axis=0, tiled=True)
    middle, *blocks = second_norm(at, mixed, out_all, after(tokens_part, cot_mine), rows_small)
    second_sent = sent_rows(jnp.concatenate(swapped(blocks, 1, "second")))

    second_got = exchanged(second_sent, "rows")
    middle_late = after(middle, second_sent)
    middle_parts = swapped(
        [lax.dynamic_slice_in_dim(middle_late, (tp_at + s) % PARTS * width, width, 1) for s in range(PARTS)], 1, "middle"
    )
    second_got, middle_parts = lax.optimization_barrier((second_got, middle_parts))
    mine = join(second_got, held)
    parts = [copied(m, "rows") for m in mine]
    expert_grads = side_by_side(after(cot_all, mine[0])).reshape(held, -1, model)
    active_grad = jnp.einsum("emd,efd->emf", expert_grads, w_down, preferred_element_type=F32)
    done = [run_expert(e, at, parts[e], w_up, up_bias, active_grad) for e in range(held)]
    back_parts = [p for d in done for p in swapped(d[3:], -1, "back")]
    active_low = jnp.stack([d[0] for d in done])
    results = expert_results(active_low, w_down)
    back_sent = spread(back_parts, jnp.zeros((held, width), F32), capacity)
    back_sent, results = lax.optimization_barrier((back_sent, results))
    back_got = exchanged(back_sent, "back")
    result_sum = lax.psum_scatter(results, "tp", scatter_dimension=0, tiled=True)
    active_late, rows_late, hidden_late, grads_late = lax.optimization_barrier(
        (active_low, [d[2] for d in done], [d[1] for d in done], expert_grads, back_sent)
    )[:4]
    w_down_grad = jnp.einsum("emf,emd->efd", active_late, grads_late, preferred_element_type=F32)
    w_up_grad = jnp.einsum(
        "emd,emf->edf", jnp.stack(rows_late), jnp.stack(hidden_late), preferred_element_type=F32
    )
    back_got, w_down_grad, w_up_grad = lax.optimization_barrier((back_got, w_down_grad, w_up_grad))
    grad_blocks = swapped(to_tokens(target, back_got.reshape(slots, width)), -1, "grads")
    grad_blocks[0], result_sum = lax.optimization_barrier((grad_blocks[0], result_sum))
    bias_columns = lax.dynamic_slice_in_dim(down_bias, tp_at * width, width, 1).astype(F32)
    result_sent = spread([result_sum.reshape(-1, width)], bias_columns, capacity)
    result_got = exchanged(result_sent, "result")

    branch_low, second_sums, *mixed_grads = second_norm_back(at, grad_blocks, out_all, cot_part, middle, rows_small)
    grads_t = swapped(mixed_grads, -1, "mixedgrads")
    branch_all = lax.all_gather(branch_low, "tp", axis=0, tiled=True)

    dq_far, dkv_far = attend_backward(False, at, q_t, grads_t, exact_t, lse, start, kv_far)
    kv_back = lax.ppermute(dkv_far, "ctx", [(1, 0)])
    (near_grad,) = attend_backward(True, at, q_t, grads_t, exact_t, lse, start, kv, dq_far)

    result_got = after(result_got, near_grad, kv_back)
    block_columns = block_output(at, target, result_got.reshape(slots, width), middle_parts)
    block_all = lax.all_gather(block_columns, "tp", axis=0, tiled=True)
    near_grad, block_columns = lax.optimization_barrier((near_grad, block_columns))
    stacked, *first_blocks = first_gradient(at, near_grad, kv_back, packed)
    first_parts = swapped(first_blocks, 1, "firstsum")

    weight_tiles = weight_gradients(first_low, stacked, branch_all, exact_t, groups)
    weight_got = exchanged(weight_tiles, "weights")
    first_parts, block_all = lax.optimization_barrier((first_parts, block_all))

    tokens_grad_part, first_sums = first_norm_back(first_parts, tokens_part, branch_low, rows_small)
    tokens_grad = lax.all_gather(tokens_grad_part, "tp", axis=0, tiled=True)
    block_out = side_by_side(after(block_all, tokens_grad_part))
    stacked, second_sums = lax.optimization_barrier((stacked, second_sums, tokens_grad_part))[:2]
    sums = jnp.concatenate([first_sums[:2], second_sums[:3]])
    stacked_sum = jnp.sum(stacked.astype(F32), axis=0)
    bias_sum = jnp.stack([stacked_sum[:channels], stacked_sum[2 * channels :]])
    bias_tiles = bias_sum.reshape(2, heads, groups, -1).transpose(2, 0, 1, 3).reshape(groups, -1)
    sum_tiles = sums.reshape(5, groups, shard).transpose(1, 0, 2).reshape(groups, -1)
    tail = jnp.concatenate([sum_tiles, bias_tiles], axis=1)
    tail = jnp.pad(tail, ((0, 0), (0, 256 - tail.shape[1]))).reshape(groups, 1, 256)
    tail, weight_got = lax.optimization_barrier((tail, weight_got))
    tail = exchanged(tail, "sums").sum(axis=0)[0]
    got = weight_got.astype(F32).sum(axis=0)
    qkv_shard = jnp.moveaxis(got[:, : 3 * channels].reshape(shard, 3, channels), 1, 0)
    out_shard = got[:, 3 * channels :].T
    bias_shard = tail[5 * shard : 5 * shard + bias_size].reshape(qv_bias.shape)
    norms = sum(copied(tail[: 5 * shard].reshape(5, shard), "norms"))

    hidden_late, cot_late = lax.optimization_barrier((jnp.stack(hidden_late), expert_grads, tokens_grad_part))[:2]
    up_bias_grad = jnp.sum(hidden_late.astype(F32), axis=1)
    down_bias_grad = jnp.sum(cot_late.astype(F32), axis=1)
    gain_shard = jnp.stack([norms[0], norms[2]])
    shift_shard = jnp.stack([norms[1], norms[3], norms[4]])
    return (block_out, tokens_grad, qkv_shard, out_shard, gain_shard, shift_shard, bias_shard,
            w_up_grad, up_bias_grad, w_down_grad, down_bias_grad)


def solution(mesh):
    devices = mesh.devices.reshape(2, 4, 2, mesh.shape["ctx"], mesh.shape["tp"])
    chips = Mesh(devices, ("y_hi", "z", "core", "ctx", "tp"))
    token, weight = P(FC, None), P(None, FC)
    experts = P(FC, None, "tp"), P(FC, "tp"), P(FC, "tp", None), P(FC, None)
    shared = P(None, FC, "tp"), P("tp", FC), weight, weight, P(None, "tp", FC)
    return jax.shard_map(
        on_device,
        mesh=chips,
        in_specs=(token, token, token, P(FC[:3]), token, *shared, *experts),
        out_specs=(token, token, *shared, *experts),
        check_vma=False,
    )
```
